128 devices in a mesh: fsdp: 8 (over x, z_lo), tensor: 16 (over y, z_hi, core).
Axes of the slice: x: 4, y: 4, z: 4 (z_hi: 2, z_lo: 2; z = z_hi * 2 + z_lo), core: 2. Of those that a mesh axis runs over, the one named last changes fastest.
Arguments:
- hidden_in: bfloat16 [4, 8, 512, 2048], P(None, 'fsdp', 'tensor'), may hold values from -6 to 6
- cotangent: bfloat16 [4, 8, 512, 2048], P(None, 'fsdp', 'tensor'), may hold values from -6 to 6
- gain_attn: bfloat16 [2048], P('fsdp'), may hold values from 0.5 to 1.5
- w_query: bfloat16 [2048, 2048], P('fsdp', 'tensor'), may hold values from -0.125 to 0.125
- w_key: bfloat16 [2048, 2048], P('fsdp', 'tensor'), may hold values from -0.125 to 0.125
- w_value: bfloat16 [2048, 2048], P('fsdp', 'tensor'), may hold values from -0.125 to 0.125
- w_output: bfloat16 [2048, 2048], P('tensor', 'fsdp'), may hold values from -0.5 to 0.5
- gain_mlp: bfloat16 [2048], P('fsdp'), may hold values from 0.5 to 1.5
- w_gate: bfloat16 [2048, 5504], P('fsdp', 'tensor'), may hold values from -0.125 to 0.125
- w_up: bfloat16 [2048, 5504], P('fsdp', 'tensor'), may hold values from -0.125 to 0.125
- w_down: bfloat16 [5504, 2048], P('tensor', 'fsdp'), may hold values from -0.15625 to 0.15625
Outputs:
- block_out: bfloat16 [4, 8, 512, 2048], P(None, 'fsdp', 'tensor')
- grad_in: bfloat16 [4, 8, 512, 2048], P(None, 'fsdp', 'tensor')
- grad_gain_attn: float32 [2048], P('fsdp')
- grad_query: float32 [2048, 2048], P('fsdp', 'tensor')
- grad_key: float32 [2048, 2048], P('fsdp', 'tensor')
- grad_value: float32 [2048, 2048], P('fsdp', 'tensor')
- grad_output: float32 [2048, 2048], P('tensor', 'fsdp')
- grad_gain_mlp: float32 [2048], P('fsdp')
- grad_gate: float32 [2048, 5504], P('fsdp', 'tensor')
- grad_up: float32 [2048, 5504], P('fsdp', 'tensor')
- grad_down: float32 [5504, 2048], P('tensor', 'fsdp')
The draws below stay inside these ranges and needn't reach their ends.
All inputs are finite; a program needn't handle non-finite values.
Results may differ from the reference program's by a relative error of at most 0.025.
Values may be sent and summed in bfloat16 or wider, within the bound.
A program may use at most 128 MiB of HBM per device.

```python
import jax
import jax.numpy as jnp
from jax import lax

D = 2048
HEADS = 16
HD = 128
FF = 5504
L = 512
MICRO = 4
SEQS = 8


def steps_of(stream_key, extent, pieces, least, top_value):
    gain, own = 1.0, jax.random.fold_in(stream_key, 6)
    for position, shards_of in pieces:
        steps = jnp.exp(jax.random.uniform(jax.random.fold_in(own, position), (shards_of,), jnp.float32, least / len(pieces), top_value / len(pieces)))
        gain = gain * jnp.repeat(steps, extent[position] // shards_of).reshape([-1 if axis == position else 1 for axis in range(len(extent))])
    return gain


def normal_values(rng, shape, scale, reach, pieces=(), kind=jnp.bfloat16):
    result = scale * jax.random.normal(rng, shape, jnp.float32)
    if pieces:
        result = result * steps_of(rng, shape, pieces, -0.22, 0.18)
    return jnp.clip(result, -reach, reach).astype(kind)


def setup_inputs(seed: int = 0) -> dict:
    streams_of = jax.random.split(jax.random.key(seed), 12)
    return {
        "hidden_in": normal_values(streams_of[0], (MICRO, SEQS, L, D), 1.0, 6.0, ((1, 8), (2, 16))),
        "cotangent": normal_values(streams_of[1], (MICRO, SEQS, L, D), 1.0, 6.0, ((1, 8), (2, 16))),
        "gain_attn": jnp.clip(1.0 + 0.1 * jax.random.normal(streams_of[2], (D,), jnp.float32), 0.5, 1.5).astype(jnp.bfloat16),
        "w_query": normal_values(streams_of[3], (D, HEADS * HD), D ** -0.5, 0.125, ((0, 8), (1, 16))),
        "w_key": normal_values(streams_of[4], (D, HEADS * HD), D ** -0.5, 0.125, ((0, 8), (1, 16))),
        "w_value": normal_values(streams_of[5], (D, HEADS * HD), D ** -0.5, 0.125, ((0, 8), (1, 16))),
        "w_output": normal_values(streams_of[6], (HEADS * HD, D), (HEADS * HD // 16) ** -0.5, 0.5, ((0, 16), (1, 8))),
        "gain_mlp": jnp.clip(1.0 + 0.1 * jax.random.normal(streams_of[7], (D,), jnp.float32), 0.5, 1.5).astype(jnp.bfloat16),
        "w_gate": normal_values(streams_of[8], (D, FF), D ** -0.5, 0.125, ((0, 8), (1, 16))),
        "w_up": normal_values(streams_of[9], (D, FF), D ** -0.5, 0.125, ((0, 8), (1, 16))),
        "w_down": normal_values(streams_of[10], (FF, D), (FF // 4) ** -0.5, 0.15625, ((0, 16), (1, 8))),
    }


EPSILON = 1e-05
THETA = 10000.0
PRECISE = lax.Precision.HIGHEST

@jax.custom_vjp
def low(v):
    return lax.optimization_barrier(v.astype(jnp.bfloat16)).astype(jnp.float32)

@jax.custom_vjp
def low_back(v):
    return v

def low_keep(v):
    return (low(v), None)

def low_pass(kept, grad):
    return (grad,)

def back_keep(v):
    return (v, None)

def back_low(kept, grad):
    return (low(grad),)
low.defvjp(low_keep, low_pass)
low_back.defvjp(back_keep, back_low)

def tables(length, size):
    half_size = size // 2
    inverse_freq = THETA ** (-(jnp.arange(half_size, dtype=jnp.float32) * 2.0) / size)
    angles = jnp.arange(length, dtype=jnp.float32)[:, None] * inverse_freq[None, :]
    return (jnp.cos(angles)[:, None, :], jnp.sin(angles)[:, None, :])

def rotate(tensor, cos_t, sin_t):
    half_size = tensor.shape[-1] // 2
    upper_half = tensor[..., :half_size]
    lower_half = tensor[..., half_size:]
    return jnp.concatenate([upper_half * cos_t - lower_half * sin_t, lower_half * cos_t + upper_half * sin_t], axis=-1)

def rms_norm(rows_in, gain_vec):
    return rows_in * lax.rsqrt(lax.optimization_barrier(jnp.mean(rows_in * rows_in, axis=-1, keepdims=True)) + EPSILON) * gain_vec

def layer(rows_in, params):
    gain_attn, w_query, w_key, w_value, w_output, gain_mlp, w_gate, w_up, w_down = params
    length = rows_in.shape[0]
    cos_t, sin_t = tables(length, HD)
    normed_attn = low(rms_norm(rows_in, gain_attn))

    def project_heads(weight):
        return low_back(jnp.dot(normed_attn, weight, precision=PRECISE)).reshape(length, HEADS, HD)
    queries = low(rotate(project_heads(w_query), cos_t, sin_t))
    keys_rot = low(rotate(project_heads(w_key), cos_t, sin_t))
    values = low(project_heads(w_value))
    scores = low_back(jnp.einsum('qhd,khd->hqk', queries, keys_rot, precision=PRECISE) * HD ** (-0.5))
    causal = jnp.arange(length)[:, None] >= jnp.arange(length)[None, :]
    attn_probs = low(jax.nn.softmax(jnp.where(causal[None], scores, -jnp.inf), axis=-1))
    attn_mixed = low(low_back(jnp.einsum('hqk,khd->qhd', attn_probs, values, precision=PRECISE)))
    attn_mixed = attn_mixed.reshape(length, HEADS * HD)
    middle = rows_in + low_back(jnp.dot(attn_mixed, w_output, precision=PRECISE))
    normed_mlp = low(rms_norm(middle, gain_mlp))
    gate_pre = low_back(jnp.dot(normed_mlp, w_gate, precision=PRECISE))
    up_pre = low_back(jnp.dot(normed_mlp, w_up, precision=PRECISE))
    hidden = low(jax.nn.silu(gate_pre) * up_pre)
    return middle + low_back(jnp.dot(hidden, w_down, precision=PRECISE))

def reference(hidden_in, cotangent, gain_attn, w_query, w_key, w_value, w_output, gain_mlp, w_gate, w_up, w_down):
    arr_shape = hidden_in.shape
    flattened = hidden_in.reshape(-1, arr_shape[2], arr_shape[3]).astype(jnp.float32)
    params = (gain_attn.astype(jnp.float32), w_query.astype(jnp.float32), w_key.astype(jnp.float32), w_value.astype(jnp.float32), w_output.astype(jnp.float32), gain_mlp.astype(jnp.float32), w_gate.astype(jnp.float32), w_up.astype(jnp.float32), w_down.astype(jnp.float32))

    def forward(sequences, *weights):
        runner = jax.checkpoint(lambda sequence: layer(sequence, weights))
        return lax.map(runner, sequences)
    output_rows, pullback = jax.vjp(forward, flattened, *params)
    gradients = pullback(cotangent.reshape(flattened.shape).astype(jnp.float32))
    return (output_rows.reshape(arr_shape).astype(jnp.bfloat16), gradients[0].reshape(arr_shape).astype(jnp.bfloat16), gradients[1], gradients[2], gradients[3], gradients[4], gradients[5], gradients[6], gradients[7], gradients[8], gradients[9])
```

```python
import jax
import jax.numpy as jnp
from jax import lax
from jax.sharding import PartitionSpec as P

HD = 128


EPSILON = 1e-05
THETA = 10000.0


def tables(length, size):
    half_size = size // 2
    inverse_freq = THETA ** (-(jnp.arange(half_size, dtype=jnp.float32) * 2.0) / size)
    angles = jnp.arange(length, dtype=jnp.float32)[:, None] * inverse_freq[None, :]
    return (jnp.cos(angles)[:, None, :], jnp.sin(angles)[:, None, :])


def rotate(tensor, cos_t, sin_t):
    half_size = tensor.shape[-1] // 2
    upper_half = tensor[..., :half_size]
    lower_half = tensor[..., half_size:]
    return jnp.concatenate(
        [upper_half * cos_t - lower_half * sin_t, lower_half * cos_t + upper_half * sin_t], axis=-1
    )


def rotate_back(tensor, cos_t, sin_t):
    half_size = tensor.shape[-1] // 2
    upper_half = tensor[..., :half_size]
    lower_half = tensor[..., half_size:]
    return jnp.concatenate(
        [upper_half * cos_t + lower_half * sin_t, lower_half * cos_t - upper_half * sin_t], axis=-1
    )


def norm_forward(rows_in, gain_vec):
    factor = lax.rsqrt(jnp.mean(rows_in * rows_in, axis=-1, keepdims=True) + EPSILON)
    return (rows_in * factor * gain_vec, factor)


def norm_backward(grad_out, rows_in, factor, gain_vec):
    scaled = grad_out * gain_vec
    grad_rows = factor * scaled - rows_in * factor**3 * jnp.mean(
        scaled * rows_in, axis=-1, keepdims=True
    )
    grad_gain = jnp.sum(grad_out * rows_in * factor, axis=(0, 1))
    return (grad_rows, grad_gain)


def local(
    hidden_in,
    cotangent,
    gain_attn,
    w_query,
    w_key,
    w_value,
    w_output,
    gain_mlp,
    w_gate,
    w_up,
    w_down,
):
    row_count = hidden_in.shape[2]
    length = row_count * lax.axis_size("tensor")
    cos_t, sin_t = tables(length, HD)
    causal = lax.broadcasted_iota(jnp.int32, (length, length), 0) >= lax.broadcasted_iota(
        jnp.int32, (length, length), 1
    )
    score_scale = HD ** (-0.5)

    rows_in, grad_rows_out = hidden_in[:, 0], cotangent[:, 0]
    micro = rows_in.shape[0]
    gain_one = lax.all_gather(gain_attn, "fsdp", axis=0, tiled=True).astype(jnp.float32)
    gain_two = lax.all_gather(gain_mlp, "fsdp", axis=0, tiled=True).astype(jnp.float32)
    qkv_w = lax.all_gather(
        jnp.concatenate([w_query, w_key, w_value], axis=1), "fsdp", axis=0, tiled=True
    )
    gu_w = lax.all_gather(jnp.concatenate([w_gate, w_up], axis=1), "fsdp", axis=0, tiled=True)
    od_w = lax.all_gather(jnp.concatenate([w_output, w_down], axis=0), "fsdp", axis=1, tiled=True)
    width = w_query.shape[1]
    units = w_gate.shape[1]
    output_w, down_w = od_w[:width], od_w[width:]
    rows_all = micro * length

    def gather(rows):
        return lax.all_gather(rows.astype(jnp.bfloat16), "tensor", axis=1, tiled=True).reshape(
            rows_all, rows.shape[-1]
        )

    def scatter(rows):
        return lax.psum_scatter(
            rows.astype(jnp.bfloat16).reshape(micro, length, -1),
            "tensor",
            scatter_dimension=1,
            tiled=True,
        ).astype(jnp.float32)

    def dot(left, right, dims):
        return lax.dot_general(left, right, (dims, ((), ())), preferred_element_type=jnp.float32)

    x_float = rows_in.astype(jnp.float32)
    normed_one, factor_one = norm_forward(x_float, gain_one)
    first_rows = gather(normed_one)
    grad_full = gather(grad_rows_out)
    qkv = dot(first_rows, qkv_w, ((1,), (0,)))

    def heads(part):
        return part.reshape(micro, length, HD)

    cos_t, sin_t = cos_t[:, 0], sin_t[:, 0]
    queries = rotate(heads(qkv[:, :width]), cos_t, sin_t).astype(jnp.bfloat16)
    keys_rot = rotate(heads(qkv[:, width : 2 * width]), cos_t, sin_t).astype(jnp.bfloat16)
    values = heads(qkv[:, 2 * width :]).astype(jnp.bfloat16)
    scores = (
        jnp.einsum("mqd,mkd->mqk", queries, keys_rot, preferred_element_type=jnp.float32)
        * score_scale
    )
    scores = jnp.where(causal[None], scores, -jnp.inf)
    row_peak = jnp.max(scores, axis=-1, keepdims=True)
    log_total = row_peak + jnp.log(jnp.sum(jnp.exp(scores - row_peak), axis=-1, keepdims=True))
    probs = jnp.exp(scores - log_total)
    probs_low = probs.astype(jnp.bfloat16)
    mixed = jnp.einsum("mqk,mkd->mqd", probs_low, values, preferred_element_type=jnp.float32)
    mixed = mixed.astype(jnp.bfloat16).reshape(rows_all, width)
    middle = x_float + scatter(dot(mixed, output_w, ((1,), (0,))))
    normed_two, factor_two = norm_forward(middle, gain_two)
    second_rows = gather(normed_two)
    gu = dot(second_rows, gu_w, ((1,), (0,)))
    gate_pre, up_pre = gu[:, :units], gu[:, units:]
    gate_sig = jax.nn.sigmoid(gate_pre)
    silu_val = gate_pre * gate_sig
    hidden = (silu_val * up_pre).astype(jnp.bfloat16)
    block_rows = middle + scatter(dot(hidden, down_w, ((1,), (0,))))
    down_grad = dot(hidden, grad_full, ((0,), (0,)))
    grad_hidden = dot(grad_full, down_w, ((1,), (1,)))
    grad_gu = jnp.concatenate(
        [
            grad_hidden * up_pre * gate_sig * (1.0 + gate_pre * (1.0 - gate_sig)),
            grad_hidden * silu_val,
        ],
        axis=1,
    ).astype(jnp.bfloat16)
    gu_grad = dot(second_rows, grad_gu, ((0,), (0,)))
    grad_second = scatter(dot(grad_gu, gu_w, ((1,), (1,))))
    grad_mid_norm, gain_two_grad = norm_backward(grad_second, middle, factor_two, gain_two)
    grad_middle = grad_rows_out.astype(jnp.float32) + grad_mid_norm
    middle_full = gather(grad_middle)
    output_grad = dot(mixed, middle_full, ((0,), (0,)))
    grad_mixed = dot(middle_full, output_w, ((1,), (1,))).astype(jnp.bfloat16)
    grad_mixed = grad_mixed.reshape(micro, length, HD)
    grad_values = jnp.einsum(
        "mqk,mqd->mkd", probs_low, grad_mixed, preferred_element_type=jnp.float32
    )
    grad_probs = jnp.einsum(
        "mqd,mkd->mqk", grad_mixed, values, preferred_element_type=jnp.float32
    )
    row_dot = jnp.sum(probs * grad_probs, axis=-1, keepdims=True)
    grad_scores = (probs * (grad_probs - row_dot)).astype(jnp.bfloat16)
    grad_queries = (
        jnp.einsum("mqk,mkd->mqd", grad_scores, keys_rot, preferred_element_type=jnp.float32)
        * score_scale
    )
    grad_keys = (
        jnp.einsum("mqk,mqd->mkd", grad_scores, queries, preferred_element_type=jnp.float32)
        * score_scale
    )
    qkv_back = jnp.concatenate(
        [
            rotate_back(grad_queries, cos_t, sin_t).reshape(rows_all, width),
            rotate_back(grad_keys, cos_t, sin_t).reshape(rows_all, width),
            grad_values.reshape(rows_all, width),
        ],
        axis=1,
    ).astype(jnp.bfloat16)
    qkv_grad = dot(first_rows, qkv_back, ((0,), (0,)))
    grad_first = scatter(dot(qkv_back, qkv_w, ((1,), (1,))))
    grad_in_norm, gain_one_grad = norm_backward(grad_first, x_float, factor_one, gain_one)
    grad_input = grad_middle + grad_in_norm

    def owned(total, axis):
        return lax.psum_scatter(
            total.astype(jnp.bfloat16), "fsdp", scatter_dimension=axis, tiled=True
        ).astype(jnp.float32)

    gain_sums = lax.psum(jnp.stack([gain_one_grad, gain_two_grad]), "tensor")
    gain_owned = owned(gain_sums, 1)
    gu_owned = owned(gu_grad, 0)
    od_owned = owned(jnp.concatenate([output_grad, down_grad], axis=0), 1)
    qkv_owned = owned(qkv_grad, 0)
    return (
        block_rows.astype(jnp.bfloat16)[:, None],
        grad_input.astype(jnp.bfloat16)[:, None],
        gain_owned[0],
        qkv_owned[:, :width],
        qkv_owned[:, width : 2 * width],
        qkv_owned[:, 2 * width :],
        od_owned[:width],
        gain_owned[1],
        gu_owned[:, :units],
        gu_owned[:, units:],
        od_owned[width:],
    )


def solution(mesh):
    placed = (
        P(None, "fsdp", "tensor", None),
        P(None, "fsdp", "tensor", None),
        P("fsdp"),
        P("fsdp", "tensor"),
        P("fsdp", "tensor"),
        P("fsdp", "tensor"),
        P("tensor", "fsdp"),
        P("fsdp"),
        P("fsdp", "tensor"),
        P("fsdp", "tensor"),
        P("tensor", "fsdp"),
    )
    return jax.shard_map(
        local,
        mesh=mesh,
        in_specs=placed,
        out_specs=(
            P(None, "fsdp", "tensor", None),
            P(None, "fsdp", "tensor", None),
            P("fsdp"),
            P("fsdp", "tensor"),
            P("fsdp", "tensor"),
            P("fsdp", "tensor"),
            P("tensor", "fsdp"),
            P("fsdp"),
            P("fsdp", "tensor"),
            P("fsdp", "tensor"),
            P("tensor", "fsdp"),
        ),
        check_vma=False,
    )
```

```python
import jax
import jax.numpy as jnp
from jax import lax
from jax.experimental import pallas as pl
from jax.experimental.pallas import tpu as pltpu
from jax.sharding import PartitionSpec as P


HD = 128
UNITS = 384
EPSILON = 1e-05
THETA = 10000.0
MESH = pl.DeviceIdType.MESH
F32 = jnp.float32
BF16 = jnp.bfloat16
COPIES = 128
ANY = pl.BlockSpec(memory_space=pl.ANY)
VMEM = pl.BlockSpec(memory_space=pltpu.VMEM)


def wrap(value, size):
    return lax.rem(value, size)


class Place:
    def __init__(self):
        f = lax.axis_index("fsdp")
        t = lax.axis_index("tensor")
        self.x, self.zl = lax.div(f, 2), lax.rem(f, 2)
        self.y, self.m = lax.div(t, 4), lax.rem(t, 4)
        self.zh, self.c = lax.div(self.m, 2), lax.rem(self.m, 2)
        self.z = 2 * self.zh + self.zl

    def at(self, x=None, z=None, y=None, c=None):
        x = self.x if x is None else x
        z = self.z if z is None else z
        y = self.y if y is None else y
        c = self.c if c is None else c
        return (2 * x + lax.rem(z, 2), 4 * y + 2 * lax.div(z, 2) + c)

    def x_of(self, d):
        return wrap(self.x + d, 4)

    def y_of(self, d):
        return wrap(self.y + d, 4)

    def z_of(self, d):
        z = wrap(self.z + d, 4)
        return z, lax.div(z, 2), lax.rem(z, 2)

    def quad(self, j):
        zh = 1 - self.zh if j & 2 else self.zh
        c = 1 - self.c if j & 1 else self.c
        return self.at(z=2 * zh + self.zl, c=c), 2 * zh + c

    def sibling(self):
        return self.at(c=1 - self.c)

    def cols(self, zh, width):
        return pl.ds(pl.multiple_of((2 * self.c + zh) * width, 128), width)

    def core_cols(self, c, width):
        return pl.ds(pl.multiple_of(2 * c * width, 128), 2 * width)


class Copies:
    def __init__(self, send, recv, here):
        self.send, self.recv, self.here = send, recv, here
        self.sent, self.kept = [], 0

    def push(self, src, dst, device):
        k = len(self.sent)
        copy = pltpu.make_async_remote_copy(
            src_ref=src,
            dst_ref=dst,
            send_sem=self.send.at[k],
            recv_sem=self.recv.at[k],
            device_id=device,
            device_id_type=MESH,
        )
        copy.start()
        self.sent.append(copy)
        return copy

    def local(self, src, dst):
        copy = pltpu.make_async_copy(src, dst, self.here.at[self.kept])
        copy.start()
        self.kept += 1
        return copy

    def drain(self):
        for copy in self.sent:
            copy.wait_send()


def enter(place):
    barrier = pltpu.get_barrier_semaphore()
    others = [place.at(y=place.y_of(d)) for d in (1, 2, 3)]
    others += [place.at(x=place.x_of(d)) for d in (1, 2, 3)]
    others += [place.at(z=place.z_of(d)[0]) for d in (1, 2, 3)]
    others += [place.quad(1)[0], place.quad(3)[0]]
    for other in others:
        pl.semaphore_signal(barrier, inc=1, device_id=other, device_id_type=MESH)
    pl.semaphore_wait(barrier, len(others))


class Gather:
    def __init__(self, copies, place, block, whole, width):
        self.copies, self.place, self.whole, self.width = copies, place, whole, width
        own = place.cols(place.zh, width)
        self.own = copies.local(block, whole.at[place.x, place.zl, :, own])
        self.first = []
        for d in (1, 2, 3):
            self.first.append(
                copies.push(
                    block.at[pl.ds(0, 128)],
                    whole.at[place.x, place.zl, pl.ds(0, 128), own],
                    place.at(x=place.x_of(d)),
                )
            )
            self.first.append(
                copies.push(
                    block.at[pl.ds(128, 128)],
                    whole.at[place.x, place.zl, pl.ds(128, 128), own],
                    place.at(z=place.z_of(d)[0]),
                )
            )

    def spread(self):
        place, width = self.place, self.width
        self.own.wait()
        for copy in self.first:
            copy.wait_recv()
        upper = self.whole.at[:, place.zl, pl.ds(0, 128), place.cols(place.zh, width)]
        lower = self.whole.at[place.x, :, pl.ds(128, 128), place.core_cols(place.c, width)]
        self.upper, self.lower = [], []
        for d in (1, 2, 3):
            self.upper.append(self.copies.push(upper, upper, place.at(z=place.z_of(d)[0])))
            self.lower.append(self.copies.push(lower, lower, place.at(x=place.x_of(d))))

    def share(self):
        place, width = self.place, self.width
        self.shared = []
        for arrivals, start in ((self.upper, 0), (self.lower, 128)):
            for copy in arrivals:
                copy.wait_recv()
            part = self.whole.at[:, :, pl.ds(start, 128), place.core_cols(place.c, width)]
            self.shared.append(self.copies.push(part, part, place.sibling()))

    def finish(self):
        for copy in self.shared:
            copy.wait_recv()


def reduce_scratch(width):
    return [
        pltpu.VMEM((4, 2, 256, 2 * width), BF16),
        pltpu.VMEM((4, 2, 256, 2 * width), BF16),
        pltpu.VMEM((3, 4, 128, width), BF16),
        pltpu.VMEM((3, 2, 128, 2 * width), BF16),
        pltpu.VMEM((4, 128, width), BF16),
        pltpu.VMEM((2, 128, 2 * width), BF16),
        pltpu.VMEM((3, 128, width), BF16),
        pltpu.VMEM((3, 128, width), BF16),
    ]


class Reduce:
    def __init__(self, copies, place, whole, out, scratch, width):
        self.copies, self.place, self.out, self.width = copies, place, out, width
        self.mine, self.theirs = scratch[:2]
        self.upper_in, self.lower_in, self.upper, self.lower = scratch[2:6]
        self.upper_last, self.lower_last = scratch[6:]
        self.swap = copies.push(
            whole.at[:, :, :, place.core_cols(1 - place.c, width)], self.theirs, place.sibling()
        )
        self.own = copies.local(whole.at[:, :, :, place.core_cols(place.c, width)], self.mine)

    def half(self, zh):
        return pl.ds(pl.multiple_of(zh * self.width, 128), self.width)

    def first(self):
        place, mine, theirs = self.place, self.mine, self.theirs
        self.own.wait()
        self.swap.wait_recv()

        def add(i, carry):
            x, zl, rows = lax.div(i, 8), lax.rem(lax.div(i, 4), 2), lax.rem(i, 4) * 64
            where = (x, zl, pl.ds(pl.multiple_of(rows, 64), 64), slice(None))
            mine[where] = (mine[where].astype(F32) + theirs[where].astype(F32)).astype(BF16)
            return carry

        lax.fori_loop(0, 32, add, 0)
        self.upper_sent, self.lower_sent = [], []
        for d in (1, 2, 3):
            z, zh, zl = place.z_of(d)
            self.upper_sent.append(
                self.copies.push(
                    mine.at[:, zl, pl.ds(0, 128), self.half(zh)],
                    self.upper_in.at[d - 1],
                    place.at(z=z),
                )
            )
            x = place.x_of(d)
            self.lower_sent.append(
                self.copies.push(
                    mine.at[x, :, pl.ds(128, 128), :], self.lower_in.at[d - 1], place.at(x=x)
                )
            )

    def second(self):
        place, mine = self.place, self.mine
        for copy in self.upper_sent:
            copy.wait_recv()

        def add_upper(x, carry):
            total = mine[x, place.zl, pl.ds(0, 128), self.half(place.zh)].astype(F32)
            for d in range(3):
                total += self.upper_in[d, x].astype(F32)
            self.upper[x] = total.astype(BF16)
            return carry

        lax.fori_loop(0, 4, add_upper, 0)
        self.upper_done, self.lower_done = [], []
        for d in (1, 2, 3):
            x = place.x_of(d)
            self.upper_done.append(
                self.copies.push(self.upper.at[x], self.upper_last.at[d - 1], place.at(x=x))
            )
        for copy in self.lower_sent:
            copy.wait_recv()

        def add_lower(zl, carry):
            total = mine[place.x, zl, pl.ds(128, 128), :].astype(F32)
            for d in range(3):
                total += self.lower_in[d, zl].astype(F32)
            self.lower[zl] = total.astype(BF16)
            return carry

        lax.fori_loop(0, 2, add_lower, 0)
        for d in (1, 2, 3):
            z, zh, zl = place.z_of(d)
            self.lower_done.append(
                self.copies.push(
                    self.lower.at[zl, :, self.half(zh)], self.lower_last.at[d - 1], place.at(z=z)
                )
            )

    def finish(self):
        place = self.place
        for copy in self.upper_done:
            copy.wait_recv()
        total = self.upper[place.x].astype(F32)
        for d in range(3):
            total += self.upper_last[d].astype(F32)
        self.out[pl.ds(0, 128), :] = total
        for copy in self.lower_done:
            copy.wait_recv()
        total = self.lower[place.zl, :, self.half(place.zh)].astype(F32)
        for d in range(3):
            total += self.lower_last[d].astype(F32)
        self.out[pl.ds(128, 128), :] = total


class Spread:
    def __init__(self, copies, place, held, rows):
        self.copies, self.place, self.rows = copies, place, rows
        mine = rows.at[place.y, place.m]
        self.own = copies.local(held.at[place.m], mine)
        self.quad = []
        for j in (1, 2, 3):
            device, m = place.quad(j)
            self.quad.append((copies.push(held.at[m], mine, device), m))

    def along(self):
        place = self.place
        self.arrivals = []
        self.own.wait()
        parts = [place.m]
        for j, part in enumerate([(None, place.m)] + self.quad):
            if part[0] is not None:
                part[0].wait_recv()
            block = self.rows.at[place.y, part[1]]
            for d in (1, 2, 3):
                self.arrivals.append(
                    self.copies.push(block, block, place.at(y=place.y_of(d)))
                )

    def finish(self):
        for copy in self.arrivals:
            copy.wait_recv()


class RowSum:
    def __init__(self, copies, place, part, arrived, own):
        self.arrived, self.own = arrived, own
        self.kept = copies.local(part.at[place.y], own)
        self.sent = []
        for k in range(4):
            rows = pl.ds(32 * k, 32)
            self.sent.append(
                [
                    copies.push(
                        part.at[place.y_of(d), rows],
                        arrived.at[d - 1, rows],
                        place.at(y=place.y_of(d)),
                    )
                    for d in (1, 2, 3)
                ]
            )

    def total(self, k):
        if k == 0:
            self.kept.wait()
        rows = pl.ds(32 * k, 32)
        total = self.own[rows, :].astype(F32)
        for d, copy in enumerate(self.sent[k]):
            copy.wait_recv()
            total += self.arrived[d, rows, :].astype(F32)
        return total


class RowSend:
    def __init__(self, copies, place, stage, whole):
        self.copies, self.place, self.stage, self.whole = copies, place, stage, whole
        self.arrivals, self.own = [], []

    def send(self, k):
        rows = pl.ds(32 * k, 32)
        mine = self.whole.at[self.place.y, rows]
        for d in (1, 2, 3):
            self.arrivals.append(
                self.copies.push(
                    self.stage.at[rows], mine, self.place.at(y=self.place.y_of(d))
                )
            )
        self.own.append(self.copies.local(self.stage.at[rows], mine))

    def finish(self):
        for copy in self.arrivals:
            copy.wait_recv()
        for copy in self.own:
            copy.wait()


def factor_of(rows):
    return lax.rsqrt(jnp.mean(rows * rows, axis=-1, keepdims=True) + EPSILON)


def norm_back(grad, rows, gain):
    factor = factor_of(rows)
    scaled = grad * gain
    back = factor * scaled - rows * factor**3 * jnp.mean(scaled * rows, axis=-1, keepdims=True)
    return back, jnp.sum(grad * rows * factor, axis=0, keepdims=True)


def first_kernel(held, qkv, out, gains, rows, qkv_all, out_all, gains_all, send, recv, here):
    place = Place()
    enter(place)
    copies = Copies(send, recv, here)
    spread = Spread(copies, place, held, rows)
    own_gain = copies.local(gains, gains_all.at[place.x, place.zl])
    gain_first = [
        copies.push(gains, gains_all.at[place.x, place.zl], place.at(x=place.x_of(d)))
        for d in (1, 2, 3)
    ]
    gathers = [
        Gather(copies, place, qkv, qkv_all, 3 * HD),
        Gather(copies, place, out, out_all, HD),
    ]
    spread.along()
    own_gain.wait()
    for copy in gain_first:
        copy.wait_recv()
    column = gains_all.at[:, place.zl]
    gain_last = copies.push(column, column, place.at(z=2 * place.zh + 1 - place.zl))
    for gather in gathers:
        gather.spread()
    for gather in gathers:
        gather.share()
    spread.finish()
    gain_last.wait_recv()
    for gather in gathers:
        gather.finish()
    copies.drain()


def second_kernel(
    part, rows, gains, held, gate, up, down,
    normed, grads, middle, gate_all, up_all, down_all,
    arrived, own, x_own, stage, send, recv, here,
):
    place = Place()
    enter(place)
    copies = Copies(send, recv, here)
    total = RowSum(copies, place, part, arrived, own)
    mine = copies.local(rows.at[place.y], x_own)
    spread = Spread(copies, place, held, grads)
    gathers = [
        Gather(copies, place, gate, gate_all, UNITS),
        Gather(copies, place, up, up_all, UNITS),
        Gather(copies, place, down, down_all, UNITS),
    ]
    spread.along()
    mine.wait()
    sender = RowSend(copies, place, stage, normed)
    gain = gains[1:2, :]
    for k in range(4):
        if k < 3:
            gathers[k].spread()
        now = pl.ds(32 * k, 32)
        mid = x_own[now, :].astype(F32) + total.total(k)
        middle[now, :] = mid
        stage[now, :] = (mid * factor_of(mid) * gain).astype(BF16)
        sender.send(k)
    for gather in gathers:
        gather.share()
    spread.finish()
    sender.finish()
    for gather in gathers:
        gather.finish()
    copies.drain()


def third_kernel(
    part, down_part, middle, gains, grads, gate, up, down,
    mid_all, mid_grad, gain_grad, block_out, gate_out, up_out, down_out,
    arrived, own, down_arrived, down_own, dy_own, stage, out_stage, send, recv, here, *scratch,
):
    place = Place()
    enter(place)
    copies = Copies(send, recv, here)
    total = RowSum(copies, place, part, arrived, own)
    mine = copies.local(grads.at[place.y], dy_own)
    reduces = [
        Reduce(copies, place, whole, out, scratch[8 * i : 8 * i + 8], UNITS)
        for i, (whole, out) in enumerate(((down, down_out), (gate, gate_out), (up, up_out)))
    ]
    down_total = RowSum(copies, place, down_part, down_arrived, down_own)
    mine.wait()
    sender = RowSend(copies, place, stage, mid_all)
    gain = gains[1:2, :]
    gain_total = jnp.zeros((1, gain.shape[1]), F32)
    for k in range(4):
        now = pl.ds(32 * k, 32)
        if k < 3:
            reduces[k].first()
        back, gain_part = norm_back(total.total(k), middle[now, :], gain)
        gain_total += gain_part
        back += dy_own[now, :].astype(F32)
        mid_grad[now, :] = back
        stage[now, :] = back.astype(BF16)
        sender.send(k)
    gain_grad[...] = jnp.broadcast_to(gain_total, gain_grad.shape)
    for k in range(4):
        now = pl.ds(32 * k, 32)
        if k < 3:
            reduces[k].second()
        out_stage[k] = (middle[now, :] + down_total.total(k)).astype(BF16)
    spread = [copies.local(out_stage.at[place.m], block_out.at[place.m])]
    arrivals = []
    for j in (1, 2, 3):
        device, m = place.quad(j)
        arrivals.append(copies.push(out_stage.at[m], block_out.at[place.m], device))
    for reduce in reduces:
        reduce.finish()
    sender.finish()
    spread[0].wait()
    for copy in arrivals:
        copy.wait_recv()
    copies.drain()


def fourth_kernel(
    part, rows, gains, mid_grad, gain_grad, qkv, out,
    grad_in, gains_out, qkv_out, out_out,
    arrived, own, x_own, out_stage, vec, vec_y, vec_x, vec_z, vec_c, half_x, half_z, half_c,
    send, recv, here, *scratch,
):
    place = Place()
    enter(place)
    copies = Copies(send, recv, here)
    total = RowSum(copies, place, part, arrived, own)
    mine = copies.local(rows.at[place.y], x_own)
    reduces = [
        Reduce(copies, place, qkv, qkv_out, scratch[:8], 3 * HD),
        Reduce(copies, place, out, out_out, scratch[8:], HD),
    ]
    mine.wait()
    gain = gains[0:1, :]
    gain_total = jnp.zeros((1, gain.shape[1]), F32)
    reduces[0].first()
    reduces[1].first()
    for k in range(4):
        now = pl.ds(32 * k, 32)
        x_rows = x_own[now, :].astype(F32)
        back, gain_part = norm_back(total.total(k), x_rows, gain)
        gain_total += gain_part
        out_stage[k] = (mid_grad[now, :] + back).astype(BF16)
    vec[0:1, :] = gain_total
    vec[1:2, :] = gain_grad[0:1, :]
    vec[2:8, :] = jnp.zeros((6, gain.shape[1]), F32)
    here_out = copies.local(out_stage.at[place.m], grad_in.at[place.m])
    arrivals = []
    for j in (1, 2, 3):
        device, m = place.quad(j)
        arrivals.append(copies.push(out_stage.at[m], grad_in.at[place.m], device))
    gain_y = [
        copies.push(vec, vec_y.at[d - 1], place.at(y=place.y_of(d))) for d in (1, 2, 3)
    ]
    reduces[0].second()
    for copy in gain_y:
        copy.wait_recv()
    half_x[...] = vec[...] + vec_y[0] + vec_y[1] + vec_y[2]

    def of_x(x):
        return pl.ds(pl.multiple_of(x * 512, 128), 512)

    def of_z(zl):
        return pl.ds(pl.multiple_of(zl * 256, 128), 256)

    gain_x = [
        copies.push(
            half_x.at[:, of_x(place.x_of(d))], vec_x.at[d - 1], place.at(x=place.x_of(d))
        )
        for d in (1, 2, 3)
    ]
    reduces[1].second()
    for copy in gain_x:
        copy.wait_recv()
    half_z[...] = half_x[:, of_x(place.x)] + vec_x[0] + vec_x[1] + vec_x[2]
    gain_z = []
    for d in (1, 2, 3):
        z, zh, zl = place.z_of(d)
        gain_z.append(copies.push(half_z.at[:, of_z(zl)], vec_z.at[d - 1], place.at(z=z)))
    for copy in gain_z:
        copy.wait_recv()
    half_c[...] = half_z[:, of_z(place.zl)] + vec_z[0] + vec_z[1] + vec_z[2]
    gain_c = copies.push(half_c, vec_c, place.sibling())
    for reduce in reduces:
        reduce.finish()
    gain_c.wait_recv()
    gains_out[...] = half_c[...] + vec_c[...]
    here_out.wait()
    for copy in arrivals:
        copy.wait_recv()
    copies.drain()


def call(kernel, number, args, in_specs, outs, out_specs, scratch=(), tail=()):
    return pl.pallas_call(
        kernel,
        out_shape=[jax.ShapeDtypeStruct(shape, dtype) for shape, dtype in outs],
        in_specs=in_specs,
        out_specs=out_specs,
        scratch_shapes=[
            *scratch,
            pltpu.SemaphoreType.DMA((COPIES,)),
            pltpu.SemaphoreType.DMA((COPIES,)),
            pltpu.SemaphoreType.DMA((16,)),
            *tail,
        ],
        compiler_params=pltpu.CompilerParams(
            collective_id=number, has_side_effects=True, vmem_limit_bytes=52 * 2**20
        ),
    )(*args)


def tables(length):
    half_size = HD // 2
    inverse_freq = THETA ** (-(jnp.arange(half_size, dtype=F32) * 2.0) / HD)
    angles = jnp.arange(length, dtype=F32)[:, None] * inverse_freq[None, :]
    return jnp.cos(angles), jnp.sin(angles)


def rotate(tensor, cos_t, sin_t):
    u, w = tensor[..., : HD // 2], tensor[..., HD // 2 :]
    return jnp.concatenate([u * cos_t - w * sin_t, w * cos_t + u * sin_t], axis=-1)


def rotate_back(tensor, cos_t, sin_t):
    return rotate(tensor, cos_t, -sin_t)


def dot(left, right, dims):
    return lax.dot_general(left, right, (dims, ((), ())), preferred_element_type=F32)


def product(left, right):
    return dot(left, right, ((1,), (0,)))


def product_t(left, right):
    return dot(left, right, ((1,), (1,)))


def t_product(left, right):
    return dot(left, right, ((0,), (0,)))


def local(
    hidden_in,
    cotangent,
    gain_attn,
    w_query,
    w_key,
    w_value,
    w_output,
    gain_mlp,
    w_gate,
    w_up,
    w_down,
):
    held, grad_held = hidden_in[:, 0], cotangent[:, 0]
    width = held.shape[2]
    length = 512
    units = w_gate.shape[1]

    def wide(weight):
        return jnp.pad(weight, ((0, 0), (0, UNITS - units)))

    qkv = jnp.concatenate([w_query, w_key, w_value], axis=1)
    gains = jnp.pad(jnp.stack([gain_attn, gain_mlp]).astype(F32), ((0, 6), (0, 0)))
    rows, qkv_w, out_w, gains_all = call(
        first_kernel,
        0,
        (held, qkv, w_output.T, gains),
        [ANY] * 4,
        [
            ((4, 4, 32, width), BF16),
            ((4, 2, 256, 12 * HD), BF16),
            ((4, 2, 256, 4 * HD), BF16),
            ((4, 2, 8, 256), F32),
        ],
        [ANY] * 4,
    )
    gains_row = gains_all.transpose(2, 0, 1, 3).reshape(8, width)
    qkv_w = qkv_w.reshape(width, 12 * HD)
    out_w = out_w.reshape(width, 4 * HD)
    cos_t, sin_t = tables(length)
    x_full = rows.reshape(length, width).astype(F32)
    first_rows = (x_full * factor_of(x_full) * gains_row[0:1]).astype(BF16)
    projected = product(first_rows, qkv_w).reshape(length, 4, 3, HD).transpose(1, 2, 0, 3)
    queries = rotate(projected[:, 0], cos_t, sin_t).astype(BF16)
    keys = rotate(projected[:, 1], cos_t, sin_t).astype(BF16)
    values = projected[:, 2].astype(BF16)
    causal = lax.broadcasted_iota(jnp.int32, (length, length), 0) >= lax.broadcasted_iota(
        jnp.int32, (length, length), 1
    )
    scale = HD**-0.5

    def bmm(spec, left, right):
        return jnp.einsum(spec, left, right, preferred_element_type=F32)

    scores = jnp.where(causal, bmm("hqd,hkd->hqk", queries, keys) * scale, -jnp.inf)
    peak = jnp.max(scores, axis=-1, keepdims=True)
    log_total = peak + jnp.log(jnp.sum(jnp.exp(scores - peak), axis=-1, keepdims=True))
    probs = jnp.exp(scores - log_total)
    probs_low = probs.astype(BF16)
    mixed = bmm("hqk,hkd->qhd", probs_low, values).astype(BF16).reshape(length, 4 * HD)
    out_part = product_t(mixed, out_w).astype(BF16).reshape(4, 128, width)

    normed, grads, middle, gate_w, up_w, down_w = call(
        second_kernel,
        1,
        (out_part, rows.reshape(4, 128, width), gains_row, grad_held,
         wide(w_gate), wide(w_up), wide(w_down.T)),
        [ANY, ANY, VMEM] + [ANY] * 4,
        [
            ((4, 128, width), BF16),
            ((4, 4, 32, width), BF16),
            ((128, width), F32),
            ((4, 2, 256, 4 * UNITS), BF16),
            ((4, 2, 256, 4 * UNITS), BF16),
            ((4, 2, 256, 4 * UNITS), BF16),
        ],
        [ANY, ANY, VMEM, ANY, ANY, ANY],
        [
            pltpu.VMEM((3, 128, width), BF16),
            pltpu.VMEM((128, width), BF16),
            pltpu.VMEM((128, width), BF16),
            pltpu.VMEM((128, width), BF16),
        ],
    )
    second_rows = normed.reshape(length, width)
    grad_full = grads.reshape(length, width)
    gate_w, up_w, down_w = (w.reshape(width, 4 * UNITS) for w in (gate_w, up_w, down_w))
    gate = product(second_rows, gate_w)
    up = product(second_rows, up_w)
    sig = jax.nn.sigmoid(gate)
    silu = gate * sig
    hidden = (silu * up).astype(BF16)
    down_part = product_t(hidden, down_w).astype(BF16).reshape(4, 128, width)
    grad_hidden = product(grad_full, down_w)
    grad_gate = (grad_hidden * up * sig * (1.0 + gate * (1.0 - sig))).astype(BF16)
    grad_up = (grad_hidden * silu).astype(BF16)
    second_part = (product_t(grad_gate, gate_w) + product_t(grad_up, up_w)).astype(BF16)

    def plane(total):
        return total.astype(BF16).reshape(4, 2, 256, total.shape[1])

    mid_all, mid_grad, gain_grad, block_out, gate_g, up_g, down_g = call(
        third_kernel,
        2,
        (second_part.reshape(4, 128, width), down_part, middle, gains_row,
         grads.reshape(4, 128, width), plane(t_product(second_rows, grad_gate)),
         plane(t_product(second_rows, grad_up)), plane(t_product(grad_full, hidden))),
        [ANY, ANY, VMEM, VMEM] + [ANY] * 4,
        [
            ((4, 128, width), BF16),
            ((128, width), F32),
            ((8, width), F32),
            ((4, 32, width), BF16),
            ((256, UNITS), F32),
            ((256, UNITS), F32),
            ((256, UNITS), F32),
        ],
        [ANY, VMEM, VMEM, ANY, VMEM, VMEM, VMEM],
        [
            pltpu.VMEM((3, 128, width), BF16),
            pltpu.VMEM((128, width), BF16),
            pltpu.VMEM((3, 128, width), BF16),
            pltpu.VMEM((128, width), BF16),
            pltpu.VMEM((128, width), BF16),
            pltpu.VMEM((128, width), BF16),
            pltpu.VMEM((4, 32, width), BF16),
        ],
        reduce_scratch(UNITS) * 3,
    )
    mid_full = mid_all.reshape(length, width)
    grad_mixed = product(mid_full, out_w).astype(BF16).reshape(length, 4, HD).transpose(1, 0, 2)
    grad_values = bmm("hqk,hqd->hkd", probs_low, grad_mixed)
    grad_probs = bmm("hqd,hkd->hqk", grad_mixed, values)
    row_dot = jnp.sum(probs * grad_probs, axis=-1, keepdims=True)
    grad_scores = (probs * (grad_probs - row_dot)).astype(BF16)
    grad_queries = bmm("hqk,hkd->hqd", grad_scores, keys) * scale
    grad_keys = bmm("hqk,hqd->hkd", grad_scores, queries) * scale
    qkv_grad = jnp.stack(
        [
            rotate_back(grad_queries, cos_t, sin_t).astype(BF16),
            rotate_back(grad_keys, cos_t, sin_t).astype(BF16),
            grad_values.astype(BF16),
        ],
        axis=1,
    )
    qkv_grad = qkv_grad.transpose(2, 0, 1, 3).reshape(length, 12 * HD)
    first_part = product_t(qkv_grad, qkv_w).astype(BF16).reshape(4, 128, width)

    grad_in, gains_out, qkv_g, out_g = call(
        fourth_kernel,
        3,
        (first_part, rows.reshape(4, 128, width), gains_row, mid_grad, gain_grad,
         plane(t_product(first_rows, qkv_grad)), plane(t_product(mid_full, mixed))),
        [ANY, ANY, VMEM, VMEM, VMEM, ANY, ANY],
        [
            ((4, 32, width), BF16),
            ((8, 256), F32),
            ((256, 3 * HD), F32),
            ((256, HD), F32),
        ],
        [ANY, VMEM, VMEM, VMEM],
        [
            pltpu.VMEM((3, 128, width), BF16),
            pltpu.VMEM((128, width), BF16),
            pltpu.VMEM((128, width), BF16),
            pltpu.VMEM((4, 32, width), BF16),
            pltpu.VMEM((8, width), F32),
            pltpu.VMEM((3, 8, width), F32),
            pltpu.VMEM((3, 8, 512), F32),
            pltpu.VMEM((3, 8, 256), F32),
            pltpu.VMEM((8, 256), F32),
            pltpu.VMEM((8, width), F32),
            pltpu.VMEM((8, 512), F32),
            pltpu.VMEM((8, 256), F32),
        ],
        reduce_scratch(3 * HD) + reduce_scratch(HD),
    )
    return (
        block_out[:, None],
        grad_in[:, None],
        gains_out[0],
        qkv_g[:, :HD],
        qkv_g[:, HD : 2 * HD],
        qkv_g[:, 2 * HD :],
        out_g.T,
        gains_out[1],
        gate_g[:, :units],
        up_g[:, :units],
        down_g[:, :units].T,
    )


def solution(mesh):
    rows = P(None, "fsdp", "tensor", None)
    into, out_of = P("fsdp", "tensor"), P("tensor", "fsdp")
    return jax.shard_map(
        local,
        mesh=mesh,
        in_specs=(
            rows, rows, P("fsdp"), into, into, into, out_of, P("fsdp"), into, into, out_of,
        ),
        out_specs=(
            rows, rows, P("fsdp"), into, into, into, out_of, P("fsdp"), into, into, out_of,
        ),
        check_vma=False,
    )
```

```python
import jax
import jax.numpy as jnp
from jax import lax
from jax.experimental import pallas as pl
from jax.experimental.pallas import tpu as pltpu
from jax.sharding import PartitionSpec as P


HD = 128
UNITS = 384
EPSILON = 1e-05
THETA = 10000.0
MESH = pl.DeviceIdType.MESH
F32 = jnp.float32
BF16 = jnp.bfloat16
COPIES = 176
LOCALS = 62
TILES = 8
ANY = pl.BlockSpec(memory_space=pl.ANY)
VMEM = pl.BlockSpec(memory_space=pltpu.VMEM)


def wrap(value, size):
    return lax.rem(value, size)


class Place:
    def __init__(self):
        f = lax.axis_index("fsdp")
        t = lax.axis_index("tensor")
        self.x, self.zl = lax.div(f, 2), lax.rem(f, 2)
        self.y, self.m = lax.div(t, 4), lax.rem(t, 4)
        self.zh, self.c = lax.div(self.m, 2), lax.rem(self.m, 2)
        self.z = 2 * self.zh + self.zl

    def at(self, x=None, z=None, y=None, c=None):
        x = self.x if x is None else x
        z = self.z if z is None else z
        y = self.y if y is None else y
        c = self.c if c is None else c
        return (2 * x + lax.rem(z, 2), 4 * y + 2 * lax.div(z, 2) + c)

    def x_of(self, d):
        return wrap(self.x + d, 4)

    def y_of(self, d):
        return wrap(self.y + d, 4)

    def z_of(self, d):
        z = wrap(self.z + d, 4)
        return z, lax.div(z, 2), lax.rem(z, 2)

    def quad(self, j):
        zh = 1 - self.zh if j & 2 else self.zh
        c = 1 - self.c if j & 1 else self.c
        return self.at(z=2 * zh + self.zl, c=c), 2 * zh + c

    def sibling(self):
        return self.at(c=1 - self.c)

    def cols(self, zh, width):
        return pl.ds(pl.multiple_of((2 * self.c + zh) * width, 128), width)

    def core_cols(self, c, width):
        return pl.ds(pl.multiple_of(2 * c * width, 128), 2 * width)


class Copies:
    def __init__(self, send, recv, here):
        self.send, self.recv, self.here = send, recv, here
        self.sent, self.kept = [], 0

    def push(self, src, dst, device):
        k = len(self.sent)
        copy = pltpu.make_async_remote_copy(
            src_ref=src,
            dst_ref=dst,
            send_sem=self.send.at[k],
            recv_sem=self.recv.at[k],
            device_id=device,
            device_id_type=MESH,
        )
        copy.start()
        self.sent.append(copy)
        return copy

    def local(self, src, dst):
        assert self.kept < LOCALS
        copy = pltpu.make_async_copy(src, dst, self.here.at[self.kept])
        copy.start()
        self.kept += 1
        return copy

    def drain(self, waited=()):
        for copy in self.sent:
            if not any(copy is other for other in waited):
                copy.wait_send()


def enter(place):
    barrier = pltpu.get_barrier_semaphore()
    others = [place.at(y=place.y_of(d)) for d in (1, 2, 3)]
    others += [place.at(x=place.x_of(d)) for d in (1, 2, 3)]
    others += [place.at(z=place.z_of(d)[0]) for d in (1, 2, 3)]
    others += [place.quad(1)[0], place.quad(3)[0]]
    for other in others:
        pl.semaphore_signal(barrier, inc=1, device_id=other, device_id_type=MESH)
    pl.semaphore_wait(barrier, len(others))


class Gather:
    def __init__(self, copies, place, block, whole, width):
        self.copies, self.place, self.whole, self.width = copies, place, whole, width
        own = place.cols(place.zh, width)
        self.own = copies.local(block, whole.at[place.x, place.zl, :, own])
        self.first = []
        for d in (1, 2, 3):
            self.first.append(
                copies.push(
                    block.at[pl.ds(0, 128)],
                    whole.at[place.x, place.zl, pl.ds(0, 128), own],
                    place.at(x=place.x_of(d)),
                )
            )
            self.first.append(
                copies.push(
                    block.at[pl.ds(128, 128)],
                    whole.at[place.x, place.zl, pl.ds(128, 128), own],
                    place.at(z=place.z_of(d)[0]),
                )
            )

    def spread(self):
        place, width = self.place, self.width
        self.own.wait()
        for copy in self.first:
            copy.wait_recv()
        upper = self.whole.at[:, place.zl, pl.ds(0, 128), place.cols(place.zh, width)]
        lower = self.whole.at[place.x, :, pl.ds(128, 128), place.core_cols(place.c, width)]
        self.upper, self.lower = [], []
        for d in (1, 2, 3):
            self.upper.append(self.copies.push(upper, upper, place.at(z=place.z_of(d)[0])))
            self.lower.append(self.copies.push(lower, lower, place.at(x=place.x_of(d))))

    def share(self):
        place, width = self.place, self.width
        self.shared = []
        for arrivals, start in ((self.upper, 0), (self.lower, 128)):
            for copy in arrivals:
                copy.wait_recv()
            part = self.whole.at[:, :, pl.ds(start, 128), place.core_cols(place.c, width)]
            self.shared.append(self.copies.push(part, part, place.sibling()))

    def finish(self):
        for copy in self.shared:
            copy.wait_recv()


class Reduce:
    def __init__(self, copies, place, out, width, mine, swap, load, theirs, landed, last):
        self.copies, self.place, self.out, self.width = copies, place, out, width
        self.mine, self.swap, self.load, self.theirs = mine, swap, load, theirs
        self.upper_in, self.lower_in = landed
        self.upper_last, self.lower_last = last
        self.swapped = []

    def half(self, zh):
        return pl.ds(pl.multiple_of(zh * self.width, 128), self.width)

    def fill(self, left, right):
        place, width = self.place, self.width
        own, other = place.core_cols(place.c, width), place.core_cols(1 - place.c, width)
        for part in range(2):

            def tile(i, carry):
                x, zl = lax.div(i, 2), lax.rem(i, 2)
                block = left(pl.ds(pl.multiple_of(256 * i, 256), 256)).T
                self.swap[x, zl] = dot(block, right[:, other], ((1,), (0,))).astype(BF16)
                self.mine[x, zl] = dot(block, right[:, own], ((1,), (0,))).astype(BF16)
                return carry

            lax.fori_loop(4 * part, 4 * part + 4, tile, 0)
            block = pl.ds(2 * part, 2)
            self.swapped.append(
                self.copies.push(self.swap.at[block], self.theirs.at[block], place.sibling())
            )

    def freed(self):
        for copy in self.swapped:
            copy.wait_send()

    def first(self):
        place, mine = self.place, self.mine
        loads = []
        for part, copy in enumerate(self.swapped):
            copy.wait_recv()
            block = pl.ds(2 * part, 2)
            loads.append(self.copies.local(self.theirs.at[block], self.load.at[block]))
        for part in range(2):
            loads[part].wait()

            def add(i, carry):
                x, zl, rows = lax.div(i, 8), lax.rem(lax.div(i, 4), 2), lax.rem(i, 4) * 64
                where = (x, zl, pl.ds(pl.multiple_of(rows, 64), 64), slice(None))
                mine[where] = (mine[where].astype(F32) + self.load[where].astype(F32)).astype(BF16)
                return carry

            lax.fori_loop(16 * part, 16 * part + 16, add, 0)
        self.upper_sent, self.lower_sent = [], []
        for d in (1, 2, 3):
            z, zh, zl = place.z_of(d)
            self.upper_sent.append(
                self.copies.push(
                    mine.at[:, zl, pl.ds(0, 128), self.half(zh)],
                    self.upper_in.at[d - 1],
                    place.at(z=z),
                )
            )
            x = place.x_of(d)
            self.lower_sent.append(
                self.copies.push(
                    mine.at[x, :, pl.ds(128, 128), :], self.lower_in.at[d - 1], place.at(x=x)
                )
            )

    def second(self, upper_load, lower_load):
        place, mine = self.place, self.mine
        for copy in self.upper_sent:
            copy.wait_recv()
        load_upper = self.copies.local(self.upper_in, upper_load)
        for copy in self.lower_sent:
            copy.wait_recv()
        load_lower = self.copies.local(self.lower_in, lower_load)
        load_upper.wait()

        def add_upper(x, carry):
            where = (x, place.zl, pl.ds(0, 128), self.half(place.zh))
            total = mine[where].astype(F32)
            for d in range(3):
                total += upper_load[d, x].astype(F32)
            mine[where] = total.astype(BF16)
            return carry

        lax.fori_loop(0, 4, add_upper, 0)
        self.upper_done, self.lower_done = [], []
        for d in (1, 2, 3):
            x = place.x_of(d)
            self.upper_done.append(
                self.copies.push(
                    mine.at[x, place.zl, pl.ds(0, 128), self.half(place.zh)],
                    self.upper_last.at[d - 1],
                    place.at(x=x),
                )
            )
        load_lower.wait()

        def add_lower(zl, carry):
            where = (place.x, zl, pl.ds(128, 128), slice(None))
            total = mine[where].astype(F32)
            for d in range(3):
                total += lower_load[d, zl].astype(F32)
            mine[where] = total.astype(BF16)
            return carry

        lax.fori_loop(0, 2, add_lower, 0)
        for d in (1, 2, 3):
            z, zh, zl = place.z_of(d)
            self.lower_done.append(
                self.copies.push(
                    mine.at[place.x, zl, pl.ds(128, 128), self.half(zh)],
                    self.lower_last.at[d - 1],
                    place.at(z=z),
                )
            )

    def parted(self):
        return self.upper_sent + self.lower_sent + self.upper_done + self.lower_done

    def done(self):
        for copy in self.parted():
            copy.wait_send()

    def finish(self):
        place = self.place
        half = self.half(place.zh)
        for copies, start, last in (
            (self.upper_done, 0, self.upper_last),
            (self.lower_done, 128, self.lower_last),
        ):
            for copy in copies:
                copy.wait_recv()
            total = self.mine[place.x, place.zl, pl.ds(start, 128), half].astype(F32)
            for d in range(3):
                total += last[d].astype(F32)
            self.out[pl.ds(start, 128), :] = total


class Spread:
    def __init__(self, copies, place, held, rows):
        self.copies, self.place, self.rows = copies, place, rows
        mine = rows.at[place.y, place.m]
        self.own = copies.local(held.at[place.m], mine)
        self.quad = []
        for j in (1, 2, 3):
            device, m = place.quad(j)
            self.quad.append((copies.push(held.at[m], mine, device), m))

    def along(self):
        place = self.place
        self.arrivals = []
        self.own.wait()
        for part in [(None, place.m)] + self.quad:
            if part[0] is not None:
                part[0].wait_recv()
            block = self.rows.at[place.y, part[1]]
            for d in (1, 2, 3):
                self.arrivals.append(
                    self.copies.push(block, block, place.at(y=place.y_of(d)))
                )

    def finish(self):
        for copy in self.arrivals:
            copy.wait_recv()


class RowSum:
    def __init__(self, copies, place, part, arrived, own):
        self.arrived, self.own = arrived, own
        self.sent = []
        for k in range(4):
            rows = pl.ds(32 * k, 32)
            block = k if len(part.shape) == 4 else rows
            self.sent.append(
                [
                    copies.push(
                        part.at[place.y_of(d), block],
                        arrived.at[d - 1, rows],
                        place.at(y=place.y_of(d)),
                    )
                    for d in (1, 2, 3)
                ]
            )

    def total(self, k):
        rows = pl.ds(32 * k, 32)
        own = self.own[k] if len(self.own.shape) == 3 else self.own[rows, :]
        total = own.astype(F32)
        for d, copy in enumerate(self.sent[k]):
            copy.wait_recv()
            total += self.arrived[d, rows, :].astype(F32)
        return total


class RowSend:
    def __init__(self, copies, place, stage, whole):
        self.copies, self.place, self.stage, self.whole = copies, place, stage, whole
        self.arrivals, self.own = [], []

    def send(self, k):
        rows = pl.ds(32 * k, 32)
        mine = self.whole.at[self.place.y, rows]
        for d in (1, 2, 3):
            self.arrivals.append(
                self.copies.push(
                    self.stage.at[rows], mine, self.place.at(y=self.place.y_of(d))
                )
            )
        self.own.append(self.copies.local(self.stage.at[rows], mine))

    def finish(self):
        for copy in self.arrivals:
            copy.wait_recv()
        for copy in self.own:
            copy.wait()


def factor_of(rows):
    return lax.rsqrt(jnp.mean(rows * rows, axis=-1, keepdims=True) + EPSILON)


def norm_back(grad, rows, gain):
    factor = factor_of(rows)
    scaled = grad * gain
    back = factor * scaled - rows * factor**3 * jnp.mean(scaled * rows, axis=-1, keepdims=True)
    return back, jnp.sum(grad * rows * factor, axis=0, keepdims=True)


def dot(left, right, dims):
    return lax.dot_general(left, right, (dims, ((), ())), preferred_element_type=F32)


def turn(rows, cos_t, sin_t):
    return rows * cos_t + pltpu.roll(rows, HD // 2, 1) * sin_t


def turn_back(rows, cos_t, sin_t):
    return rows * cos_t - pltpu.roll(rows, HD // 2, 1) * sin_t


def head_cols(h, part):
    return pl.ds(pl.multiple_of(h * 3 * HD + part * HD, HD), HD)


def tile_cols(i, size):
    return pl.ds(pl.multiple_of(i * size, size), size)


def columns(rows, cols, size):
    return rows[(slice(None),) * (len(rows.shape) - 1) + (cols,)].reshape(512, size)


def back_product(target, pairs):
    def tile(i, carry):
        x, zl = lax.div(i, 2), lax.rem(i, 2)
        total = None
        for left, right in pairs:
            part = dot(left[...], right[x, zl], ((1,), (1,)))
            total = part if total is None else total + part
        target[:, :, tile_cols(i, 256)] = total.astype(BF16).reshape(4, 128, 256)
        return carry

    lax.fori_loop(0, TILES, tile, 0)


def fore_kernel(
    held, grad_held, qkv_block, out_block, gain_block, gate_block, up_block, down_block,
    cos_in, sin_in,
    x_out, first_out, qkv_out, probs_out, mixed_out, second_out, grads_out, hidden_out,
    gate_out, up_out, middle_out, part_out, down_part_out, qkv_w_out, out_w_out, gain_out,
    rows, first, second, grads, qkv, probs, mixed, gate, up, hidden, part, down_part,
    arrived, middle, stage, qkv_w, out_w, gate_w, up_w, down_w, gains, gain_row,
    send, recv, here,
):
    place = Place()
    enter(place)
    copies = Copies(send, recv, here)
    width = rows.shape[-1]
    spread = Spread(copies, place, held, rows)
    own_gain = copies.local(gain_block, gains.at[place.x, place.zl])
    gain_first = [
        copies.push(gain_block, gains.at[place.x, place.zl], place.at(x=place.x_of(d)))
        for d in (1, 2, 3)
    ]
    qkv_gather = Gather(copies, place, qkv_block, qkv_w, 3 * HD)
    out_gather = Gather(copies, place, out_block, out_w, HD)
    spread.along()
    own_gain.wait()
    for copy in gain_first:
        copy.wait_recv()
    column = gains.at[:, place.zl]
    gain_last = copies.push(column, column, place.at(z=2 * place.zh + 1 - place.zl))
    qkv_gather.spread()
    out_gather.spread()
    grad_spread = Spread(copies, place, grad_held, grads)
    gate_gather = Gather(copies, place, gate_block, gate_w, UNITS)
    up_gather = Gather(copies, place, up_block, up_w, UNITS)
    down_gather = Gather(copies, place, down_block, down_w, UNITS)
    gain_last.wait_recv()
    for i in range(TILES):
        gain_row[:, 256 * i : 256 * i + 256] = gains[i // 2, i % 2]
    spread.finish()
    grad_spread.along()
    gain = gain_row[0:1, :]

    def norm(i, carry):
        y, j = lax.div(i, 4), lax.rem(i, 4)
        x = rows[y, j].astype(F32)
        first[y, pl.ds(pl.multiple_of(32 * j, 32), 32), :] = (x * factor_of(x) * gain).astype(BF16)
        return carry

    lax.fori_loop(0, 16, norm, 0)
    kept = [copies.local(first, first_out), copies.local(rows.at[place.y], x_out)]
    qkv_gather.share()
    out_gather.share()
    gate_gather.spread()
    qkv_gather.finish()
    kept.append(copies.local(qkv_w, qkv_w_out))

    def project(i, carry):
        both = dot(
            first[...].reshape(512, width),
            qkv_w[:, :, :, tile_cols(i, 768)].reshape(width, 768),
            ((1,), (0,)),
        )
        for k in range(2):
            head = 2 * i + k
            for p in range(3):
                one = both[:, (3 * k + p) * HD : (3 * k + p + 1) * HD]
                if p < 2:
                    one = turn(one, cos_in[...], sin_in[...])
                qkv[:, head_cols(head, p)] = one.astype(BF16)
        return carry

    lax.fori_loop(0, 2, project, 0)
    kept.append(copies.local(qkv, qkv_out))
    up_gather.spread()

    def attend(h, carry):
        for b in range(4):
            size = 128 * (b + 1)
            now = slice(128 * b, size)
            scores = dot(qkv[now, head_cols(h, 0)], qkv[0:size, head_cols(h, 1)], ((1,), (1,)))
            allowed = lax.broadcasted_iota(jnp.int32, (128, size), 0) + 128 * b
            allowed = allowed >= lax.broadcasted_iota(jnp.int32, (128, size), 1)
            scores = jnp.where(allowed, scores * HD**-0.5, -jnp.inf)
            weight = jnp.exp(scores - jnp.max(scores, axis=-1, keepdims=True))
            weight = weight * (1.0 / jnp.sum(weight, axis=-1, keepdims=True))
            weight = weight.astype(BF16)
            probs[h, now, 0:size] = weight
            if b < 3:
                probs[h, now, size:] = jnp.zeros((128, 512 - size), BF16)
            blend = dot(weight, qkv[0:size, head_cols(h, 2)], ((1,), (0,)))
            mixed[now, tile_cols(h, HD)] = blend.astype(BF16)
        return carry

    lax.fori_loop(0, 4, attend, 0)
    kept += [copies.local(probs, probs_out), copies.local(mixed, mixed_out)]
    out_gather.finish()
    kept.append(copies.local(out_w, out_w_out))
    back_product(part, [(mixed, out_w)])
    total = RowSum(copies, place, part, arrived, part.at[place.y])
    down_gather.spread()
    gate_gather.share()
    sender = RowSend(copies, place, stage, second)
    gain = gain_row[1:2, :]
    for k in range(4):
        now = pl.ds(32 * k, 32)
        mid = rows[place.y, k].astype(F32) + total.total(k)
        middle[now, :] = mid
        stage[now, :] = (mid * factor_of(mid) * gain).astype(BF16)
        sender.send(k)
    kept += [copies.local(middle, middle_out), copies.local(gain_row, gain_out)]
    up_gather.share()
    sender.finish()
    kept.append(copies.local(second, second_out))

    def fill(target, weight):
        def tile(i, carry):
            target[:, tile_cols(i, 768)] = dot(
                second[...].reshape(512, width),
                weight[:, :, :, tile_cols(i, 768)].reshape(width, 768),
                ((1,), (0,)),
            ).astype(BF16)
            return carry

        lax.fori_loop(0, 2, tile, 0)

    gate_gather.finish()
    fill(gate, gate_w)
    up_gather.finish()
    fill(up, up_w)
    grad_spread.finish()
    kept.append(copies.local(grads, grads_out))
    down_gather.share()
    down_gather.finish()

    def units(i, carry):
        cols = tile_cols(i, 256)
        back = dot(
            grads[...].reshape(512, width), down_w[:, :, :, cols].reshape(width, 256), ((1,), (0,))
        )
        opened, lifted = gate[:, cols].astype(F32), up[:, cols].astype(F32)
        sig = 1.0 / (1.0 + jnp.exp(-opened))
        silu = opened * sig
        hidden[:, cols] = (silu * lifted).astype(BF16)
        gate[:, cols] = (back * lifted * sig * (1.0 + opened * (1.0 - sig))).astype(BF16)
        up[:, cols] = (back * silu).astype(BF16)
        return carry

    lax.fori_loop(0, 6, units, 0)
    kept += [
        copies.local(hidden, hidden_out),
        copies.local(gate, gate_out),
        copies.local(up, up_out),
    ]
    waited = [copy for group in total.sent for copy in group]
    for copy in waited:
        copy.wait_send()
    back_product(part, [(gate, gate_w), (up, up_w)])
    kept.append(copies.local(part, part_out))
    back_product(down_part, [(hidden, down_w)])
    kept.append(copies.local(down_part, down_part_out))
    for copy in kept:
        copy.wait()
    copies.drain(waited)


def back_kernel(
    part_in, down_part_in, middle_in, grads_in, second_in, gate_in, up_in, hidden_in,
    qkv_w_in, out_w_in, first_in, qkv_in, probs_in, mixed_in, x_in, gains, cos_in, sin_in,
    block_out, grad_out, gains_out, qkv_out, out_out, gate_out, up_out, down_out,
    their_qkv, their_out, their_gate, their_up, their_down,
    up_qkv, up_outw, up_gate, up_up, up_down, low_qkv, low_outw, low_gate, low_up, low_down,
    grads, second, hidden, gate, up, mid_all, qkv_tile, out_w, probs, mixed, mixed_grad,
    arrived, down_arrived, own, down_own, middle, mid_grad, x_own, stage, out_stage, in_stage,
    key_grad, value_grad,
    mine_a, mine_b, mine_c, mine_o, swap_a, swap_b, load, upper_load, lower_load,
    last_a, last_b, last_c, last_d, last_o, low_a, low_b, low_c, low_d, low_o,
    vec, vec_y, vec_x, vec_z, vec_c, half_x, half_z, half_c,
    send, recv, here,
):
    place = Place()
    enter(place)
    copies = Copies(send, recv, here)
    width = mid_all.shape[-1]
    waited = []
    load_hidden = copies.local(hidden_in, hidden)
    load_grads = copies.local(grads_in, grads)
    total = RowSum(copies, place, part_in, arrived, own)
    load_own = copies.local(part_in.at[place.y], own)
    load_second = copies.local(second_in, second)
    load_gate = copies.local(gate_in, gate)
    load_up = copies.local(up_in, up)
    load_middle = copies.local(middle_in, middle)
    load_x = copies.local(x_in, x_own)
    load_mixed = copies.local(mixed_in, mixed)
    load_out_w = copies.local(out_w_in, out_w)
    load_probs = copies.local(probs_in, probs)
    load_down = copies.local(down_part_in.at[place.y], down_own)

    def whole(ref):
        return lambda cols: columns(ref, cols, 256)

    down = Reduce(copies, place, down_out, UNITS, mine_a, swap_a, load,
                  their_down, (up_down, low_down), (last_a, low_a))
    opened = Reduce(copies, place, gate_out, UNITS, mine_b, swap_b, load,
                    their_gate, (up_gate, low_gate), (last_b, low_b))
    lifted = Reduce(copies, place, up_out, UNITS, mine_c, swap_a, load,
                    their_up, (up_up, low_up), (last_c, low_c))
    attn = Reduce(copies, place, qkv_out, 3 * HD, mine_a, swap_b, load,
                  their_qkv, (up_qkv, low_qkv), (last_d, low_d))
    small = pl.ds(0, 2 * HD)
    outw = Reduce(copies, place, out_out, HD, mine_o, swap_a.at[:, :, :, small],
                  load.at[:, :, :, small], their_out, (up_outw, low_outw),
                  (last_o, low_o))
    load_hidden.wait()
    load_grads.wait()
    down.fill(whole(grads), hidden)
    load_second.wait()
    load_gate.wait()
    opened.fill(whole(second), gate)
    down.first()
    load_up.wait()
    down.freed()
    waited += down.swapped
    lifted.fill(whole(second), up)
    for copy in (load_own, load_middle, load_x, load_down):
        copy.wait()
    sender = RowSend(copies, place, stage, mid_all)
    gain = gains[1:2, :]
    gain_total = jnp.zeros((1, width), F32)
    for k in range(4):
        now = pl.ds(32 * k, 32)
        back, gain_part = norm_back(total.total(k), middle[now, :], gain)
        gain_total += gain_part
        back += grads[place.y, k].astype(F32)
        mid_grad[now, :] = back
        stage[now, :] = back.astype(BF16)
        sender.send(k)
    vec[1:2, :] = gain_total
    down_total = RowSum(copies, place, down_part_in, down_arrived, down_own)
    opened.first()
    lifted.first()
    down.second(upper_load, lower_load)
    for copy in (load_mixed, load_out_w, load_probs):
        copy.wait()
    load_qkv = copies.local(qkv_in, hidden)
    sender.finish()
    load_first = copies.local(first_in, second)

    def unmix(i, carry):
        mixed_grad[:, tile_cols(i, 256)] = dot(
            mid_all[...].reshape(512, width),
            out_w[:, :, :, tile_cols(i, 256)].reshape(width, 256),
            ((1,), (0,)),
        ).astype(BF16)
        return carry

    lax.fori_loop(0, 2, unmix, 0)
    opened.second(upper_load, lower_load)
    load_qkv.wait()
    heads, heads_grad = hidden, gate

    def attend(h, carry):
        key_grad[...] = jnp.zeros(key_grad.shape, F32)
        value_grad[...] = jnp.zeros(value_grad.shape, F32)
        for b in range(4):
            size = 128 * (b + 1)
            now, so_far = slice(128 * b, size), slice(0, size)
            weight = probs[h, now, so_far]
            mix = mixed_grad[now, tile_cols(h, HD)]
            value_grad[so_far, :] += dot(weight, mix, ((0,), (0,)))
            change = dot(mix, heads[so_far, head_cols(h, 2)], ((1,), (1,)))
            weight = weight.astype(F32)
            change = weight * (change - jnp.sum(weight * change, axis=-1, keepdims=True))
            change = change.astype(BF16)
            query = dot(change, heads[so_far, head_cols(h, 1)], ((1,), (0,))) * HD**-0.5
            query = turn_back(query, cos_in[now, :], sin_in[now, :])
            heads_grad[now, head_cols(h, 0)] = query.astype(BF16)
            key_grad[so_far, :] += dot(change, heads[now, head_cols(h, 0)], ((0,), (0,)))
        key = turn_back(key_grad[...] * HD**-0.5, cos_in[...], sin_in[...])
        heads_grad[:, head_cols(h, 1)] = key.astype(BF16)
        heads_grad[:, head_cols(h, 2)] = value_grad[...].astype(BF16)
        return carry

    lax.fori_loop(0, 4, attend, 0)
    part = grads

    def fetch(i, slot):
        return pltpu.make_async_copy(
            qkv_w_in.at[i // 2, i % 2], qkv_tile.at[slot], here.at[LOCALS + slot]
        )

    fetch(0, 0).start()
    for i in range(TILES):
        if i + 1 < TILES:
            fetch(i + 1, (i + 1) % 2).start()
        fetch(i, i % 2).wait()
        part[:, :, :, 256 * i : 256 * i + 256] = (
            dot(heads_grad[...], qkv_tile[i % 2], ((1,), (1,))).astype(BF16).reshape(4, 4, 32, 256)
        )
    first_total = RowSum(copies, place, part, arrived, part.at[place.y])
    down.finish()
    down.done()
    waited += down.parted()
    opened.freed()
    waited += opened.swapped
    load_first.wait()
    attn.fill(whole(second), heads_grad)
    lifted.freed()
    waited += lifted.swapped
    outw.fill(whole(mid_all), mixed)
    attn.first()
    lifted.second(upper_load, lower_load)
    outw.first()
    for k in range(4):
        now = pl.ds(32 * k, 32)
        out_stage[k] = (middle[now, :] + down_total.total(k)).astype(BF16)
    kept = [copies.local(out_stage.at[place.m], block_out.at[place.m])]
    arrivals = []
    for j in (1, 2, 3):
        device, m = place.quad(j)
        arrivals.append(copies.push(out_stage.at[m], block_out.at[place.m], device))
    gain = gains[0:1, :]
    gain_total = jnp.zeros((1, width), F32)
    for k in range(4):
        now = pl.ds(32 * k, 32)
        back, gain_part = norm_back(first_total.total(k), x_own[k].astype(F32), gain)
        gain_total += gain_part
        in_stage[k] = (mid_grad[now, :] + back).astype(BF16)
    vec[0:1, :] = gain_total
    vec[2:8, :] = jnp.zeros((6, width), F32)
    kept.append(copies.local(in_stage.at[place.m], grad_out.at[place.m]))
    for j in (1, 2, 3):
        device, m = place.quad(j)
        arrivals.append(copies.push(in_stage.at[m], grad_out.at[place.m], device))
    gain_y = [copies.push(vec, vec_y.at[d - 1], place.at(y=place.y_of(d))) for d in (1, 2, 3)]
    attn.second(upper_load, lower_load)
    for copy in gain_y:
        copy.wait_recv()
    half_x[...] = vec[...] + vec_y[0] + vec_y[1] + vec_y[2]

    def of_x(x):
        return pl.ds(pl.multiple_of(x * 512, 128), 512)

    def of_z(zl):
        return pl.ds(pl.multiple_of(zl * 256, 128), 256)

    gain_x = [
        copies.push(
            half_x.at[:, of_x(place.x_of(d))], vec_x.at[d - 1], place.at(x=place.x_of(d))
        )
        for d in (1, 2, 3)
    ]
    outw.second(upper_load.at[:, :, :, pl.ds(0, HD)], lower_load.at[:, :, :, small])
    for copy in gain_x:
        copy.wait_recv()
    half_z[...] = half_x[:, of_x(place.x)] + vec_x[0] + vec_x[1] + vec_x[2]
    gain_z = []
    for d in (1, 2, 3):
        z, zh, zl = place.z_of(d)
        gain_z.append(copies.push(half_z.at[:, of_z(zl)], vec_z.at[d - 1], place.at(z=z)))
    opened.finish()
    lifted.finish()
    for copy in gain_z:
        copy.wait_recv()
    half_c[...] = half_z[:, of_z(place.zl)] + vec_z[0] + vec_z[1] + vec_z[2]
    gain_c = copies.push(half_c, vec_c, place.sibling())
    attn.finish()
    outw.finish()
    gain_c.wait_recv()
    gains_out[...] = half_c[...] + vec_c[...]
    for copy in kept:
        copy.wait()
    for copy in arrivals:
        copy.wait_recv()
    copies.drain(waited)


def call(kernel, number, args, in_specs, outs, out_specs, scratch):
    return pl.pallas_call(
        kernel,
        out_shape=[jax.ShapeDtypeStruct(shape, dtype) for shape, dtype in outs],
        in_specs=in_specs,
        out_specs=out_specs,
        scratch_shapes=[
            *[pltpu.VMEM(shape, dtype) for shape, dtype in scratch],
            pltpu.SemaphoreType.DMA((COPIES,)),
            pltpu.SemaphoreType.DMA((COPIES,)),
            pltpu.SemaphoreType.DMA((LOCALS + 2,)),
        ],
        compiler_params=pltpu.CompilerParams(
            collective_id=number, has_side_effects=True, vmem_limit_bytes=58 * 2**20
        ),
    )(*args)


def tables(length):
    half_size = HD // 2
    inverse_freq = THETA ** (-(jnp.arange(half_size, dtype=F32) * 2.0) / HD)
    angles = jnp.arange(length, dtype=F32)[:, None] * inverse_freq[None, :]
    cos_t, sin_t = jnp.cos(angles), jnp.sin(angles)
    return jnp.concatenate([cos_t, cos_t], axis=1), jnp.concatenate([-sin_t, sin_t], axis=1)


def local(
    hidden_in,
    cotangent,
    gain_attn,
    w_query,
    w_key,
    w_value,
    w_output,
    gain_mlp,
    w_gate,
    w_up,
    w_down,
):
    held, grad_held = hidden_in[:, 0], cotangent[:, 0]
    width = held.shape[2]
    length = 512
    units = w_gate.shape[1]

    def wide(weight):
        return jnp.pad(weight, ((0, 0), (0, UNITS - units)))

    qkv = jnp.concatenate([w_query, w_key, w_value], axis=1)
    gains = jnp.pad(jnp.stack([gain_attn, gain_mlp]).astype(F32), ((0, 6), (0, 0)))
    cos_t, sin_t = tables(length)
    blocks = ((4, 4, 32, width), BF16)
    rows = ((4, 128, width), BF16)
    hidden = ((length, 4 * UNITS), BF16)
    probs = ((4, length, length), BF16)
    mixed = ((length, 4 * HD), BF16)
    own, own_f32 = ((128, width), BF16), ((128, width), F32)
    parts = ((4, 32, width), BF16)

    def plane(size):
        return ((4, 2, 256, 4 * size), BF16)

    gain_row = ((8, width), F32)
    arrived = ((3, 128, width), BF16)
    fore = call(
        fore_kernel,
        0,
        (held, grad_held, qkv, w_output.T, gains, wide(w_gate), wide(w_up), wide(w_down.T),
         cos_t, sin_t),
        [ANY] * 8 + [VMEM] * 2,
        [parts, rows, hidden, probs, mixed, rows, blocks, hidden, hidden, hidden,
         own_f32, rows, rows, plane(3 * HD), plane(HD), gain_row],
        [ANY] * 16,
        [blocks, rows, rows, blocks, hidden, probs, mixed, hidden, hidden, hidden, rows, rows,
         arrived, own_f32, own, plane(3 * HD), plane(HD), plane(UNITS), plane(UNITS),
         plane(UNITS), ((4, 2, 8, 256), F32), gain_row],
    )
    (x_own, first, heads, weights, blend, second, grads, units_mid, gate, up, middle, part,
     down_part, qkv_w, out_w, gain_rows) = fore

    sizes = (3 * HD, HD, UNITS, UNITS, UNITS)

    def mine(size):
        return ((4, 2, 256, 2 * size), BF16)

    def upper(size):
        return ((3, 4, 128, size), BF16)

    def lower(size):
        return ((3, 2, 128, 2 * size), BF16)

    def last(size):
        return ((3, 128, size), BF16)

    ends = [last(size) for size in (UNITS, UNITS, UNITS, 3 * HD, HD)]
    back = call(
        back_kernel,
        1,
        (part, down_part, middle, grads, second, gate, up, units_mid, qkv_w, out_w, first,
         heads, weights, blend, x_own, gain_rows, cos_t, sin_t),
        [ANY] * 15 + [VMEM] * 3,
        [parts, parts, ((8, 256), F32)]
        + [((256, size), F32) for size in sizes]
        + [mine(size) for size in sizes]
        + [upper(size) for size in sizes]
        + [lower(size) for size in sizes],
        [ANY, ANY] + [VMEM] * 6 + [ANY] * 15,
        [blocks, rows, hidden, hidden, hidden, rows, ((2, 256, 12 * HD), BF16), plane(HD), probs,
         mixed, mixed, arrived, arrived, own, own, own_f32, own_f32, parts, own, parts, parts,
         ((length, HD), F32), ((length, HD), F32),
         mine(UNITS), mine(UNITS), mine(UNITS), mine(HD), mine(UNITS), mine(UNITS), mine(UNITS),
         upper(UNITS), lower(UNITS)]
        + ends + ends
        + [gain_row, ((3, 8, width), F32), ((3, 8, 512), F32), ((3, 8, 256), F32),
           ((8, 256), F32), gain_row, ((8, 512), F32), ((8, 256), F32)],
    )
    block_out, grad_in, gains_out, qkv_g, out_g, gate_g, up_g, down_g = back[:8]
    return (
        block_out[:, None],
        grad_in[:, None],
        gains_out[0],
        qkv_g[:, :HD],
        qkv_g[:, HD : 2 * HD],
        qkv_g[:, 2 * HD :],
        out_g.T,
        gains_out[1],
        gate_g[:, :units],
        up_g[:, :units],
        down_g[:, :units].T,
    )


def solution(mesh):
    rows = P(None, "fsdp", "tensor", None)
    into, out_of = P("fsdp", "tensor"), P("tensor", "fsdp")
    return jax.shard_map(
        local,
        mesh=mesh,
        in_specs=(
            rows, rows, P("fsdp"), into, into, into, out_of, P("fsdp"), into, into, out_of,
        ),
        out_specs=(
            rows, rows, P("fsdp"), into, into, into, out_of, P("fsdp"), into, into, out_of,
        ),
        check_vma=False,
    )
```

```python
import jax
import jax.numpy as jnp
import numpy as np
from jax import lax
from jax.experimental import pallas as pl
from jax.experimental.pallas import tpu as pltpu
from jax.sharding import PartitionSpec as P


HD = 128
UNITS = 352
ROWS = (128, 128, 96)
FIRST = (64, 64, 48, 64, 64)
EPSILON = 1e-05
THETA = 10000.0
MESH = pl.DeviceIdType.MESH
F32 = jnp.float32
BF16 = jnp.bfloat16
COPIES = 344
LOCALS = 120
TILES = 8
ALL = slice(None)
RECV, SENT, HERE = range(3)
ANY = pl.BlockSpec(memory_space=pl.ANY)
VMEM = pl.BlockSpec(memory_space=pltpu.VMEM)
VMEM_LIMIT = 62 * 2**20

ORDER = (
    0, 38, 39, 40, 7, 44, 35, 43, 1, 36, 8, 42, 41, 46, 2, 3, 48, 4, 37, 45, 49, 21, 50, 10, 5, 9,
    47, 11, 58, 53, 14, 51, 54, 6, 60, 52, 61, 59, 55, 62, 22, 12, 56, 63, 13, 64, 65, 15, 23, 68,
    69, 28, 66, 24, 57, 25, 67, 70, 16, 17, 72, 73, 18, 71, 26, 29, 77, 74, 19, 76, 75, 27, 108,
    20, 79, 31, 30, 32, 78, 80, 81, 82, 83, 33, 84, 85, 110, 109, 111, 34, 112, 113, 137, 86, 139,
    138, 140, 141, 166, 87, 89, 114, 88, 91, 90, 93, 92, 94, 95, 169, 115, 167, 142, 116, 118, 170,
    143, 98, 96, 119, 97, 168, 99, 144, 117, 120, 122, 121, 123, 171, 124, 145, 147, 172, 146, 104,
    100, 174, 149, 175, 173, 101, 150, 105, 223, 148, 127, 125, 126, 128, 178, 151, 177, 176, 102,
    103, 180, 106, 152, 153, 107, 179, 191, 133, 192, 129, 215, 193, 130, 156, 181, 194, 196, 134,
    157, 183, 154, 197, 184, 216, 155, 182, 195, 198, 200, 224, 199, 201, 202, 185, 187, 217, 186,
    188, 189, 218, 162, 205, 203, 225, 131, 204, 226, 206, 132, 135, 136, 163, 228, 221, 158, 159,
    229, 247, 211, 222, 248, 227, 230, 212, 232, 231, 219, 233, 234, 160, 220, 190, 161, 164, 165,
    207, 208, 249, 237, 251, 235, 238, 236, 250, 252, 255, 209, 253, 210, 213, 256, 214, 239, 240,
    243, 257, 244, 241, 242, 258, 245, 254, 259, 246,
)


class Place:
    def __init__(self):
        f = lax.axis_index("fsdp")
        t = lax.axis_index("tensor")
        self.x, self.zl = lax.div(f, 2), lax.rem(f, 2)
        self.y, self.m = lax.div(t, 4), lax.rem(t, 4)
        self.zh, self.c = lax.div(self.m, 2), lax.rem(self.m, 2)
        self.z = 2 * self.zh + self.zl

    def at(self, x=None, z=None, y=None, c=None):
        x = self.x if x is None else x
        z = self.z if z is None else z
        y = self.y if y is None else y
        c = self.c if c is None else c
        return (2 * x + lax.rem(z, 2), 4 * y + 2 * lax.div(z, 2) + c)

    def x_of(self, d):
        return lax.rem(self.x + d, 4)

    def y_of(self, d):
        return lax.rem(self.y + d, 4)

    def z_of(self, d):
        z = lax.rem(self.z + d, 4)
        return z, lax.div(z, 2), lax.rem(z, 2)

    def quad(self, j):
        zh = 1 - self.zh if j & 2 else self.zh
        c = 1 - self.c if j & 1 else self.c
        return self.at(z=2 * zh + self.zl, c=c), 2 * zh + c

    def sibling(self):
        return self.at(c=1 - self.c)


class Copies:
    def __init__(self, send, recv, here):
        self.send, self.recv, self.here = send, recv, here
        self.sent, self.waited, self.kept = [], [], 0

    def push(self, src, dst, device):
        k = len(self.sent)
        assert k < COPIES
        copy = pltpu.make_async_remote_copy(
            src_ref=src,
            dst_ref=dst,
            send_sem=self.send.at[k],
            recv_sem=self.recv.at[k],
            device_id=device,
            device_id_type=MESH,
        )
        copy.start()
        self.sent.append(copy)
        return copy

    def local(self, src, dst):
        assert self.kept < LOCALS
        copy = pltpu.make_async_copy(src, dst, self.here.at[self.kept])
        copy.start()
        self.kept += 1
        return copy

    def wait(self, copy, kind):
        if kind == RECV:
            copy.wait_recv()
        elif kind == HERE:
            copy.wait()
        elif not any(copy is other for other in self.waited):
            copy.wait_send()
            self.waited.append(copy)

    def drain(self):
        for copy in self.sent:
            self.wait(copy, SENT)


def recv(copies):
    return [(copy, RECV) for copy in copies]


def sent(copies):
    return [(copy, SENT) for copy in copies]


def here(copies):
    return [(copy, HERE) for copy in copies]


def nothing():
    return ()


class Tasks:
    def __init__(self, copies):
        self.copies, self.all = copies, []

    def add(self, after, run=nothing, needs=nothing):
        self.all.append((list(after), needs, run))
        return len(self.all) - 1


def drive(tasks, order):
    done = set()
    for number in order:
        after, needs, run = tasks.all[number]
        assert done.issuperset(after), number
        for copy, kind in needs():
            tasks.copies.wait(copy, kind)
        run()
        done.add(number)
    assert len(done) == len(tasks.all)


def enter(place):
    barrier = pltpu.get_barrier_semaphore()
    others = [place.at(y=place.y_of(d)) for d in (1, 2, 3)]
    others += [place.at(x=place.x_of(d)) for d in (1, 2, 3)]
    others += [place.at(z=place.z_of(d)[0]) for d in (1, 2, 3)]
    others += [place.quad(1)[0], place.quad(3)[0]]
    for other in others:
        pl.semaphore_signal(barrier, inc=1, device_id=other, device_id_type=MESH)
    pl.semaphore_wait(barrier, len(others))


def dot(left, right, dims):
    return lax.dot_general(left, right, (dims, ((), ())), preferred_element_type=F32)


def turn(rows, cos_t, sin_t):
    return rows * cos_t + pltpu.roll(rows, HD // 2, 1) * sin_t


def turn_back(rows, cos_t, sin_t):
    return rows * cos_t - pltpu.roll(rows, HD // 2, 1) * sin_t


def head_cols(h, part):
    return pl.ds(pl.multiple_of(h * 3 * HD + part * HD, HD), HD)


def tile_cols(i, size):
    return pl.ds(pl.multiple_of(i * size, size), size)


def columns(rows, cols, size):
    return rows[:, :, :, cols].reshape(512, size)


def factor_of(rows):
    return lax.rsqrt(jnp.mean(rows * rows, axis=-1, keepdims=True) + EPSILON)


def norm_back(grad, rows, gain):
    factor = factor_of(rows)
    scaled = grad * gain
    back = factor * scaled - rows * factor**3 * jnp.mean(scaled * rows, axis=-1, keepdims=True)
    return back, jnp.sum(grad * rows * factor, axis=0, keepdims=True)


def fit(ref, shape):
    index = tuple(
        ALL if have == want else pl.ds(0, want) for have, want in zip(ref.shape, shape, strict=True)
    )
    return ref.at[index]


class Form:
    def __init__(self, place, rows, first):
        self.place = place
        self.up, self.low = pl.ds(0, first), pl.ds(first, rows - first)

    def upper(self, ref, x, zl, zh):
        return ref.at[x, zl, 2 * self.place.c + zh, :, self.up]

    def lower(self, ref, x, zl, zh=None):
        block = pl.ds(2 * self.place.c, 2) if zh is None else 2 * self.place.c + zh
        return ref.at[x, zl, block, :, self.low]

    def core(self, ref, x, c):
        return ref.at[x, :, pl.ds(2 * c, 2)]


class Gather:
    def __init__(self, copies, place, form, whole, block, placed=False):
        self.copies, self.place, self.whole, self.block = copies, place, whole, block
        self.form, self.placed = form, placed

    def plan(self, tasks):
        self.passed, self.shared = [], []
        begin = tasks.add((), self.begin)
        spread = tasks.add([begin], self.spread, lambda: here(self.local) + recv(self.first))
        ahead = tasks.add([spread], lambda: self.relay(0), lambda: recv(self.ahead))
        behind = tasks.add([spread], lambda: self.relay(1), lambda: recv(self.behind))
        near = tasks.add([ahead, behind], self.near)
        far = tasks.add([near], self.far, lambda: recv(self.passed))
        self.have = tasks.add([far], needs=lambda: recv(self.shared))

    def busy(self):
        return sent(self.ahead + self.behind + self.passed + self.shared)

    def begin(self):
        place, block, form = self.place, self.block, self.form
        self.local = []
        if not self.placed:
            target = self.whole.at[place.x, place.zl, 2 * place.c + place.zh]
            self.local.append(self.copies.local(block, target))
        upper, lower = block.at[:, form.up], block.at[:, form.low]
        to_upper = form.upper(self.whole, place.x, place.zl, place.zh)
        to_lower = form.lower(self.whole, place.x, place.zl, place.zh)
        self.first = []
        for d in (1, 3, 2):
            self.first.append(self.copies.push(upper, to_upper, place.at(x=place.x_of(d))))
            self.first.append(self.copies.push(lower, to_lower, place.at(z=place.z_of(d)[0])))

    def both(self, upper, lower, to):
        place = self.place
        return [
            self.copies.push(upper, upper, place.at(z=place.z_of(to)[0])),
            self.copies.push(lower, lower, place.at(x=place.x_of(to))),
        ]

    def spread(self):
        place = self.place
        upper = self.form.upper(self.whole, ALL, place.zl, place.zh)
        lower = self.form.lower(self.whole, place.x, ALL)
        self.ahead = self.both(upper, lower, 1)
        self.behind = self.both(upper, lower, 3)

    def relay(self, half):
        side, onto = ((3, 1), (1, 3))[half]
        _, zh, zl = self.place.z_of(side)
        upper = self.form.upper(self.whole, pl.ds(2 * half, 2), zl, zh)
        lower = self.form.lower(self.whole, self.place.x_of(side), pl.ds(half, 1))
        self.passed += self.both(upper, lower, onto)

    def to_sibling(self, d):
        place, form = self.place, self.form
        _, zh, zl = place.z_of(d)
        for part in (
            form.upper(self.whole, ALL, zl, zh),
            form.lower(self.whole, place.x_of(d), ALL),
        ):
            self.shared.append(self.copies.push(part, part, place.sibling()))

    def near(self):
        for d in (0, 1, 3):
            self.to_sibling(d)

    def far(self):
        self.to_sibling(2)


class Reduce:
    def __init__(self, copies, place, form, whole, spaces, buffers, put):
        self.copies, self.place, self.whole, self.put = copies, place, whole, put
        self.form, self.buffers = form, buffers
        (self.theirs, up_relayed, low_relayed, up_landed, low_landed, up_last, low_last) = spaces
        self.relayed, self.landed = (up_relayed, low_relayed), (up_landed, low_landed)
        self.last = (up_last, low_last)
        self.swapped, self.relays, self.sent = [], [], []
        self.arrivals, self.done, self.loads = ([], []), ([], []), {}

    def fetched(self, tasks, buffer, after, use, fetch, needs):
        loads = []

        def load():
            loads.extend(self.copies.local(src, dst) for src, dst in fetch())

        first = tasks.add(list(after) + self.buffers.users.get(buffer, []), load, needs)
        last = tasks.add([first], use, lambda: here(loads))
        self.buffers.users[buffer] = [last]
        return last

    def plan(self, tasks, tile, after, needs):
        buffers = self.buffers
        fills = [tasks.add(after, lambda: self.fill(tile, 0), needs)]
        fills.append(tasks.add(fills, lambda: self.fill(tile, 1)))
        self.filled = fills[1]
        adds = []
        for x in range(4):
            slot = fit(buffers.theirs.at[x % 2], self.theirs.shape[1:])
            adds.append(
                self.fetched(
                    tasks,
                    (0, x % 2),
                    [fills[x // 2]],
                    lambda x=x, slot=slot: self.add(x, slot),
                    lambda x=x, slot=slot: [(self.theirs.at[x], slot)],
                    (lambda x=x: recv(self.swapped[x // 2 : x // 2 + 1])) if x % 2 == 0 else nothing,
                )
            )
            if x % 2:
                tasks.all[adds[x] - 1][0].append(adds[x - 1] - 1)
        push = tasks.add(adds, self.push)
        relays = []
        for i in range(2):
            upper = fit(buffers.relayed[0].at[i], self.relayed[0].shape[1:])
            lower = fit(buffers.relayed[1].at[i], self.relayed[1].shape[1:])
            relays.append(
                self.fetched(
                    tasks,
                    (1, i),
                    [push],
                    lambda i=i, upper=upper, lower=lower: self.relay(i, upper, lower),
                    lambda i=i, upper=upper, lower=lower: [
                        (self.relayed[0].at[i], upper),
                        (self.relayed[1].at[i], lower),
                    ],
                    lambda i=i: recv(self.relays[i]),
                )
            )
        self.ended = []
        for i in range(2):
            slot = fit(buffers.landed[i], self.landed[i].shape)
            own = self.fetched(
                tasks,
                (2, i),
                relays,
                lambda i=i, slot=slot: self.own(i, slot),
                lambda i=i, slot=slot: [(self.landed[i], slot)],
                lambda i=i: recv(self.arrivals[i]),
            )
            slot = fit(buffers.landed[0].at[i, pl.ds(0, 3)], self.last[i].shape)
            self.ended.append(
                self.fetched(
                    tasks,
                    (2, 0),
                    [own],
                    lambda i=i, slot=slot: self.end(i, slot),
                    lambda i=i, slot=slot: [(self.last[i], slot)],
                    lambda i=i: recv(self.done[i]),
                )
            )

    def busy(self):
        return sent(self.sent)

    def fill(self, tile, part):
        place = self.place

        for x in (2 * part, 2 * part + 1):
            tile(x, self.whole, 1 - place.c)
            tile(x, self.whole, place.c)
        block = pl.ds(2 * part, 2)
        self.swapped.append(
            self.copies.push(
                self.form.core(self.whole, block, 1 - place.c),
                self.theirs.at[block],
                place.sibling(),
            )
        )
        self.sent.append(self.swapped[-1])

    def add(self, x, load):
        def body(zl, carry):
            to = self.whole.at[x, zl, pl.ds(2 * self.place.c, 2)]
            to[...] = (to[...].astype(F32) + load[zl].astype(F32)).astype(BF16)
            return carry

        lax.fori_loop(0, 2, body, 0)

    def push(self):
        place, whole = self.place, self.whole
        _, zh, zl = place.z_of(2)
        x = place.x_of(2)
        for half, to in ((0, 1), (1, 3)):
            upper = self.form.upper(whole, pl.ds(2 * half, 2), zl, zh)
            lower = self.form.lower(whole, x, pl.ds(half, 1))
            self.relays.append([
                self.copies.push(upper, self.relayed[0].at[half], place.at(z=place.z_of(to)[0])),
                self.copies.push(lower, self.relayed[1].at[half], place.at(x=place.x_of(to))),
            ])
            self.sent += self.relays[-1]
        for half, to in ((0, 1), (1, 3)):
            self.onward(half, 1 - half, to)

    def onward(self, slot, half, to):
        place = self.place
        z, zh, zl = place.z_of(to)
        x = place.x_of(to)
        two, one = pl.ds(2 * half, 2), pl.ds(half, 1)
        pair = (
            self.copies.push(
                self.form.upper(self.whole, two, zl, zh), self.landed[0].at[slot, two], place.at(z=z)
            ),
            self.copies.push(
                self.form.lower(self.whole, x, one), self.landed[1].at[slot, one], place.at(x=x)
            ),
        )
        for i in range(2):
            self.arrivals[i].append(pair[i])
        self.sent += pair

    def relay(self, half, upper, lower):
        to = (1, 3)[half]
        _, zh, zl = self.place.z_of(to)
        for i in range(2):
            at = self.form.upper(self.whole, 2 * half + i, zl, zh)
            at[...] = (at[...].astype(F32) + upper[i].astype(F32)).astype(BF16)
        at = self.form.lower(self.whole, self.place.x_of(to), half)
        at[...] = (at[...].astype(F32) + lower[0].astype(F32)).astype(BF16)
        self.onward(half, half, to)

    def own(self, i, load):
        place, whole = self.place, self.whole
        for k in range((4, 2)[i]):
            at = (
                self.form.upper(whole, k, place.zl, place.zh)
                if i == 0
                else self.form.lower(whole, place.x, k)
            )
            total = at[...].astype(F32) + load[0, k].astype(F32) + load[1, k].astype(F32)
            at[...] = total.astype(BF16)
        for d in (1, 3, 2):
            if i == 0:
                x = place.x_of(d)
                part, device = self.form.upper(whole, x, place.zl, place.zh), place.at(x=x)
            else:
                z, zh, zl = place.z_of(d)
                part, device = self.form.lower(whole, place.x, zl, zh), place.at(z=z)
            self.done[i].append(self.copies.push(part, self.last[i].at[d - 1], device))
        self.sent += self.done[i]

    def end(self, i, load):
        place = self.place
        if i == 0:
            at = self.form.upper(self.whole, place.x, place.zl, place.zh)
        else:
            at = self.form.lower(self.whole, place.x, place.zl, place.zh)
        total = at[...].astype(F32)
        for d in range(3):
            total += load[d].astype(F32)
        self.put(i, total)


class Buffers:
    def __init__(self, theirs, up_relayed, low_relayed, up_landed, low_landed):
        self.theirs, self.relayed = theirs, (up_relayed, low_relayed)
        self.landed = (up_landed, low_landed)
        self.users = {}


def both_ways(copies, place, src, dst):
    return [copies.push(src, dst, place.at(y=place.y_of(d))) for d in (1, 3)]


class Rows:
    def __init__(self, copies, place, whole):
        self.copies, self.place, self.whole = copies, place, whole
        self.sent, self.passed, self.parts = {}, {}, [0, 1, 2, 3]

    def send(self, k, src=None):
        mine = self.whole.at[self.place.y, self.parts[k]]
        self.sent[k] = both_ways(self.copies, self.place, mine if src is None else src, mine)

    def pass_on(self, k):
        side, onto = (3, 1) if k < 2 else (1, 3)
        place = self.place
        block = self.whole.at[place.y_of(side), self.parts[k]]
        self.passed[k] = self.copies.push(block, block, place.at(y=place.y_of(onto)))

    def plan(self, tasks, before):
        self.passes = [
            tasks.add(
                [before[k]],
                lambda k=k: self.pass_on(k),
                lambda k=k: recv([self.sent[k][0 if k < 2 else 1]]),
            )
            for k in range(4)
        ]
        self.have = tasks.add(
            self.passes,
            needs=lambda: recv(
                [self.sent[k][1 if k < 2 else 0] for k in range(4)]
                + [self.passed[k] for k in range(4)]
            ),
        )

    def busy(self):
        return sent([copy for pair in self.sent.values() for copy in pair]) + sent(
            list(self.passed.values())
        )


class Spread(Rows):
    def __init__(self, copies, place, held, whole):
        super().__init__(copies, place, whole)
        self.held = held
        self.parts = [place.m] + [place.quad(j)[1] for j in (1, 2, 3)]

    def quad(self):
        place = self.place
        mine = self.whole.at[place.y, place.m]
        self.own = self.copies.local(self.held.at[place.m], mine)
        self.came = []
        for j in (1, 2, 3):
            device, m = place.quad(j)
            self.came.append(self.copies.push(self.held.at[m], mine, device))

    def plan(self, tasks):
        quad = tasks.add((), self.quad)
        along = [
            tasks.add(
                [quad],
                lambda k=k: self.send(k),
                lambda k=k: recv([self.came[k - 1]]) if k else here([self.own]),
            )
            for k in range(4)
        ]
        super().plan(tasks, along)


class RowSum:
    def __init__(self, copies, place, part, buffers):
        self.copies, self.place, self.part = copies, place, part
        self.relayed, self.stage, self.arrived = buffers
        self.passed = {}

    def sides(self):
        ahead, behind = self.place.y_of(1), self.place.y_of(3)
        return (ahead, behind), (self.place.at(y=ahead), self.place.at(y=behind))

    def send(self):
        place = self.place
        near, onto = self.sides()
        across = place.y_of(2)
        self.first = [
            self.copies.push(self.part.at[across, k], self.relayed.at[k], onto[k // 2])
            for k in (0, 2, 1, 3)
        ]
        self.first = [self.first[i] for i in (0, 2, 1, 3)]
        self.direct = [
            self.copies.push(
                self.part.at[near[1 - k // 2], k], self.arrived.at[1 - k // 2, k], onto[1 - k // 2]
            )
            for k in range(4)
        ]

    def relay(self, k):
        near, onto = self.sides()
        total = self.part[near[k // 2], k].astype(F32) + self.relayed[k].astype(F32)
        self.stage[k] = total.astype(BF16)
        self.passed[k] = self.copies.push(
            self.stage.at[k], self.arrived.at[k // 2, k], onto[k // 2]
        )

    def plan(self, tasks, after, needs=nothing):
        send = tasks.add(after, self.send, needs)
        self.sums = [
            tasks.add([send], lambda k=k: self.relay(k), lambda k=k: recv([self.first[k]]))
            for k in range(4)
        ]

    def came(self, k):
        return recv([self.direct[k], self.passed[k]])

    def total(self, k):
        total = self.part[self.place.y, k].astype(F32)
        return total + self.arrived[0, k].astype(F32) + self.arrived[1, k].astype(F32)

    def busy(self):
        return sent(self.first + self.direct + list(self.passed.values()))


def lift(left, piece, kind, count):
    total = None
    for i in range(TILES):
        weight = piece[i // 2, i % 2, :, kind].reshape(count, 256)
        one = dot(columns(left, pl.ds(256 * i, 256), 256), weight, ((1,), (1,)))
        total = one if total is None else total + one
    return total


def layer_kernel(*refs):
    (held, grad_held, query_block, key_block, value_block, out_block, gain_block, unit_block,
     cos_in, sin_in,
     block_out, grad_out, gains_out, qkv_out, tall_out, out_out, first_out, x_out) = refs[:18]
    spaces = refs[18:53]
    rest = refs[53:]
    (rows, first, second, grads, qkv, probs, mixed, act, back, units, part,
     relayed, summed, arrived, down_relayed, down_summed, down_arrived, middle,
     stage, key_grad, value_grad,
     piece_a, piece_b, piece_c, qkv_w, out_w, gains, gain_row, ends,
     vec, vec_y, vec_x, vec_z, vec_c, half_x, half_z, half_c,
     send_sems, recv_sems, here_sems) = rest[:21] + rest[26:]
    place = Place()
    enter(place)
    copies = Copies(send_sems, recv_sems, here_sems)
    tasks = Tasks(copies)
    width = rows.shape[-1]
    buffers = Buffers(*rest[21:26])

    qkv_block = qkv_w.at[place.x, place.zl, 2 * place.c + place.zh]
    for kind, block in enumerate((query_block, key_block, value_block)):
        qkv_block[kind] = block[...].T
    pieces = (piece_a, piece_b, piece_c)
    forms = [Form(place, ROWS[p], FIRST[p]) for p in range(3)]
    head_form, out_form = Form(place, HD, FIRST[3]), Form(place, HD, FIRST[4])
    gather_q = Gather(copies, place, head_form, qkv_w, qkv_block, True)
    gather_o = Gather(copies, place, out_form, out_w, out_block)
    gathers = [
        Gather(copies, place, forms[p], pieces[p], unit_block.at[:, pl.ds(128 * p, ROWS[p])])
        for p in range(3)
    ]
    for gather in (gather_q, gather_o, *gathers):
        gather.plan(tasks)

    class Gains:
        pass

    gain = Gains()

    def begin_gains():
        target = gains.at[place.x, place.zl]
        gain.local = copies.local(gain_block, target)
        gain.first = [copies.push(gain_block, target, place.at(x=place.x_of(d))) for d in (1, 2, 3)]

    def spread_gains():
        column = gains.at[:, place.zl]
        gain.last = copies.push(column, column, place.at(z=2 * place.zh + 1 - place.zl))

    def have_gains():
        for i in range(TILES):
            gain_row[:, 256 * i : 256 * i + 256] = gains[i // 2, i % 2]

    begun = tasks.add((), begin_gains)
    passed = tasks.add([begun], spread_gains, lambda: here([gain.local]) + recv(gain.first))
    have_gain = tasks.add([passed], have_gains, lambda: recv([gain.last]))

    spread_x = Spread(copies, place, held, rows)
    spread_x.plan(tasks)
    spread_dy = Spread(copies, place, grad_held, grads)
    spread_dy.plan(tasks)

    def norm_first():
        def body(i, carry):
            y, j = lax.div(i, 4), lax.rem(i, 4)
            x = rows[y, j].astype(F32)
            first[y, j] = (x * factor_of(x) * gain_row[0:1, :]).astype(BF16)
            return carry

        lax.fori_loop(0, 16, body, 0)
        gain.x_out = copies.local(rows.at[place.y], x_out)
        gain.first_out = copies.local(first, first_out)

    norm1 = tasks.add([spread_x.have, have_gain], norm_first)

    def project(kind):
        both = lift(first, qkv_w, kind, 4 * HD)
        for h in range(4):
            one = both[:, h * HD : (h + 1) * HD]
            if kind < 2:
                one = turn(one, cos_in[...], sin_in[...])
            qkv[:, h * 3 * HD + kind * HD : h * 3 * HD + kind * HD + HD] = one.astype(BF16)

    projects = [
        tasks.add([norm1, gather_q.have], lambda kind=kind: project(kind)) for kind in range(3)
    ]

    def attend(i):
        for h in (2 * i, 2 * i + 1):
            for b in range(4):
                size = 128 * (b + 1)
                now = slice(128 * b, size)
                at = [slice(h * 3 * HD + k * HD, h * 3 * HD + k * HD + HD) for k in range(3)]
                scores = dot(qkv[now, at[0]], qkv[0:size, at[1]], ((1,), (1,)))
                allowed = lax.broadcasted_iota(jnp.int32, (128, size), 0) + 128 * b
                allowed = allowed >= lax.broadcasted_iota(jnp.int32, (128, size), 1)
                scores = jnp.where(allowed, scores * HD**-0.5, -jnp.inf)
                weight = jnp.exp(scores - jnp.max(scores, axis=-1, keepdims=True))
                weight = weight * (1.0 / jnp.sum(weight, axis=-1, keepdims=True))
                weight = weight.astype(BF16)
                start = 64 * b * (b + 1)
                probs[h, :, start : start + size] = weight
                blend = dot(weight, qkv[0:size, at[2]], ((1,), (0,)))
                mixed[now, h * HD : (h + 1) * HD] = blend.astype(BF16)

    attends = [tasks.add(projects, lambda i=i: attend(i)) for i in range(2)]

    def output():
        for i in range(TILES):
            weight = out_w[i // 2, i % 2].reshape(4 * HD, 256)
            total = dot(mixed[...], weight, ((1,), (0,)))
            part[:, :, :, tile_cols(i, 256)] = total.astype(BF16).reshape(4, 4, 32, 256)

    outputs = tasks.add([*attends, gather_o.have], output)
    sum_out = RowSum(copies, place, part, (relayed, summed, arrived))
    sum_out.plan(tasks, [outputs])
    rows_a = Rows(copies, place, second)

    def middle_part(k):
        now = pl.ds(32 * k, 32)
        mid = rows[place.y, k].astype(F32) + sum_out.total(k)
        middle[now, :] = mid
        stage[k] = (mid * factor_of(mid) * gain_row[1:2, :]).astype(BF16)
        rows_a.send(k, stage.at[k])
        second[place.y, k] = stage[k]

    mids = [
        tasks.add(
            [sum_out.sums[k], norm1],
            lambda k=k: middle_part(k),
            lambda k=k: sum_out.came(k) + spread_x.busy(),
        )
        for k in range(4)
    ]
    rows_a.plan(tasks, mids)

    def lift_back(p):
        count = 4 * ROWS[p]
        back[:, 512 * p : 512 * p + count] = lift(grads, pieces[p], 2, count).astype(BF16)

    def open_units(p, kind):
        count = 4 * ROWS[p]
        act[kind, :, 0:count] = lift(second, pieces[p], kind, count).astype(BF16)

    def gating(p):
        for j in range(4 * ROWS[p] // 128):
            cols = slice(128 * j, 128 * j + 128)
            opened, lifted = act[0, :, cols].astype(F32), act[1, :, cols].astype(F32)
            change = back[:, 512 * p + 128 * j : 512 * p + 128 * j + 128].astype(F32)
            sig = 1.0 / (1.0 + jnp.exp(-opened))
            silu = opened * sig
            result = (
                (change * lifted * sig * (1.0 + opened * (1.0 - sig))).astype(BF16),
                (change * silu).astype(BF16),
                (silu * lifted).astype(BF16),
            )
            for kind in range(3):
                act[kind, :, cols] = result[kind]
                turned, at = result[kind].T, 0
                while at < 128:
                    c, row = divmod(128 * j + at, 2 * ROWS[p])
                    size = min(128 - at, 2 * ROWS[p] - row)
                    units[p % 2, c, kind, row : row + size, :] = turned[at : at + size]
                    at += size

    def sum_up(target, p, kinds):
        count = 4 * ROWS[p]

        for i in range(TILES):
            cols = tile_cols(i, 256)
            total = None
            for kind in kinds:
                weight = pieces[p][i // 2, i % 2, :, kind].reshape(count, 256)
                one = dot(act[kind, :, 0:count], weight, ((1,), (0,)))
                total = one if total is None else total + one
            if p:
                total += columns(target, cols, 256).astype(F32)
            target[:, :, :, cols] = total.astype(BF16).reshape(4, 4, 32, 256)

    def of_units(count, turned, middle_rows, right):
        def tile(x, target, c):
            cols = tile_cols(x, 512)
            pair = dot(
                turned[c, 0:2, 0 : 2 * count].reshape(4 * count, 512),
                columns(middle_rows, cols, 512),
                ((1,), (0,)),
            ).astype(BF16)
            one = dot(turned[c, 2, 0 : 2 * count], columns(right, cols, 512), ((1,), (0,)))
            one = one.astype(BF16)
            for zl in range(2):
                at = slice(256 * zl, 256 * zl + 256)
                for zh in range(2):
                    block = target.at[x, zl, 2 * c + zh]
                    for kind in range(2):
                        start = (2 * kind + zh) * count
                        block[kind] = pair[start : start + count, at]
                    block[2] = one[zh * count : (zh + 1) * count, at]

        return tile

    slots = [None, None]

    def put_units(p):
        def put(i, total):
            if slots[i] is not None:
                slots[i].wait()
            start, size = FIRST[p] * i, (FIRST[p], ROWS[p] - FIRST[p])[i]
            ends[i, :, 0:size, :] = total
            slots[i] = copies.local(
                ends.at[i, :, pl.ds(0, size)], tall_out.at[:, pl.ds(128 * p + start, size)]
            )

        return put

    def put_heads(i, total):
        for kind in range(3):
            qkv_out[kind, :, FIRST[3] * i : (FIRST[3], HD)[i]] = total[kind].T

    def put_out(i, total):
        out_out[FIRST[4] * i : (FIRST[4], HD)[i], :] = total[0]

    reduces = [
        Reduce(copies, place, form, whole, spaces[7 * i : 7 * i + 7], buffers, put)
        for i, (form, whole, put) in enumerate((
            (forms[0], piece_a, put_units(0)),
            (forms[1], piece_b, put_units(1)),
            (forms[2], piece_c, put_units(2)),
            (head_form, piece_a, put_heads),
            (out_form, out_w, put_out),
        ))
    ]
    earlier, filled = [], []
    for p in range(3):
        have = gathers[p].have
        lifted = tasks.add([spread_dy.have, have], lambda p=p: lift_back(p))
        opened = [
            tasks.add([rows_a.have, have] + earlier, lambda p=p, kind=kind: open_units(p, kind))
            for kind in range(2)
        ]
        gated = tasks.add([lifted] + opened + filled[: max(0, p - 1)], lambda p=p: gating(p))
        da2 = tasks.add(
            [gated] + mids,
            lambda p=p: sum_up(part, p, (0, 1)),
            sum_out.busy if p == 0 else nothing,
        )
        downed = tasks.add(
            [gated] + projects,
            lambda p=p: sum_up(first, p, (2,)),
            (lambda: here([gain.first_out])) if p == 0 else nothing,
        )
        earlier = [da2, downed]
        reduces[p].plan(tasks, of_units(ROWS[p], units.at[p % 2], second, grads), earlier, gathers[p].busy)
        filled = filled + [reduces[p].filled]

    sum_mid = RowSum(copies, place, part, (relayed, summed, arrived))
    sum_mid.plan(tasks, [da2])
    rows_m = Rows(copies, place, rows)
    gain.mlp = jnp.zeros((1, width), F32)

    def mid_back(k):
        now = pl.ds(32 * k, 32)
        result, gain_part = norm_back(sum_mid.total(k), middle[now, :], gain_row[1:2, :])
        gain.mlp += gain_part
        result += grads[place.y, k].astype(F32)
        stage[k] = result.astype(BF16)
        rows_m.send(k, stage.at[k])
        rows[place.y, k] = stage[k]

    dmids = []
    for k in range(4):
        dmids += [tasks.add(
            [sum_mid.sums[k], rows_a.passes[k]] + dmids[:1],
            lambda k=k: mid_back(k),
            lambda k=k: sum_mid.came(k) + sent(rows_a.sent[k]) + (here([gain.x_out]) if k == 0 else []),
        )]
    rows_m.plan(tasks, dmids)
    sum_down = RowSum(copies, place, first, (down_relayed, down_summed, down_arrived))
    sum_down.plan(tasks, [downed])

    out_stage = down_relayed

    def out_part(k):
        now = pl.ds(32 * k, 32)
        out_stage[k] = (middle[now, :] + sum_down.total(k)).astype(BF16)

    def to_quad(source, target, state):
        state.append(copies.local(source.at[place.m], target.at[place.m]))
        for j in (1, 2, 3):
            device, m = place.quad(j)
            state.append(copies.push(source.at[m], target.at[place.m], device))

    out_state, in_state = [], []
    outs = [
        tasks.add([sum_down.sums[k]], lambda k=k: out_part(k), lambda k=k: sum_down.came(k))
        for k in range(4)
    ]
    gone = tasks.add(outs, lambda: to_quad(out_stage, block_out, out_state))
    tasks.add([gone], needs=lambda: here(out_state[:1]) + recv(out_state[1:]))

    def unmix():
        act[0] = sum(
            dot(
                columns(rows, pl.ds(256 * i, 256), 256),
                out_w[i // 2, i % 2].reshape(4 * HD, 256),
                ((1,), (1,)),
            )
            for i in range(TILES)
        ).astype(BF16)

    unmixed = tasks.add([rows_m.have, *earlier], unmix)

    def of_mixed(x, target, c):
        left = mixed[:, pl.ds(pl.multiple_of(2 * c * HD, 128), 2 * HD)].T
        one = dot(left, columns(rows, tile_cols(x, 512), 512), ((1,), (0,))).astype(BF16)
        for zl in range(2):
            for zh in range(2):
                target[x, zl, 2 * c + zh, 0] = one[
                    zh * HD : (zh + 1) * HD, 256 * zl : 256 * zl + 256
                ]

    reduces[4].plan(tasks, of_mixed, [unmixed], gather_o.busy)

    def attend_back(i):
        for h in (2 * i, 2 * i + 1):
            at = [slice(h * 3 * HD + k * HD, h * 3 * HD + k * HD + HD) for k in range(3)]
            key_grad[...] = jnp.zeros(key_grad.shape, F32)
            value_grad[...] = jnp.zeros(value_grad.shape, F32)
            for b in range(4):
                size = 128 * (b + 1)
                now, so_far = slice(128 * b, size), slice(0, size)
                start = 64 * b * (b + 1)
                weight = probs[h, :, start : start + size]
                mix = act[0, now, h * HD : (h + 1) * HD]
                value_grad[so_far, :] += dot(weight, mix, ((0,), (0,)))
                change = dot(mix, qkv[so_far, at[2]], ((1,), (1,)))
                weight = weight.astype(F32)
                change = weight * (change - jnp.sum(weight * change, axis=-1, keepdims=True))
                change = change.astype(BF16)
                query = dot(change, qkv[so_far, at[1]], ((1,), (0,))) * HD**-0.5
                query = turn_back(query, cos_in[now, :], sin_in[now, :])
                back[now, at[0]] = query.astype(BF16)
                key_grad[so_far, :] += dot(change, qkv[now, at[0]], ((0,), (0,)))
            key = turn_back(key_grad[...] * HD**-0.5, cos_in[...], sin_in[...])
            back[:, at[1]] = key.astype(BF16)
            back[:, at[2]] = value_grad[...].astype(BF16)
            start = h % 2 * HD
            for kind in range(3):
                units[1, h // 2, kind, start : start + HD, :] = back[:, at[kind]].T

    abacks = [tasks.add([unmixed, gated] + filled, lambda i=i: attend_back(i)) for i in range(2)]

    def first_back():
        for i in range(TILES):
            weight = qkv_w[i // 2, i % 2].reshape(12 * HD, 256)
            total = dot(back[...], weight, ((1,), (0,)))
            grads[:, :, :, tile_cols(i, 256)] = total.astype(BF16).reshape(4, 4, 32, 256)

    da1 = tasks.add([*abacks, *filled, *dmids], first_back, spread_dy.busy)
    sum_first = RowSum(copies, place, grads, (relayed, summed, arrived))
    sum_first.plan(tasks, [da1] + rows_m.passes, sum_mid.busy)

    def reload():
        gain.first_in = copies.local(first_out, second)

    reloaded = tasks.add(filled, reload, rows_a.busy)
    reduces[3].plan(
        tasks,
        of_units(HD, units.at[1], second, second),
        [*abacks, reloaded, *reduces[0].ended],
        lambda: here([gain.first_in]) + reduces[0].busy(),
    )
    gain.attn = jnp.zeros((1, width), F32)

    def in_part(k):
        now = pl.ds(32 * k, 32)
        result, gain_part = norm_back(
            sum_first.total(k), stage[k].astype(F32), gain_row[0:1, :]
        )
        gain.attn += gain_part
        stage[k] = (rows[place.y, k].astype(F32) + result).astype(BF16)

    def load_x():
        gain.x_in = copies.local(x_out, stage)

    def sent_m():
        return sent([copy for pair in rows_m.sent.values() for copy in pair])

    got_x = tasks.add([*dmids, *rows_m.passes], load_x, sent_m)
    have_x = tasks.add([got_x], needs=lambda: here([gain.x_in]))
    ins = [
        tasks.add(
            [sum_first.sums[k], have_x], lambda k=k: in_part(k), lambda k=k: sum_first.came(k)
        )
        for k in range(4)
    ]
    gone = tasks.add(ins, lambda: to_quad(stage, grad_out, in_state))
    tasks.add([gone], needs=lambda: here(in_state[:1]) + recv(in_state[1:]))

    def gain_y():
        vec[0:1, :] = gain.attn
        vec[1:2, :] = gain.mlp
        vec[2:8, :] = jnp.zeros((6, width), F32)
        gain.y = [copies.push(vec, vec_y.at[d - 1], place.at(y=place.y_of(d))) for d in (1, 3, 2)]

    def of_x(x):
        return pl.ds(pl.multiple_of(x * 512, 128), 512)

    def of_z(zl):
        return pl.ds(pl.multiple_of(zl * 256, 128), 256)

    def gain_x():
        half_x[...] = vec[...] + vec_y[0] + vec_y[1] + vec_y[2]
        gain.x = []
        for d in (1, 3, 2):
            x = place.x_of(d)
            gain.x.append(copies.push(half_x.at[:, of_x(x)], vec_x.at[d - 1], place.at(x=x)))

    def gain_z():
        half_z[...] = half_x[:, of_x(place.x)] + vec_x[0] + vec_x[1] + vec_x[2]
        gain.z = []
        for d in (1, 3, 2):
            z, zh, zl = place.z_of(d)
            gain.z.append(copies.push(half_z.at[:, of_z(zl)], vec_z.at[d - 1], place.at(z=z)))

    def gain_c():
        half_c[...] = half_z[:, of_z(place.zl)] + vec_z[0] + vec_z[1] + vec_z[2]
        gain.c = copies.push(half_c, vec_c, place.sibling())

    def gain_end():
        gains_out[...] = half_c[...] + vec_c[...]

    over_y = tasks.add(ins + dmids, gain_y)
    over_x = tasks.add([over_y], gain_x, lambda: recv(gain.y))
    over_z = tasks.add([over_x], gain_z, lambda: recv(gain.x))
    over_c = tasks.add([over_z], gain_c, lambda: recv(gain.z))
    tasks.add([over_c], gain_end, lambda: recv([gain.c]))

    drive(tasks, ORDER)
    for copy in slots:
        copy.wait()
    copies.drain()


def tables(length):
    half_size = HD // 2
    inverse_freq = np.float32(THETA) ** (-(np.arange(half_size, dtype=np.float32) * 2.0) / HD)
    angles = np.arange(length, dtype=np.float32)[:, None] * inverse_freq.astype(np.float32)[None]
    cos_t, sin_t = np.cos(angles), np.sin(angles)
    return (
        jnp.asarray(np.concatenate([cos_t, cos_t], axis=1), F32),
        jnp.asarray(np.concatenate([-sin_t, sin_t], axis=1), F32),
    )


def local(
    hidden_in,
    cotangent,
    gain_attn,
    w_query,
    w_key,
    w_value,
    w_output,
    gain_mlp,
    w_gate,
    w_up,
    w_down,
):
    held, grad_held = hidden_in[:, 0], cotangent[:, 0]
    width = held.shape[2]
    length = 512
    count = w_gate.shape[1]
    unit_block = jnp.pad(
        jnp.stack([w_gate.T, w_up.T, w_down]), ((0, 0), (0, UNITS - count), (0, 0))
    )
    which = lax.broadcasted_iota(jnp.int32, (8, 256), 0)
    gains = jnp.where(which == 0, gain_attn[None].astype(F32), gain_mlp[None].astype(F32))
    cos_t, sin_t = tables(length)
    blocks = ((4, 4, 32, width), BF16)
    heads = ((length, 12 * HD), BF16)
    square = ((length, length), BF16)
    own_f32 = ((128, width), F32)
    parts = ((4, 32, width), BF16)
    sums = [parts, parts, ((2, 4, 32, width), BF16)]

    def spaces(kinds, size, first):
        up, low = (kinds, first, 256), (kinds, size - first, 256)
        return [
            ((4, 2, 2, kinds, size, 256), BF16),
            ((2, 2, *up), BF16),
            ((2, 1, 2, *low), BF16),
            ((2, 4, *up), BF16),
            ((2, 2, 2, *low), BF16),
            ((3, *up), BF16),
            ((3, *low), BF16),
        ]

    def whole(kinds, size):
        return ((4, 2, 4, kinds, size, 256), BF16)

    landing = []
    for i, size in enumerate((*ROWS, HD, HD)):
        landing += spaces(1 if i == 4 else 3, size, FIRST[i])
    outs = [
        parts, parts, ((8, 256), F32), ((3, 256, HD), F32), ((3, UNITS, 256), F32),
        ((HD, 256), F32), blocks, parts,
    ]
    up, low = max(FIRST), HD - min(FIRST[0], FIRST[1], FIRST[3])
    buffers = [
        ((2, 2, 2, 3, HD, 256), BF16),
        ((2, 2, 3, up, 256), BF16), ((2, 1, 2, 3, low, 256), BF16),
        ((2, 4, 3, max(up, low), 256), BF16), ((2, 2, 2, 3, low, 256), BF16),
    ]
    scratch = [
        blocks, blocks, blocks, blocks, heads, ((4, 128, 1280), BF16), square,
        ((3, length, length), BF16), heads, ((2, 2, 3, 256, length), BF16), blocks,
        *sums, *sums, own_f32, parts,
        ((length, HD), F32), ((length, HD), F32), *buffers,
        whole(3, ROWS[0]), whole(3, ROWS[1]), whole(3, ROWS[2]), whole(3, HD), whole(1, HD),
        ((4, 2, 8, 256), F32), ((8, width), F32), ((2, 3, max(up, low), 256), F32),
        ((8, width), F32), ((3, 8, width), F32), ((3, 8, 512), F32), ((3, 8, 256), F32),
        ((8, 256), F32), ((8, width), F32), ((8, 512), F32), ((8, 256), F32),
    ]
    block_out, grad_in, gains_out, qkv_g, tall_g, out_g = pl.pallas_call(
        layer_kernel,
        out_shape=[jax.ShapeDtypeStruct(shape, dtype) for shape, dtype in outs + landing],
        in_specs=[ANY] * 2 + [VMEM] * 3 + [ANY] * 3 + [VMEM] * 2,
        out_specs=[ANY, ANY, VMEM, VMEM, ANY, VMEM, ANY, ANY] + [ANY] * len(landing),
        scratch_shapes=[
            *[pltpu.VMEM(shape, dtype) for shape, dtype in scratch],
            pltpu.SemaphoreType.DMA((COPIES,)),
            pltpu.SemaphoreType.DMA((COPIES,)),
            pltpu.SemaphoreType.DMA((LOCALS,)),
        ],
        compiler_params=pltpu.CompilerParams(
            collective_id=0, has_side_effects=True, vmem_limit_bytes=VMEM_LIMIT
        ),
    )(held, grad_held, w_query, w_key, w_value, w_output[None], gains, unit_block, cos_t, sin_t)[:6]
    return (
        block_out[:, None],
        grad_in[:, None],
        gains_out[0],
        qkv_g[0],
        qkv_g[1],
        qkv_g[2],
        out_g,
        gains_out[1],
        tall_g[0, :count].T,
        tall_g[1, :count].T,
        tall_g[2, :count],
    )


def solution(mesh):
    rows = P(None, "fsdp", "tensor", None)
    into, out_of = P("fsdp", "tensor"), P("tensor", "fsdp")
    return jax.shard_map(
        local,
        mesh=mesh,
        in_specs=(
            rows, rows, P("fsdp"), into, into, into, out_of, P("fsdp"), into, into, out_of,
        ),
        out_specs=(
            rows, rows, P("fsdp"), into, into, into, out_of, P("fsdp"), into, into, out_of,
        ),
        check_vma=False,
    )
```

```python
import jax
import jax.numpy as jnp
import numpy as np
from jax import lax
from jax.experimental import pallas as pl
from jax.experimental.pallas import tpu as pltpu
from jax.sharding import PartitionSpec as P


HD = 128
UNITS = 352
ROWS = (128, 128, 96)
FIRST = (64, 64, 48, 64, 64)
EPSILON = 1e-05
THETA = 10000.0
MESH = pl.DeviceIdType.MESH
F32 = jnp.float32
BF16 = jnp.bfloat16
COPIES = 400
LOCALS = 130
TILES = 8
ALL = slice(None)
RECV, SENT, HERE = range(3)
ANY = pl.BlockSpec(memory_space=pl.ANY)
VMEM = pl.BlockSpec(memory_space=pltpu.VMEM)
VMEM_LIMIT = 62 * 2**20

ORDER = (
    9, 0, 57, 54, 59, 58, 55, 63, 1, 60, 61, 10, 64, 4, 3, 18, 2, 6, 5, 65, 12, 67, 11, 14, 62, 13,
    56, 69, 7, 66, 19, 68, 77, 45, 70, 15, 73, 8, 78, 79, 71, 16, 72, 17, 22, 74, 21, 24, 20, 23,
    80, 27, 82, 46, 75, 25, 81, 26, 83, 84, 76, 28, 87, 48, 88, 36, 49, 51, 86, 85, 90, 47, 29, 30,
    33, 31, 50, 91, 92, 52, 37, 32, 89, 34, 53, 94, 95, 156, 96, 40, 93, 35, 98, 39, 42, 38, 41,
    97, 99, 100, 101, 102, 43, 103, 104, 105, 44, 128, 127, 129, 130, 131, 158, 157, 159, 160, 185,
    106, 108, 132, 107, 109, 110, 112, 133, 111, 113, 114, 186, 188, 134, 161, 162, 135, 137, 187,
    115, 117, 189, 116, 118, 138, 163, 136, 139, 141, 190, 192, 244, 140, 142, 143, 164, 166, 123,
    124, 193, 191, 119, 146, 144, 147, 145, 167, 165, 168, 196, 194, 170, 171, 169, 120, 195, 172,
    197, 152, 199, 125, 126, 153, 198, 210, 211, 236, 202, 173, 121, 175, 212, 200, 176, 122, 174,
    213, 234, 201, 214, 215, 245, 235, 203, 217, 246, 237, 216, 219, 247, 181, 218, 220, 221, 248,
    182, 238, 250, 249, 252, 224, 222, 239, 251, 254, 225, 223, 253, 255, 256, 269, 207, 154, 205,
    206, 148, 204, 208, 149, 177, 259, 270, 178, 242, 230, 231, 241, 271, 273, 292, 257, 260, 243,
    258, 272, 274, 293, 155, 275, 183, 277, 276, 278, 279, 226, 240, 209, 295, 265, 296, 266, 227,
    184, 297, 282, 280, 294, 300, 281, 283, 261, 262, 150, 232, 298, 301, 284, 288, 285, 151, 179,
    302, 289, 233, 180, 228, 229, 263, 299, 264, 303, 286, 267, 268, 304, 287, 290, 291,
)


class Place:
    def __init__(self):
        f = lax.axis_index("fsdp")
        t = lax.axis_index("tensor")
        self.x, self.zl = lax.div(f, 2), lax.rem(f, 2)
        self.y, self.m = lax.div(t, 4), lax.rem(t, 4)
        self.zh, self.c = lax.div(self.m, 2), lax.rem(self.m, 2)
        self.z = 2 * self.zh + self.zl

    def at(self, x=None, z=None, y=None, c=None):
        x = self.x if x is None else x
        z = self.z if z is None else z
        y = self.y if y is None else y
        c = self.c if c is None else c
        return (2 * x + lax.rem(z, 2), 4 * y + 2 * lax.div(z, 2) + c)

    def x_of(self, d):
        return lax.rem(self.x + d, 4)

    def y_of(self, d):
        return lax.rem(self.y + d, 4)

    def z_of(self, d):
        z = lax.rem(self.z + d, 4)
        return z, lax.div(z, 2), lax.rem(z, 2)

    def quad(self, j):
        zh = 1 - self.zh if j & 2 else self.zh
        c = 1 - self.c if j & 1 else self.c
        return self.at(z=2 * zh + self.zl, c=c), 2 * zh + c

    def sibling(self):
        return self.at(c=1 - self.c)


class Copies:
    def __init__(self, send, recv, here):
        self.send, self.recv, self.here = send, recv, here
        self.sent, self.waited, self.kept = [], [], 0

    def push(self, src, dst, device):
        k = len(self.sent)
        assert k < COPIES
        copy = pltpu.make_async_remote_copy(
            src_ref=src,
            dst_ref=dst,
            send_sem=self.send.at[k],
            recv_sem=self.recv.at[k],
            device_id=device,
            device_id_type=MESH,
        )
        copy.start()
        self.sent.append(copy)
        return copy

    def local(self, src, dst):
        assert self.kept < LOCALS
        copy = pltpu.make_async_copy(src, dst, self.here.at[self.kept])
        copy.start()
        self.kept += 1
        return copy

    def wait(self, copy, kind):
        if kind == RECV:
            copy.wait_recv()
        elif kind == HERE:
            copy.wait()
        elif not any(copy is other for other in self.waited):
            copy.wait_send()
            self.waited.append(copy)

    def drain(self):
        for copy in self.sent:
            self.wait(copy, SENT)


def recv(copies):
    return [(copy, RECV) for copy in copies]


def sent(copies):
    return [(copy, SENT) for copy in copies]


def here(copies):
    return [(copy, HERE) for copy in copies]


def nothing():
    return ()


class Tasks:
    def __init__(self, copies):
        self.copies, self.all = copies, []

    def add(self, after, run=nothing, needs=nothing):
        self.all.append((list(after), needs, run))
        return len(self.all) - 1


def drive(tasks, order):
    done = set()
    for number in order:
        after, needs, run = tasks.all[number]
        assert done.issuperset(after), number
        for copy, kind in needs():
            tasks.copies.wait(copy, kind)
        run()
        done.add(number)
    assert len(done) == len(tasks.all)


def enter(place):
    barrier = pltpu.get_barrier_semaphore()
    others = [place.at(y=place.y_of(d)) for d in (1, 2, 3)]
    others += [place.at(x=place.x_of(d)) for d in (1, 2, 3)]
    others += [place.at(z=place.z_of(d)[0]) for d in (1, 2, 3)]
    others += [place.quad(1)[0], place.quad(3)[0]]
    for other in others:
        pl.semaphore_signal(barrier, inc=1, device_id=other, device_id_type=MESH)
    pl.semaphore_wait(barrier, len(others))


def dot(left, right, dims):
    return lax.dot_general(left, right, (dims, ((), ())), preferred_element_type=F32)


def turn(rows, cos_t, sin_t):
    return rows * cos_t + pltpu.roll(rows, HD // 2, 1) * sin_t


def turn_back(rows, cos_t, sin_t):
    return rows * cos_t - pltpu.roll(rows, HD // 2, 1) * sin_t


def head_cols(h, part):
    return pl.ds(pl.multiple_of(h * 3 * HD + part * HD, HD), HD)


def tile_cols(i, size):
    return pl.ds(pl.multiple_of(i * size, size), size)


def columns(rows, cols, size):
    return rows[:, :, :, cols].reshape(512, size)


def factor_of(rows):
    return lax.rsqrt(jnp.mean(rows * rows, axis=-1, keepdims=True) + EPSILON)


def norm_back(grad, rows, gain):
    factor = factor_of(rows)
    scaled = grad * gain
    back = factor * scaled - rows * factor**3 * jnp.mean(scaled * rows, axis=-1, keepdims=True)
    return back, jnp.sum(grad * rows * factor, axis=0, keepdims=True)


def fit(ref, shape):
    index = tuple(
        ALL if have == want else pl.ds(0, want) for have, want in zip(ref.shape, shape, strict=True)
    )
    return ref.at[index]


class Form:
    def __init__(self, place, rows, first):
        self.place = place
        self.up, self.low = pl.ds(0, first), pl.ds(first, rows - first)

    def upper(self, ref, x, zl, zh):
        return ref.at[x, zl, 2 * self.place.c + zh, :, self.up]

    def lower(self, ref, x, zl, zh=None):
        block = pl.ds(2 * self.place.c, 2) if zh is None else 2 * self.place.c + zh
        return ref.at[x, zl, block, :, self.low]

    def core(self, ref, x, c):
        return ref.at[x, :, pl.ds(2 * c, 2)]


class Gather:
    def __init__(self, copies, place, form, whole, block, placed=False):
        self.copies, self.place, self.whole, self.block = copies, place, whole, block
        self.form, self.placed = form, placed

    def plan(self, tasks):
        self.passed, self.shared = [], []
        begin = tasks.add((), self.begin)
        spread = tasks.add([begin], self.spread, lambda: here(self.local) + recv(self.first))
        ahead = tasks.add([spread], lambda: self.relay(0), lambda: recv(self.ahead))
        behind = tasks.add([spread], lambda: self.relay(1), lambda: recv(self.behind))
        near = [tasks.add([spread], lambda: self.to_sibling(0))]
        near.append(tasks.add([ahead], lambda: self.to_sibling(3)))
        near.append(tasks.add([behind], lambda: self.to_sibling(1)))
        far = tasks.add(
            [ahead, behind, *near], lambda: self.to_sibling(2), lambda: recv(self.passed)
        )
        self.have = tasks.add([far], needs=lambda: recv(self.shared))

    def busy(self):
        return sent(self.ahead + self.behind + self.passed + self.shared)

    def begin(self):
        place, block, form = self.place, self.block, self.form
        self.local = []
        if not self.placed:
            target = self.whole.at[place.x, place.zl, 2 * place.c + place.zh]
            self.local.append(self.copies.local(block, target))
        upper, lower = block.at[:, form.up], block.at[:, form.low]
        to_upper = form.upper(self.whole, place.x, place.zl, place.zh)
        to_lower = form.lower(self.whole, place.x, place.zl, place.zh)
        self.first = []
        for d in (1, 3, 2):
            self.first.append(self.copies.push(upper, to_upper, place.at(x=place.x_of(d))))
            self.first.append(self.copies.push(lower, to_lower, place.at(z=place.z_of(d)[0])))

    def both(self, upper, lower, to):
        place = self.place
        return [
            self.copies.push(upper, upper, place.at(z=place.z_of(to)[0])),
            self.copies.push(lower, lower, place.at(x=place.x_of(to))),
        ]

    def spread(self):
        place = self.place
        upper = self.form.upper(self.whole, ALL, place.zl, place.zh)
        lower = self.form.lower(self.whole, place.x, ALL)
        self.ahead = self.both(upper, lower, 1)
        self.behind = self.both(upper, lower, 3)

    def relay(self, half):
        side, onto = ((3, 1), (1, 3))[half]
        _, zh, zl = self.place.z_of(side)
        upper = self.form.upper(self.whole, pl.ds(2 * half, 2), zl, zh)
        lower = self.form.lower(self.whole, self.place.x_of(side), pl.ds(half, 1))
        self.passed += self.both(upper, lower, onto)

    def to_sibling(self, d):
        place, form = self.place, self.form
        _, zh, zl = place.z_of(d)
        for part in (
            form.upper(self.whole, ALL, zl, zh),
            form.lower(self.whole, place.x_of(d), ALL),
        ):
            self.shared.append(self.copies.push(part, part, place.sibling()))


class Reduce:
    def __init__(self, copies, place, form, whole, spaces, buffers, put):
        self.copies, self.place, self.whole, self.put = copies, place, whole, put
        self.form, self.buffers = form, buffers
        (self.theirs, up_relayed, low_relayed, up_landed, low_landed, up_last, low_last) = spaces
        self.relayed, self.landed = (up_relayed, low_relayed), (up_landed, low_landed)
        self.last = (up_last, low_last)
        self.swapped, self.relays, self.sent = [], [], []
        self.arrivals, self.done, self.loads = ([], []), ([], []), {}

    def fetched(self, tasks, buffer, after, use, fetch, needs):
        loads = []

        def load():
            loads.extend(self.copies.local(src, dst) for src, dst in fetch())

        first = tasks.add(list(after) + self.buffers.users.get(buffer, []), load, needs)
        last = tasks.add([first], use, lambda: here(loads))
        self.buffers.users[buffer] = [last]
        return last

    def plan(self, tasks, tile, after, needs):
        buffers = self.buffers
        fills = [tasks.add(after, lambda: self.fill(tile, 0), needs)]
        fills.append(tasks.add(fills, lambda: self.fill(tile, 1)))
        self.filled = fills[1]
        adds = []
        for x in range(4):
            slot = fit(buffers.theirs.at[x % 2], self.theirs.shape[1:])
            adds.append(
                self.fetched(
                    tasks,
                    (0, x % 2),
                    [fills[x // 2]],
                    lambda x=x, slot=slot: self.add(x, slot),
                    lambda x=x, slot=slot: [(self.theirs.at[x], slot)],
                    (lambda x=x: recv(self.swapped[x // 2 : x // 2 + 1])) if x % 2 == 0 else nothing,
                )
            )
            if x % 2:
                tasks.all[adds[x] - 1][0].append(adds[x - 1] - 1)
        push = tasks.add(adds, self.push)
        relays = []
        for i in range(2):
            upper = fit(buffers.relayed[0].at[i], self.relayed[0].shape[1:])
            lower = fit(buffers.relayed[1].at[i], self.relayed[1].shape[1:])
            relays.append(
                self.fetched(
                    tasks,
                    (1, i),
                    [push],
                    lambda i=i, upper=upper, lower=lower: self.relay(i, upper, lower),
                    lambda i=i, upper=upper, lower=lower: [
                        (self.relayed[0].at[i], upper),
                        (self.relayed[1].at[i], lower),
                    ],
                    lambda i=i: recv(self.relays[i]),
                )
            )
        self.ended = []
        for i in range(2):
            slot = fit(buffers.landed[i], self.landed[i].shape)
            own = self.fetched(
                tasks,
                (2, i),
                relays,
                lambda i=i, slot=slot: self.own(i, slot),
                lambda i=i, slot=slot: [(self.landed[i], slot)],
                lambda i=i: recv(self.arrivals[i]),
            )
            slot = fit(buffers.last[i], self.last[i].shape)
            self.ended.append(
                self.fetched(
                    tasks,
                    (3, i),
                    [own],
                    lambda i=i, slot=slot: self.end(i, slot),
                    lambda i=i, slot=slot: [(self.last[i], slot)],
                    lambda i=i: recv(self.done[i]),
                )
            )

    def busy(self):
        return sent(self.sent)

    def fill(self, tile, part):
        place = self.place

        for x in (2 * part, 2 * part + 1):
            tile(x, self.whole, 1 - place.c)
            tile(x, self.whole, place.c)
        block = pl.ds(2 * part, 2)
        self.swapped.append(
            self.copies.push(
                self.form.core(self.whole, block, 1 - place.c),
                self.theirs.at[block],
                place.sibling(),
            )
        )
        self.sent.append(self.swapped[-1])

    def add(self, x, load):
        def body(zl, carry):
            to = self.whole.at[x, zl, pl.ds(2 * self.place.c, 2)]
            to[...] = (to[...].astype(F32) + load[zl].astype(F32)).astype(BF16)
            return carry

        lax.fori_loop(0, 2, body, 0)

    def push(self):
        place, whole = self.place, self.whole
        _, zh, zl = place.z_of(2)
        x = place.x_of(2)
        for half, to in ((0, 1), (1, 3)):
            upper = self.form.upper(whole, pl.ds(2 * half, 2), zl, zh)
            lower = self.form.lower(whole, x, pl.ds(half, 1))
            self.relays.append([
                self.copies.push(upper, self.relayed[0].at[half], place.at(z=place.z_of(to)[0])),
                self.copies.push(lower, self.relayed[1].at[half], place.at(x=place.x_of(to))),
            ])
            self.sent += self.relays[-1]
        for half, to in ((0, 1), (1, 3)):
            self.onward(half, 1 - half, to)

    def onward(self, slot, half, to):
        place = self.place
        z, zh, zl = place.z_of(to)
        x = place.x_of(to)
        two, one = pl.ds(2 * half, 2), pl.ds(half, 1)
        pair = (
            self.copies.push(
                self.form.upper(self.whole, two, zl, zh), self.landed[0].at[slot, two], place.at(z=z)
            ),
            self.copies.push(
                self.form.lower(self.whole, x, one), self.landed[1].at[slot, one], place.at(x=x)
            ),
        )
        for i in range(2):
            self.arrivals[i].append(pair[i])
        self.sent += pair

    def relay(self, half, upper, lower):
        to = (1, 3)[half]
        _, zh, zl = self.place.z_of(to)
        for i in range(2):
            at = self.form.upper(self.whole, 2 * half + i, zl, zh)
            at[...] = (at[...].astype(F32) + upper[i].astype(F32)).astype(BF16)
        at = self.form.lower(self.whole, self.place.x_of(to), half)
        at[...] = (at[...].astype(F32) + lower[0].astype(F32)).astype(BF16)
        self.onward(half, half, to)

    def own(self, i, load):
        place, whole = self.place, self.whole
        for k in range((4, 2)[i]):
            at = (
                self.form.upper(whole, k, place.zl, place.zh)
                if i == 0
                else self.form.lower(whole, place.x, k)
            )
            total = at[...].astype(F32) + load[0, k].astype(F32) + load[1, k].astype(F32)
            at[...] = total.astype(BF16)
        for d in (1, 3, 2):
            if i == 0:
                x = place.x_of(d)
                part, device = self.form.upper(whole, x, place.zl, place.zh), place.at(x=x)
            else:
                z, zh, zl = place.z_of(d)
                part, device = self.form.lower(whole, place.x, zl, zh), place.at(z=z)
            self.done[i].append(self.copies.push(part, self.last[i].at[d - 1], device))
        self.sent += self.done[i]

    def end(self, i, load):
        place = self.place
        if i == 0:
            at = self.form.upper(self.whole, place.x, place.zl, place.zh)
        else:
            at = self.form.lower(self.whole, place.x, place.zl, place.zh)
        total = at[...].astype(F32)
        for d in range(3):
            total += load[d].astype(F32)
        self.put(i, total)


class Buffers:
    def __init__(self, theirs, up_relayed, low_relayed, up_landed, low_landed, up_last, low_last):
        self.theirs, self.relayed = theirs, (up_relayed, low_relayed)
        self.landed, self.last = (up_landed, low_landed), (up_last, low_last)
        self.users = {}


def both_ways(copies, place, src, dst):
    return [copies.push(src, dst, place.at(y=place.y_of(d))) for d in (1, 3)]


class Rows:
    def __init__(self, copies, place, whole):
        self.copies, self.place, self.whole = copies, place, whole
        self.sent, self.passed, self.parts = {}, {}, [0, 1, 2, 3]

    def send(self, k, src=None):
        mine = self.whole.at[self.place.y, self.parts[k]]
        self.sent[k] = both_ways(self.copies, self.place, mine if src is None else src, mine)

    def pass_on(self, k):
        side, onto = (3, 1) if k < 2 else (1, 3)
        place = self.place
        block = self.whole.at[place.y_of(side), self.parts[k]]
        self.passed[k] = self.copies.push(block, block, place.at(y=place.y_of(onto)))

    def plan(self, tasks, before):
        self.passes = [
            tasks.add(
                [before[k]],
                lambda k=k: self.pass_on(k),
                lambda k=k: recv([self.sent[k][0 if k < 2 else 1]]),
            )
            for k in range(4)
        ]
        self.have = tasks.add(
            self.passes,
            needs=lambda: recv(
                [self.sent[k][1 if k < 2 else 0] for k in range(4)]
                + [self.passed[k] for k in range(4)]
            ),
        )

    def busy(self):
        return sent([copy for pair in self.sent.values() for copy in pair]) + sent(
            list(self.passed.values())
        )


class Spread(Rows):
    def __init__(self, copies, place, held, whole):
        super().__init__(copies, place, whole)
        self.held = held
        self.parts = [place.m] + [place.quad(j)[1] for j in (1, 2, 3)]

    def quad(self):
        place = self.place
        mine = self.whole.at[place.y, place.m]
        self.own = self.copies.local(self.held.at[place.m], mine)
        self.came = []
        for j in (1, 2, 3):
            device, m = place.quad(j)
            self.came.append(self.copies.push(self.held.at[m], mine, device))

    def plan(self, tasks):
        quad = tasks.add((), self.quad)
        along = [
            tasks.add(
                [quad],
                lambda k=k: self.send(k),
                lambda k=k: recv([self.came[k - 1]]) if k else here([self.own]),
            )
            for k in range(4)
        ]
        super().plan(tasks, along)


class RowSum:
    def __init__(self, copies, place, part, buffers):
        self.copies, self.place, self.part = copies, place, part
        self.relayed, self.stage, self.arrived = buffers
        self.passed = {}

    def sides(self):
        ahead, behind = self.place.y_of(1), self.place.y_of(3)
        return (ahead, behind), (self.place.at(y=ahead), self.place.at(y=behind))

    def send(self):
        place = self.place
        near, onto = self.sides()
        across = place.y_of(2)
        self.first = [
            self.copies.push(self.part.at[across, k], self.relayed.at[k], onto[k // 2])
            for k in (0, 2, 1, 3)
        ]
        self.first = [self.first[i] for i in (0, 2, 1, 3)]
        self.direct = [
            self.copies.push(
                self.part.at[near[1 - k // 2], k], self.arrived.at[1 - k // 2, k], onto[1 - k // 2]
            )
            for k in range(4)
        ]

    def relay(self, k):
        near, onto = self.sides()
        total = self.part[near[k // 2], k].astype(F32) + self.relayed[k].astype(F32)
        self.stage[k] = total.astype(BF16)
        self.passed[k] = self.copies.push(
            self.stage.at[k], self.arrived.at[k // 2, k], onto[k // 2]
        )

    def plan(self, tasks, after, needs=nothing):
        send = tasks.add(after, self.send, needs)
        self.sums = [
            tasks.add([send], lambda k=k: self.relay(k), lambda k=k: recv([self.first[k]]))
            for k in range(4)
        ]

    def came(self, k):
        return recv([self.direct[k], self.passed[k]])

    def total(self, k):
        total = self.part[self.place.y, k].astype(F32)
        return total + self.arrived[0, k].astype(F32) + self.arrived[1, k].astype(F32)

    def busy(self):
        return sent(self.first + self.direct + list(self.passed.values()))


def lift(left, piece, kind, count):
    total = None
    for i in range(TILES):
        weight = piece[i // 2, i % 2, :, kind].reshape(count, 256)
        one = dot(columns(left, pl.ds(256 * i, 256), 256), weight, ((1,), (1,)))
        total = one if total is None else total + one
    return total


def layer_kernel(*refs):
    (held, grad_held, query_block, key_block, value_block, out_block, attn_gain, mlp_gain, unit_block,
     cos_in, sin_in,
     block_out, grad_out, gains_out, qkv_out, tall_out, out_out, first_out, x_out) = refs[:19]
    spaces = refs[19:61]
    rest = refs[61:]
    (rows, first, second, grads, qkv, probs, mixed, act, back, units, part,
     relayed, summed, arrived, down_relayed, down_summed, down_arrived, middle,
     stage, key_grad, value_grad,
     piece_a, piece_b, piece_c, qkv_w, out_w, gains, gain_row, ends,
     vec, vec_y, vec_x, vec_z, vec_c, half_x, half_z, half_c,
     send_sems, recv_sems, here_sems) = rest[:21] + rest[28:]
    place = Place()
    enter(place)
    copies = Copies(send_sems, recv_sems, here_sems)
    tasks = Tasks(copies)
    width = rows.shape[-1]
    buffers = Buffers(*rest[21:28])

    qkv_block = qkv_w.at[place.x, place.zl, 2 * place.c + place.zh]
    for kind, block in enumerate((query_block, key_block, value_block)):
        qkv_block[kind] = block[...].T
    pieces = (piece_a, piece_b, piece_c)
    forms = [Form(place, ROWS[p], FIRST[p]) for p in range(3)]
    head_form, out_form = Form(place, HD, FIRST[3]), Form(place, HD, FIRST[4])
    pair, single = pl.ds(0, 2), pl.ds(2, 1)
    gather_q = Gather(
        copies, place, head_form, qkv_w.at[:, :, :, pair], qkv_block.at[pair], True
    )
    gather_v = Gather(
        copies, place, head_form, qkv_w.at[:, :, :, single], qkv_block.at[single], True
    )
    gather_o = Gather(copies, place, out_form, out_w, out_block)
    gathers = [
        Gather(copies, place, forms[p], pieces[p], unit_block.at[:, pl.ds(128 * p, ROWS[p])])
        for p in range(3)
    ]
    for gather in (gather_q, gather_v, gather_o, *gathers):
        gather.plan(tasks)

    class Gains:
        pass

    gain = Gains()

    gain_block = vec.at[:, pl.ds(0, 256)]

    def begin_gains():
        vec[0:1, 0:256] = attn_gain[...].astype(F32).reshape(1, 256)
        vec[1:2, 0:256] = mlp_gain[...].astype(F32).reshape(1, 256)
        vec[2:8, 0:256] = jnp.zeros((6, 256), F32)
        target = gains.at[place.x, place.zl]
        gain.local = copies.local(gain_block, target)
        gain.first = [copies.push(gain_block, target, place.at(x=place.x_of(d))) for d in (1, 2, 3)]

    def spread_gains():
        column = gains.at[:, place.zl]
        gain.last = copies.push(column, column, place.at(z=2 * place.zh + 1 - place.zl))

    def have_gains():
        for i in range(TILES):
            gain_row[:, 256 * i : 256 * i + 256] = gains[i // 2, i % 2]

    begun = tasks.add((), begin_gains)
    passed = tasks.add([begun], spread_gains, lambda: here([gain.local]) + recv(gain.first))
    have_gain = tasks.add([passed], have_gains, lambda: recv([gain.last]))

    spread_x = Spread(copies, place, held, rows)
    spread_x.plan(tasks)
    spread_dy = Spread(copies, place, grad_held, grads)
    spread_dy.plan(tasks)

    def norm_first():
        def body(i, carry):
            y, j = lax.div(i, 4), lax.rem(i, 4)
            x = rows[y, j].astype(F32)
            first[y, j] = (x * factor_of(x) * gain_row[0:1, :]).astype(BF16)
            return carry

        lax.fori_loop(0, 16, body, 0)
        gain.x_out = copies.local(rows.at[place.y], x_out)
        gain.first_out = copies.local(first, first_out)

    norm1 = tasks.add([spread_x.have, have_gain], norm_first)

    def project(kind):
        both = lift(first, qkv_w, kind, 4 * HD)
        for h in range(4):
            one = both[:, h * HD : (h + 1) * HD]
            if kind < 2:
                one = turn(one, cos_in[...], sin_in[...])
            qkv[:, h * 3 * HD + kind * HD : h * 3 * HD + kind * HD + HD] = one.astype(BF16)

    projects = [
        tasks.add(
            [norm1, (gather_q, gather_v)[kind // 2].have], lambda kind=kind: project(kind)
        )
        for kind in range(3)
    ]

    def attend(i):
        for h in (2 * i, 2 * i + 1):
            for b in range(4):
                size = 128 * (b + 1)
                now = slice(128 * b, size)
                at = [slice(h * 3 * HD + k * HD, h * 3 * HD + k * HD + HD) for k in range(3)]
                scores = dot(qkv[now, at[0]], qkv[0:size, at[1]], ((1,), (1,)))
                allowed = lax.broadcasted_iota(jnp.int32, (128, size), 0) + 128 * b
                allowed = allowed >= lax.broadcasted_iota(jnp.int32, (128, size), 1)
                scores = jnp.where(allowed, scores * HD**-0.5, -jnp.inf)
                weight = jnp.exp(scores - jnp.max(scores, axis=-1, keepdims=True))
                weight = weight * (1.0 / jnp.sum(weight, axis=-1, keepdims=True))
                weight = weight.astype(BF16)
                start = 64 * b * (b + 1)
                probs[h, :, start : start + size] = weight
                blend = dot(weight, qkv[0:size, at[2]], ((1,), (0,)))
                mixed[now, h * HD : (h + 1) * HD] = blend.astype(BF16)

    attends = [tasks.add(projects, lambda i=i: attend(i)) for i in range(2)]

    def output():
        for i in range(TILES):
            weight = out_w[i // 2, i % 2].reshape(4 * HD, 256)
            total = dot(mixed[...], weight, ((1,), (0,)))
            part[:, :, :, tile_cols(i, 256)] = total.astype(BF16).reshape(4, 4, 32, 256)

    outputs = tasks.add([*attends, gather_o.have], output)
    sum_out = RowSum(copies, place, part, (relayed, summed, arrived))
    sum_out.plan(tasks, [outputs])
    rows_a = Rows(copies, place, second)

    def middle_part(k):
        now = pl.ds(32 * k, 32)
        mid = rows[place.y, k].astype(F32) + sum_out.total(k)
        middle[now, :] = mid
        stage[k] = (mid * factor_of(mid) * gain_row[1:2, :]).astype(BF16)
        rows_a.send(k, stage.at[k])
        second[place.y, k] = stage[k]

    mids = [
        tasks.add(
            [sum_out.sums[k], norm1],
            lambda k=k: middle_part(k),
            lambda k=k: sum_out.came(k) + spread_x.busy(),
        )
        for k in range(4)
    ]
    rows_a.plan(tasks, mids)

    def lift_back(p):
        count = 4 * ROWS[p]
        back[:, 512 * p : 512 * p + count] = lift(grads, pieces[p], 2, count).astype(BF16)

    def open_units(p, kind):
        count = 4 * ROWS[p]
        act[kind, :, 0:count] = lift(second, pieces[p], kind, count).astype(BF16)

    def gating(p):
        for j in range(4 * ROWS[p] // 128):
            cols = slice(128 * j, 128 * j + 128)
            opened, lifted = act[0, :, cols].astype(F32), act[1, :, cols].astype(F32)
            change = back[:, 512 * p + 128 * j : 512 * p + 128 * j + 128].astype(F32)
            sig = 1.0 / (1.0 + jnp.exp(-opened))
            silu = opened * sig
            result = (
                (change * lifted * sig * (1.0 + opened * (1.0 - sig))).astype(BF16),
                (change * silu).astype(BF16),
                (silu * lifted).astype(BF16),
            )
            back[:, 512 * p + 128 * j : 512 * p + 128 * j + 128] = result[2]
            for kind in range(3):
                if kind < 2:
                    act[kind, :, cols] = result[kind]
                turned, at = result[kind].T, 0
                while at < 128:
                    c, row = divmod(128 * j + at, 2 * ROWS[p])
                    size = min(128 - at, 2 * ROWS[p] - row)
                    units[p % 2, c, kind, row : row + size, :] = turned[at : at + size]
                    at += size

    def sum_up(target, p, kinds):
        count = 4 * ROWS[p]

        for i in range(TILES):
            cols = tile_cols(i, 256)
            total = None
            for kind in kinds:
                weight = pieces[p][i // 2, i % 2, :, kind].reshape(count, 256)
                left = act[kind, :, 0:count] if kind < 2 else back[:, 512 * p : 512 * p + count]
                one = dot(left, weight, ((1,), (0,)))
                total = one if total is None else total + one
            if p:
                total += columns(target, cols, 256).astype(F32)
            target[:, :, :, cols] = total.astype(BF16).reshape(4, 4, 32, 256)

    def of_units(count, turned, middle_rows, right):
        def tile(x, target, c):
            cols = tile_cols(x, 512)
            pair = dot(
                turned[c, 0:2, 0 : 2 * count].reshape(4 * count, 512),
                columns(middle_rows, cols, 512),
                ((1,), (0,)),
            ).astype(BF16)
            one = dot(turned[c, 2, 0 : 2 * count], columns(right, cols, 512), ((1,), (0,)))
            one = one.astype(BF16)
            for zl in range(2):
                at = slice(256 * zl, 256 * zl + 256)
                for zh in range(2):
                    block = target.at[x, zl, 2 * c + zh]
                    for kind in range(2):
                        start = (2 * kind + zh) * count
                        block[kind] = pair[start : start + count, at]
                    block[2] = one[zh * count : (zh + 1) * count, at]

        return tile

    def of_pair(x, target, c):
        cols = tile_cols(x, 512)
        both = dot(
            units[1, c, 0:2].reshape(4 * HD, 512), columns(second, cols, 512), ((1,), (0,))
        ).astype(BF16)
        for zl in range(2):
            for zh in range(2):
                for kind in range(2):
                    start = (2 * kind + zh) * HD
                    target[x, zl, 2 * c + zh, kind] = both[
                        start : start + HD, 256 * zl : 256 * zl + 256
                    ]

    def of_values(x, target, c):
        cols = tile_cols(x, 512)
        one = dot(units[1, c, 2], columns(second, cols, 512), ((1,), (0,))).astype(BF16)
        for zl in range(2):
            for zh in range(2):
                target[x, zl, 2 * c + zh, 0] = one[
                    zh * HD : (zh + 1) * HD, 256 * zl : 256 * zl + 256
                ]

    slots = [None, None]

    def put_units(p):
        def put(i, total):
            if slots[i] is not None:
                slots[i].wait()
            start, size = FIRST[p] * i, (FIRST[p], ROWS[p] - FIRST[p])[i]
            ends[i, :, 0:size, :] = total
            slots[i] = copies.local(
                ends.at[i, :, pl.ds(0, size)], tall_out.at[:, pl.ds(128 * p + start, size)]
            )

        return put

    def put_heads(first_kind):
        def put(i, total):
            for kind in range(total.shape[0]):
                cols = slice(FIRST[3] * i, (FIRST[3], HD)[i])
                qkv_out[first_kind + kind, :, cols] = total[kind].T

        return put

    def put_out(i, total):
        out_out[FIRST[4] * i : (FIRST[4], HD)[i], :] = total[0]

    reduces = [
        Reduce(copies, place, form, whole, spaces[7 * i : 7 * i + 7], buffers, put)
        for i, (form, whole, put) in enumerate((
            (forms[0], piece_a, put_units(0)),
            (forms[1], piece_b, put_units(1)),
            (forms[2], piece_c, put_units(2)),
            (head_form, piece_a.at[:, :, :, pair], put_heads(0)),
            (head_form, piece_a.at[:, :, :, single], put_heads(2)),
            (out_form, out_w, put_out),
        ))
    ]
    earlier, filled, all_down = [], [], []
    for p in range(3):
        have = gathers[p].have
        lifted = tasks.add([spread_dy.have, have], lambda p=p: lift_back(p))
        opened = [
            tasks.add([rows_a.have, have] + earlier, lambda p=p, kind=kind: open_units(p, kind))
            for kind in range(2)
        ]
        gated = tasks.add([lifted] + opened + filled[: max(0, p - 1)], lambda p=p: gating(p))
        da2 = tasks.add(
            [gated] + mids,
            lambda p=p: sum_up(part, p, (0, 1)),
            sum_out.busy if p == 0 else nothing,
        )
        downed = tasks.add(
            [gated] + projects + all_down[-1:],
            lambda p=p: sum_up(first, p, (2,)),
            (lambda: here([gain.first_out])) if p == 0 else nothing,
        )
        earlier = [da2]
        all_down.append(downed)
        reduces[p].plan(tasks, of_units(ROWS[p], units.at[p % 2], second, grads), [da2, downed], gathers[p].busy)
        filled = filled + [reduces[p].filled]

    sum_mid = RowSum(copies, place, part, (relayed, summed, arrived))
    sum_mid.plan(tasks, [da2])
    rows_m = Rows(copies, place, rows)
    gain.mlp = jnp.zeros((1, width), F32)

    def mid_back(k):
        now = pl.ds(32 * k, 32)
        result, gain_part = norm_back(sum_mid.total(k), middle[now, :], gain_row[1:2, :])
        gain.mlp += gain_part
        result += grads[place.y, k].astype(F32)
        stage[k] = result.astype(BF16)
        rows_m.send(k, stage.at[k])
        rows[place.y, k] = stage[k]

    dmids = []
    for k in range(4):
        dmids += [tasks.add(
            [sum_mid.sums[k], rows_a.passes[k]] + dmids[:1],
            lambda k=k: mid_back(k),
            lambda k=k: sum_mid.came(k) + sent(rows_a.sent[k]) + (here([gain.x_out]) if k == 0 else []),
        )]
    rows_m.plan(tasks, dmids)
    sum_down = RowSum(copies, place, first, (down_relayed, down_summed, down_arrived))
    sum_down.plan(tasks, all_down)

    out_stage = down_relayed

    def out_part(k):
        now = pl.ds(32 * k, 32)
        out_stage[k] = (middle[now, :] + sum_down.total(k)).astype(BF16)

    def to_quad(source, target, state):
        state.append(copies.local(source.at[place.m], target.at[place.m]))
        for j in (1, 2, 3):
            device, m = place.quad(j)
            state.append(copies.push(source.at[m], target.at[place.m], device))

    out_state, in_state = [], []
    outs = [
        tasks.add([sum_down.sums[k]], lambda k=k: out_part(k), lambda k=k: sum_down.came(k))
        for k in range(4)
    ]
    gone = tasks.add(outs, lambda: to_quad(out_stage, block_out, out_state))
    tasks.add([gone], needs=lambda: here(out_state[:1]) + recv(out_state[1:]))

    def unmix():
        act[0] = sum(
            dot(
                columns(rows, pl.ds(256 * i, 256), 256),
                out_w[i // 2, i % 2].reshape(4 * HD, 256),
                ((1,), (1,)),
            )
            for i in range(TILES)
        ).astype(BF16)

    unmixed = tasks.add([rows_m.have, *earlier], unmix)

    def of_mixed(x, target, c):
        left = mixed[:, pl.ds(pl.multiple_of(2 * c * HD, 128), 2 * HD)].T
        one = dot(left, columns(rows, tile_cols(x, 512), 512), ((1,), (0,))).astype(BF16)
        for zl in range(2):
            for zh in range(2):
                target[x, zl, 2 * c + zh, 0] = one[
                    zh * HD : (zh + 1) * HD, 256 * zl : 256 * zl + 256
                ]

    reduces[5].plan(tasks, of_mixed, [unmixed], gather_o.busy)

    def values_back(i):
        for h in (2 * i, 2 * i + 1):
            at = slice(h * 3 * HD + 2 * HD, h * 3 * HD + 3 * HD)
            value_grad[...] = jnp.zeros(value_grad.shape, F32)
            for b in range(4):
                size = 128 * (b + 1)
                start = 64 * b * (b + 1)
                weight = probs[h, :, start : start + size]
                mix = act[0, 128 * b : size, h * HD : (h + 1) * HD]
                value_grad[0:size, :] += dot(weight, mix, ((0,), (0,)))
            back[:, at] = value_grad[...].astype(BF16)
            start = h % 2 * HD
            units[1, h // 2, 2, start : start + HD, :] = back[:, at].T

    def attend_back(i):
        for h in (2 * i, 2 * i + 1):
            at = [slice(h * 3 * HD + k * HD, h * 3 * HD + k * HD + HD) for k in range(3)]
            key_grad[...] = jnp.zeros(key_grad.shape, F32)
            for b in range(4):
                size = 128 * (b + 1)
                now, so_far = slice(128 * b, size), slice(0, size)
                start = 64 * b * (b + 1)
                weight = probs[h, :, start : start + size]
                mix = act[0, now, h * HD : (h + 1) * HD]
                change = dot(mix, qkv[so_far, at[2]], ((1,), (1,)))
                weight = weight.astype(F32)
                change = weight * (change - jnp.sum(weight * change, axis=-1, keepdims=True))
                change = change.astype(BF16)
                query = dot(change, qkv[so_far, at[1]], ((1,), (0,))) * HD**-0.5
                query = turn_back(query, cos_in[now, :], sin_in[now, :])
                back[now, at[0]] = query.astype(BF16)
                key_grad[so_far, :] += dot(change, qkv[now, at[0]], ((0,), (0,)))
            key = turn_back(key_grad[...] * HD**-0.5, cos_in[...], sin_in[...])
            back[:, at[1]] = key.astype(BF16)
            start = h % 2 * HD
            for kind in range(2):
                units[1, h // 2, kind, start : start + HD, :] = back[:, at[kind]].T

    before = [unmixed, gated] + filled + all_down
    vbacks = [tasks.add(before, lambda i=i: values_back(i)) for i in range(2)]
    abacks = [tasks.add(before, lambda i=i: attend_back(i)) for i in range(2)]

    def first_back():
        for i in range(TILES):
            weight = qkv_w[i // 2, i % 2].reshape(12 * HD, 256)
            total = dot(back[...], weight, ((1,), (0,)))
            grads[:, :, :, tile_cols(i, 256)] = total.astype(BF16).reshape(4, 4, 32, 256)

    da1 = tasks.add([*abacks, *vbacks, *filled, *dmids], first_back, spread_dy.busy)
    sum_first = RowSum(copies, place, grads, (relayed, summed, arrived))
    sum_first.plan(tasks, [da1] + rows_m.passes, sum_mid.busy)

    def reload():
        gain.first_in = copies.local(first_out, second)

    reloaded = tasks.add(filled, reload, rows_a.busy)
    place_free = tasks.add(
        [reloaded, *reduces[0].ended],
        needs=lambda: here([gain.first_in]) + reduces[0].busy(),
    )
    reduces[4].plan(tasks, of_values, [*vbacks, place_free], nothing)
    reduces[3].plan(tasks, of_pair, [*abacks, place_free], nothing)

    gain.attn = jnp.zeros((1, width), F32)

    def in_part(k):
        now = pl.ds(32 * k, 32)
        result, gain_part = norm_back(
            sum_first.total(k), stage[k].astype(F32), gain_row[0:1, :]
        )
        gain.attn += gain_part
        stage[k] = (rows[place.y, k].astype(F32) + result).astype(BF16)

    def load_x():
        gain.x_in = copies.local(x_out, stage)

    def sent_m():
        return sent([copy for pair in rows_m.sent.values() for copy in pair])

    got_x = tasks.add([*dmids, *rows_m.passes], load_x, sent_m)
    have_x = tasks.add([got_x], needs=lambda: here([gain.x_in]))
    ins = [
        tasks.add(
            [sum_first.sums[k], have_x], lambda k=k: in_part(k), lambda k=k: sum_first.came(k)
        )
        for k in range(4)
    ]
    gone = tasks.add(ins, lambda: to_quad(stage, grad_out, in_state))
    tasks.add([gone], needs=lambda: here(in_state[:1]) + recv(in_state[1:]))

    def gain_y():
        vec[0:1, :] = gain.attn
        vec[1:2, :] = gain.mlp
        vec[2:8, :] = jnp.zeros((6, width), F32)
        gain.y = [copies.push(vec, vec_y.at[d - 1], place.at(y=place.y_of(d))) for d in (1, 3, 2)]

    def of_x(x):
        return pl.ds(pl.multiple_of(x * 512, 128), 512)

    def of_z(zl):
        return pl.ds(pl.multiple_of(zl * 256, 128), 256)

    def gain_x():
        half_x[...] = vec[...] + vec_y[0] + vec_y[1] + vec_y[2]
        gain.x = []
        for d in (1, 3, 2):
            x = place.x_of(d)
            gain.x.append(copies.push(half_x.at[:, of_x(x)], vec_x.at[d - 1], place.at(x=x)))

    def gain_z():
        half_z[...] = half_x[:, of_x(place.x)] + vec_x[0] + vec_x[1] + vec_x[2]
        gain.z = []
        for d in (1, 3, 2):
            z, zh, zl = place.z_of(d)
            gain.z.append(copies.push(half_z.at[:, of_z(zl)], vec_z.at[d - 1], place.at(z=z)))

    def gain_c():
        half_c[...] = half_z[:, of_z(place.zl)] + vec_z[0] + vec_z[1] + vec_z[2]
        gain.c = copies.push(half_c, vec_c, place.sibling())

    def gain_end():
        gains_out[...] = half_c[...] + vec_c[...]

    over_y = tasks.add(ins + dmids, gain_y, lambda: sent(gain.first))
    over_x = tasks.add([over_y], gain_x, lambda: recv(gain.y))
    over_z = tasks.add([over_x], gain_z, lambda: recv(gain.x))
    over_c = tasks.add([over_z], gain_c, lambda: recv(gain.z))
    tasks.add([over_c], gain_end, lambda: recv([gain.c]))

    drive(tasks, ORDER)
    for copy in slots:
        copy.wait()
    copies.drain()


def tables(length):
    half_size = HD // 2
    inverse_freq = np.float32(THETA) ** (-(np.arange(half_size, dtype=np.float32) * 2.0) / HD)
    angles = np.arange(length, dtype=np.float32)[:, None] * inverse_freq.astype(np.float32)[None]
    cos_t, sin_t = np.cos(angles), np.sin(angles)
    return (
        jnp.asarray(np.concatenate([cos_t, cos_t], axis=1), F32),
        jnp.asarray(np.concatenate([-sin_t, sin_t], axis=1), F32),
    )


def local(
    hidden_in,
    cotangent,
    gain_attn,
    w_query,
    w_key,
    w_value,
    w_output,
    gain_mlp,
    w_gate,
    w_up,
    w_down,
):
    held, grad_held = hidden_in[:, 0], cotangent[:, 0]
    width = held.shape[2]
    length = 512
    count = w_gate.shape[1]
    unit_block = jnp.pad(
        jnp.stack([w_gate.T, w_up.T, w_down]), ((0, 0), (0, UNITS - count), (0, 0))
    )
    cos_t, sin_t = tables(length)
    blocks = ((4, 4, 32, width), BF16)
    heads = ((length, 12 * HD), BF16)
    square = ((length, length), BF16)
    own_f32 = ((128, width), F32)
    parts = ((4, 32, width), BF16)
    sums = [parts, parts, ((2, 4, 32, width), BF16)]

    def spaces(kinds, size, first):
        up, low = (kinds, first, 256), (kinds, size - first, 256)
        return [
            ((4, 2, 2, kinds, size, 256), BF16),
            ((2, 2, *up), BF16),
            ((2, 1, 2, *low), BF16),
            ((2, 4, *up), BF16),
            ((2, 2, 2, *low), BF16),
            ((3, *up), BF16),
            ((3, *low), BF16),
        ]

    def whole(kinds, size):
        return ((4, 2, 4, kinds, size, 256), BF16)

    landing = []
    for i, size in enumerate((*ROWS, HD, HD, HD)):
        kinds = (3, 3, 3, 2, 1, 1)[i]
        landing += spaces(kinds, size, FIRST[min(i, 4) if i < 4 else i - 1])
    outs = [
        parts, parts, ((8, 256), F32), ((3, 256, HD), F32), ((3, UNITS, 256), F32),
        ((HD, 256), F32), blocks, parts,
    ]
    up, low = max(FIRST), HD - min(FIRST[0], FIRST[1], FIRST[3])
    buffers = [
        ((2, 2, 2, 3, HD, 256), BF16),
        ((2, 2, 3, up, 256), BF16), ((2, 1, 2, 3, low, 256), BF16),
        ((2, 4, 3, up, 256), BF16), ((2, 2, 2, 3, low, 256), BF16),
        ((3, 3, up, 256), BF16), ((3, 3, low, 256), BF16),
    ]
    scratch = [
        blocks, blocks, blocks, blocks, heads, ((4, 128, 1280), BF16), square,
        ((2, length, length), BF16), heads, ((2, 2, 3, 256, length), BF16), blocks,
        *sums, *sums, own_f32, parts,
        ((length, HD), F32), ((length, HD), F32), *buffers,
        whole(3, ROWS[0]), whole(3, ROWS[1]), whole(3, ROWS[2]), whole(3, HD), whole(1, HD),
        ((4, 2, 8, 256), F32), ((8, width), F32), ((2, 3, max(up, low), 256), F32),
        ((8, width), F32), ((3, 8, width), F32), ((3, 8, 512), F32), ((3, 8, 256), F32),
        ((8, 256), F32), ((8, width), F32), ((8, 512), F32), ((8, 256), F32),
    ]
    block_out, grad_in, gains_out, qkv_g, tall_g, out_g = pl.pallas_call(
        layer_kernel,
        out_shape=[jax.ShapeDtypeStruct(shape, dtype) for shape, dtype in outs + landing],
        in_specs=[ANY] * 2 + [VMEM] * 3 + [ANY] + [VMEM] * 2 + [ANY] + [VMEM] * 2,
        out_specs=[ANY, ANY, VMEM, VMEM, ANY, VMEM, ANY, ANY] + [ANY] * len(landing),
        scratch_shapes=[
            *[pltpu.VMEM(shape, dtype) for shape, dtype in scratch],
            pltpu.SemaphoreType.DMA((COPIES,)),
            pltpu.SemaphoreType.DMA((COPIES,)),
            pltpu.SemaphoreType.DMA((LOCALS,)),
        ],
        compiler_params=pltpu.CompilerParams(
            collective_id=0, has_side_effects=True, vmem_limit_bytes=VMEM_LIMIT
        ),
    )(held, grad_held, w_query, w_key, w_value, w_output[None], gain_attn, gain_mlp, unit_block, cos_t, sin_t)[:6]
    return (
        block_out[:, None],
        grad_in[:, None],
        gains_out[0],
        qkv_g[0],
        qkv_g[1],
        qkv_g[2],
        out_g,
        gains_out[1],
        tall_g[0, :count].T,
        tall_g[1, :count].T,
        tall_g[2, :count],
    )


def solution(mesh):
    rows = P(None, "fsdp", "tensor", None)
    into, out_of = P("fsdp", "tensor"), P("tensor", "fsdp")
    return jax.shard_map(
        local,
        mesh=mesh,
        in_specs=(
            rows, rows, P("fsdp"), into, into, into, out_of, P("fsdp"), into, into, out_of,
        ),
        out_specs=(
            rows, rows, P("fsdp"), into, into, into, out_of, P("fsdp"), into, into, out_of,
        ),
        check_vma=False,
    )
```

```python
import jax
import jax.numpy as jnp
import numpy as np
from jax import lax
from jax.experimental import pallas as pl
from jax.experimental.pallas import tpu as pltpu
from jax.sharding import PartitionSpec as P


HD = 128
UNITS = 352
ROWS = (128, 128, 96)
FIRST = (64, 64, 48, 64, 64)
EPSILON = 1e-05
THETA = 10000.0
MESH = pl.DeviceIdType.MESH
F32 = jnp.float32
BF16 = jnp.bfloat16
COPIES = 400
LOCALS = 130
TILES = 8
ALL = slice(None)
RECV, SENT, HERE = range(3)
ANY = pl.BlockSpec(memory_space=pl.ANY)
VMEM = pl.BlockSpec(memory_space=pltpu.VMEM)
VMEM_LIMIT = 62 * 2**20

ORDER = (
    57, 59, 58, 9, 60, 0, 67, 18, 68, 54, 69, 1, 61, 71, 70, 10, 13, 64, 19, 22, 63, 4, 3, 65, 2,
    5, 62, 12, 15, 6, 74, 55, 21, 11, 20, 36, 23, 45, 75, 73, 24, 27, 72, 7, 56, 66, 77, 14, 16, 8,
    79, 78, 25, 17, 80, 82, 81, 26, 83, 84, 46, 28, 86, 48, 88, 31, 85, 47, 51, 87, 50, 90, 49, 30,
    92, 29, 52, 76, 91, 37, 89, 32, 33, 96, 34, 94, 53, 95, 40, 93, 35, 98, 39, 42, 38, 156, 41,
    97, 100, 99, 101, 103, 43, 102, 104, 44, 105, 127, 128, 129, 130, 131, 157, 158, 159, 160, 185,
    106, 108, 132, 133, 109, 107, 110, 112, 113, 111, 114, 186, 134, 188, 135, 161, 187, 189, 117,
    115, 136, 137, 118, 116, 138, 162, 139, 190, 140, 141, 142, 143, 192, 164, 193, 119, 191, 163,
    244, 123, 166, 167, 124, 144, 196, 194, 146, 145, 147, 197, 165, 195, 168, 170, 292, 120, 169,
    199, 152, 125, 171, 172, 126, 153, 198, 210, 211, 236, 212, 235, 213, 215, 203, 121, 173, 202,
    200, 175, 237, 214, 122, 217, 245, 174, 216, 219, 176, 234, 201, 220, 246, 218, 221, 238, 239,
    148, 207, 204, 206, 205, 208, 222, 247, 149, 181, 248, 269, 250, 177, 270, 251, 224, 249, 252,
    223, 225, 178, 254, 253, 182, 271, 272, 241, 255, 273, 154, 256, 240, 243, 242, 274, 150, 275,
    277, 155, 278, 226, 276, 279, 183, 184, 293, 257, 259, 295, 297, 258, 230, 227, 260, 231, 294,
    296, 282, 300, 280, 281, 283, 298, 301, 151, 179, 265, 261, 262, 284, 232, 266, 288, 285, 209,
    180, 228, 302, 289, 229, 263, 303, 233, 267, 264, 286, 287, 304, 299, 268, 290, 291,
)


class Place:
    def __init__(self):
        f = lax.axis_index("fsdp")
        t = lax.axis_index("tensor")
        self.x, self.zl = lax.div(f, 2), lax.rem(f, 2)
        self.y, self.m = lax.div(t, 4), lax.rem(t, 4)
        self.zh, self.c = lax.div(self.m, 2), lax.rem(self.m, 2)
        self.z = 2 * self.zh + self.zl

    def at(self, x=None, z=None, y=None, c=None):
        x = self.x if x is None else x
        z = self.z if z is None else z
        y = self.y if y is None else y
        c = self.c if c is None else c
        return (2 * x + lax.rem(z, 2), 4 * y + 2 * lax.div(z, 2) + c)

    def x_of(self, d):
        return lax.rem(self.x + d, 4)

    def y_of(self, d):
        return lax.rem(self.y + d, 4)

    def z_of(self, d):
        z = lax.rem(self.z + d, 4)
        return z, lax.div(z, 2), lax.rem(z, 2)

    def quad(self, j):
        zh = 1 - self.zh if j & 2 else self.zh
        c = 1 - self.c if j & 1 else self.c
        return self.at(z=2 * zh + self.zl, c=c), 2 * zh + c

    def sibling(self):
        return self.at(c=1 - self.c)


class Copies:
    def __init__(self, send, recv, here):
        self.send, self.recv, self.here = send, recv, here
        self.sent, self.waited, self.kept = [], [], 0

    def push(self, src, dst, device):
        k = len(self.sent)
        assert k < COPIES
        copy = pltpu.make_async_remote_copy(
            src_ref=src,
            dst_ref=dst,
            send_sem=self.send.at[k],
            recv_sem=self.recv.at[k],
            device_id=device,
            device_id_type=MESH,
        )
        copy.start()
        self.sent.append(copy)
        return copy

    def local(self, src, dst):
        assert self.kept < LOCALS
        copy = pltpu.make_async_copy(src, dst, self.here.at[self.kept])
        copy.start()
        self.kept += 1
        return copy

    def wait(self, copy, kind):
        if kind == RECV:
            copy.wait_recv()
        elif kind == HERE:
            copy.wait()
        elif not any(copy is other for other in self.waited):
            copy.wait_send()
            self.waited.append(copy)

    def drain(self):
        for copy in self.sent:
            self.wait(copy, SENT)


def recv(copies):
    return [(copy, RECV) for copy in copies]


def sent(copies):
    return [(copy, SENT) for copy in copies]


def here(copies):
    return [(copy, HERE) for copy in copies]


def nothing():
    return ()


class Tasks:
    def __init__(self, copies):
        self.copies, self.all = copies, []

    def add(self, after, run=nothing, needs=nothing):
        self.all.append((list(after), needs, run))
        return len(self.all) - 1


def drive(tasks, order):
    done = set()
    for number in order:
        after, needs, run = tasks.all[number]
        assert done.issuperset(after), number
        for copy, kind in needs():
            tasks.copies.wait(copy, kind)
        run()
        done.add(number)
    assert len(done) == len(tasks.all)


def enter(place):
    barrier = pltpu.get_barrier_semaphore()
    others = [place.at(y=place.y_of(d)) for d in (1, 2, 3)]
    others += [place.at(x=place.x_of(d)) for d in (1, 2, 3)]
    others += [place.at(z=place.z_of(d)[0]) for d in (1, 2, 3)]
    others += [place.quad(1)[0], place.quad(3)[0]]
    for other in others:
        pl.semaphore_signal(barrier, inc=1, device_id=other, device_id_type=MESH)
    pl.semaphore_wait(barrier, len(others))


def dot(left, right, dims):
    return lax.dot_general(left, right, (dims, ((), ())), preferred_element_type=F32)


def turn(rows, cos_t, sin_t):
    return rows * cos_t + pltpu.roll(rows, HD // 2, 1) * sin_t


def turn_back(rows, cos_t, sin_t):
    return rows * cos_t - pltpu.roll(rows, HD // 2, 1) * sin_t


def head_cols(h, part):
    return pl.ds(pl.multiple_of(h * 3 * HD + part * HD, HD), HD)


def tile_cols(i, size):
    return pl.ds(pl.multiple_of(i * size, size), size)


def columns(rows, cols, size):
    return rows[:, :, :, cols].reshape(512, size)


def factor_of(rows):
    return lax.rsqrt(jnp.mean(rows * rows, axis=-1, keepdims=True) + EPSILON)


def norm_back(grad, rows, gain):
    factor = factor_of(rows)
    scaled = grad * gain
    back = factor * scaled - rows * factor**3 * jnp.mean(scaled * rows, axis=-1, keepdims=True)
    return back, jnp.sum(grad * rows * factor, axis=0, keepdims=True)


def fit(ref, shape):
    index = tuple(
        ALL if have == want else pl.ds(0, want) for have, want in zip(ref.shape, shape, strict=True)
    )
    return ref.at[index]


class Form:
    def __init__(self, place, rows, first):
        self.place = place
        self.up, self.low = pl.ds(0, first), pl.ds(first, rows - first)

    def upper(self, ref, x, zl, zh):
        return ref.at[x, zl, 2 * self.place.c + zh, :, self.up]

    def lower(self, ref, x, zl, zh=None):
        block = pl.ds(2 * self.place.c, 2) if zh is None else 2 * self.place.c + zh
        return ref.at[x, zl, block, :, self.low]

    def core(self, ref, x, c):
        return ref.at[x, :, pl.ds(2 * c, 2)]


class Gather:
    def __init__(self, copies, place, form, whole, block, placed=False):
        self.copies, self.place, self.whole, self.block = copies, place, whole, block
        self.form, self.placed = form, placed

    def plan(self, tasks):
        self.passed, self.shared = [], []
        begin = tasks.add((), self.begin)
        spread = tasks.add([begin], self.spread, lambda: here(self.local) + recv(self.first))
        ahead = tasks.add([spread], lambda: self.relay(0), lambda: recv(self.ahead))
        behind = tasks.add([spread], lambda: self.relay(1), lambda: recv(self.behind))
        near = [tasks.add([spread], lambda: self.to_sibling(0))]
        near.append(tasks.add([ahead], lambda: self.to_sibling(3)))
        near.append(tasks.add([behind], lambda: self.to_sibling(1)))
        far = tasks.add(
            [ahead, behind, *near], lambda: self.to_sibling(2), lambda: recv(self.passed)
        )
        self.have = tasks.add([far], needs=lambda: recv(self.shared))

    def busy(self):
        return sent(self.ahead + self.behind + self.passed + self.shared)

    def begin(self):
        place, block, form = self.place, self.block, self.form
        self.local = []
        if not self.placed:
            target = self.whole.at[place.x, place.zl, 2 * place.c + place.zh]
            self.local.append(self.copies.local(block, target))
        upper, lower = block.at[:, form.up], block.at[:, form.low]
        to_upper = form.upper(self.whole, place.x, place.zl, place.zh)
        to_lower = form.lower(self.whole, place.x, place.zl, place.zh)
        self.first = []
        for d in (1, 3, 2):
            self.first.append(self.copies.push(upper, to_upper, place.at(x=place.x_of(d))))
            self.first.append(self.copies.push(lower, to_lower, place.at(z=place.z_of(d)[0])))

    def both(self, upper, lower, to):
        place = self.place
        return [
            self.copies.push(upper, upper, place.at(z=place.z_of(to)[0])),
            self.copies.push(lower, lower, place.at(x=place.x_of(to))),
        ]

    def spread(self):
        place = self.place
        upper = self.form.upper(self.whole, ALL, place.zl, place.zh)
        lower = self.form.lower(self.whole, place.x, ALL)
        self.ahead = self.both(upper, lower, 1)
        self.behind = self.both(upper, lower, 3)

    def relay(self, half):
        side, onto = ((3, 1), (1, 3))[half]
        _, zh, zl = self.place.z_of(side)
        upper = self.form.upper(self.whole, pl.ds(2 * half, 2), zl, zh)
        lower = self.form.lower(self.whole, self.place.x_of(side), pl.ds(half, 1))
        self.passed += self.both(upper, lower, onto)

    def to_sibling(self, d):
        place, form = self.place, self.form
        _, zh, zl = place.z_of(d)
        for part in (
            form.upper(self.whole, ALL, zl, zh),
            form.lower(self.whole, place.x_of(d), ALL),
        ):
            self.shared.append(self.copies.push(part, part, place.sibling()))


class Reduce:
    def __init__(self, copies, place, form, whole, spaces, buffers, put):
        self.copies, self.place, self.whole, self.put = copies, place, whole, put
        self.form, self.buffers = form, buffers
        (self.theirs, up_relayed, low_relayed, up_landed, low_landed, up_last, low_last) = spaces
        self.relayed, self.landed = (up_relayed, low_relayed), (up_landed, low_landed)
        self.last = (up_last, low_last)
        self.swapped, self.relays, self.sent = [], [], []
        self.arrivals, self.done, self.loads = ([], []), ([], []), {}

    def fetched(self, tasks, buffer, after, use, fetch, needs):
        loads = []

        def load():
            loads.extend(self.copies.local(src, dst) for src, dst in fetch())

        first = tasks.add(list(after) + self.buffers.users.get(buffer, []), load, needs)
        last = tasks.add([first], use, lambda: here(loads))
        self.buffers.users[buffer] = [last]
        return last

    def plan(self, tasks, tile, after, needs):
        buffers = self.buffers
        fills = [tasks.add(after, lambda: self.fill(tile, 0), needs)]
        fills.append(tasks.add(fills, lambda: self.fill(tile, 1)))
        self.filled = fills[1]
        adds = []
        for x in range(4):
            slot = fit(buffers.theirs.at[x % 2], self.theirs.shape[1:])
            adds.append(
                self.fetched(
                    tasks,
                    (0, x % 2),
                    [fills[x // 2]],
                    lambda x=x, slot=slot: self.add(x, slot),
                    lambda x=x, slot=slot: [(self.theirs.at[x], slot)],
                    (lambda x=x: recv(self.swapped[x // 2 : x // 2 + 1])) if x % 2 == 0 else nothing,
                )
            )
            if x % 2:
                tasks.all[adds[x] - 1][0].append(adds[x - 1] - 1)
        push = tasks.add(adds, self.push)
        relays = []
        for i in range(2):
            upper = fit(buffers.relayed[0].at[i], self.relayed[0].shape[1:])
            lower = fit(buffers.relayed[1].at[i], self.relayed[1].shape[1:])
            relays.append(
                self.fetched(
                    tasks,
                    (1, i),
                    [push],
                    lambda i=i, upper=upper, lower=lower: self.relay(i, upper, lower),
                    lambda i=i, upper=upper, lower=lower: [
                        (self.relayed[0].at[i], upper),
                        (self.relayed[1].at[i], lower),
                    ],
                    lambda i=i: recv(self.relays[i]),
                )
            )
        self.ended = []
        for i in range(2):
            slot = fit(buffers.landed[i], self.landed[i].shape)
            own = self.fetched(
                tasks,
                (2, i),
                relays,
                lambda i=i, slot=slot: self.own(i, slot),
                lambda i=i, slot=slot: [(self.landed[i], slot)],
                lambda i=i: recv(self.arrivals[i]),
            )
            slot = fit(buffers.last[i], self.last[i].shape)
            self.ended.append(
                self.fetched(
                    tasks,
                    (3, i),
                    [own],
                    lambda i=i, slot=slot: self.end(i, slot),
                    lambda i=i, slot=slot: [(self.last[i], slot)],
                    lambda i=i: recv(self.done[i]),
                )
            )

    def busy(self):
        return sent(self.sent)

    def fill(self, tile, part):
        place = self.place

        for x in (2 * part, 2 * part + 1):
            tile(x, self.whole, 1 - place.c)
            tile(x, self.whole, place.c)
        block = pl.ds(2 * part, 2)
        self.swapped.append(
            self.copies.push(
                self.form.core(self.whole, block, 1 - place.c),
                self.theirs.at[block],
                place.sibling(),
            )
        )
        self.sent.append(self.swapped[-1])

    def add(self, x, load):
        def body(zl, carry):
            to = self.whole.at[x, zl, pl.ds(2 * self.place.c, 2)]
            to[...] = (to[...].astype(F32) + load[zl].astype(F32)).astype(BF16)
            return carry

        lax.fori_loop(0, 2, body, 0)

    def push(self):
        place, whole = self.place, self.whole
        _, zh, zl = place.z_of(2)
        x = place.x_of(2)
        for half, to in ((0, 1), (1, 3)):
            upper = self.form.upper(whole, pl.ds(2 * half, 2), zl, zh)
            lower = self.form.lower(whole, x, pl.ds(half, 1))
            self.relays.append([
                self.copies.push(upper, self.relayed[0].at[half], place.at(z=place.z_of(to)[0])),
                self.copies.push(lower, self.relayed[1].at[half], place.at(x=place.x_of(to))),
            ])
            self.sent += self.relays[-1]
        for half, to in ((0, 1), (1, 3)):
            self.onward(half, 1 - half, to)

    def onward(self, slot, half, to):
        place = self.place
        z, zh, zl = place.z_of(to)
        x = place.x_of(to)
        two, one = pl.ds(2 * half, 2), pl.ds(half, 1)
        pair = (
            self.copies.push(
                self.form.upper(self.whole, two, zl, zh), self.landed[0].at[slot, two], place.at(z=z)
            ),
            self.copies.push(
                self.form.lower(self.whole, x, one), self.landed[1].at[slot, one], place.at(x=x)
            ),
        )
        for i in range(2):
            self.arrivals[i].append(pair[i])
        self.sent += pair

    def relay(self, half, upper, lower):
        to = (1, 3)[half]
        _, zh, zl = self.place.z_of(to)
        for i in range(2):
            at = self.form.upper(self.whole, 2 * half + i, zl, zh)
            at[...] = (at[...].astype(F32) + upper[i].astype(F32)).astype(BF16)
        at = self.form.lower(self.whole, self.place.x_of(to), half)
        at[...] = (at[...].astype(F32) + lower[0].astype(F32)).astype(BF16)
        self.onward(half, half, to)

    def own(self, i, load):
        place, whole = self.place, self.whole
        for k in range((4, 2)[i]):
            at = (
                self.form.upper(whole, k, place.zl, place.zh)
                if i == 0
                else self.form.lower(whole, place.x, k)
            )
            total = at[...].astype(F32) + load[0, k].astype(F32) + load[1, k].astype(F32)
            at[...] = total.astype(BF16)
        for d in (1, 3, 2):
            if i == 0:
                x = place.x_of(d)
                part, device = self.form.upper(whole, x, place.zl, place.zh), place.at(x=x)
            else:
                z, zh, zl = place.z_of(d)
                part, device = self.form.lower(whole, place.x, zl, zh), place.at(z=z)
            self.done[i].append(self.copies.push(part, self.last[i].at[d - 1], device))
        self.sent += self.done[i]

    def end(self, i, load):
        place = self.place
        if i == 0:
            at = self.form.upper(self.whole, place.x, place.zl, place.zh)
        else:
            at = self.form.lower(self.whole, place.x, place.zl, place.zh)
        total = at[...].astype(F32)
        for d in range(3):
            total += load[d].astype(F32)
        self.put(i, total)


class Buffers:
    def __init__(self, theirs, up_relayed, low_relayed, up_landed, low_landed, up_last, low_last):
        self.theirs, self.relayed = theirs, (up_relayed, low_relayed)
        self.landed, self.last = (up_landed, low_landed), (up_last, low_last)
        self.users = {}


def both_ways(copies, place, src, dst):
    return [copies.push(src, dst, place.at(y=place.y_of(d))) for d in (1, 3)]


class Rows:
    def __init__(self, copies, place, whole):
        self.copies, self.place, self.whole = copies, place, whole
        self.sent, self.passed, self.parts = {}, {}, [0, 1, 2, 3]

    def send(self, k, src=None):
        mine = self.whole.at[self.place.y, self.parts[k]]
        self.sent[k] = both_ways(self.copies, self.place, mine if src is None else src, mine)

    def pass_on(self, k):
        side, onto = (3, 1) if k < 2 else (1, 3)
        place = self.place
        block = self.whole.at[place.y_of(side), self.parts[k]]
        self.passed[k] = self.copies.push(block, block, place.at(y=place.y_of(onto)))

    def plan(self, tasks, before):
        self.passes = [
            tasks.add(
                [before[k]],
                lambda k=k: self.pass_on(k),
                lambda k=k: recv([self.sent[k][0 if k < 2 else 1]]),
            )
            for k in range(4)
        ]
        self.have = tasks.add(
            self.passes,
            needs=lambda: recv(
                [self.sent[k][1 if k < 2 else 0] for k in range(4)]
                + [self.passed[k] for k in range(4)]
            ),
        )

    def busy(self):
        return sent([copy for pair in self.sent.values() for copy in pair]) + sent(
            list(self.passed.values())
        )


class Spread(Rows):
    def __init__(self, copies, place, held, whole):
        super().__init__(copies, place, whole)
        self.held = held
        self.parts = [place.m] + [place.quad(j)[1] for j in (1, 2, 3)]

    def quad(self):
        place = self.place
        mine = self.whole.at[place.y, place.m]
        self.own = self.copies.local(self.held.at[place.m], mine)
        self.came = []
        for j in (1, 2, 3):
            device, m = place.quad(j)
            self.came.append(self.copies.push(self.held.at[m], mine, device))

    def plan(self, tasks):
        quad = tasks.add((), self.quad)
        along = [
            tasks.add(
                [quad],
                lambda k=k: self.send(k),
                lambda k=k: recv([self.came[k - 1]]) if k else here([self.own]),
            )
            for k in range(4)
        ]
        super().plan(tasks, along)


class RowSum:
    def __init__(self, copies, place, part, buffers):
        self.copies, self.place, self.part = copies, place, part
        self.relayed, self.stage, self.arrived = buffers
        self.passed = {}

    def sides(self):
        ahead, behind = self.place.y_of(1), self.place.y_of(3)
        return (ahead, behind), (self.place.at(y=ahead), self.place.at(y=behind))

    def send(self):
        place = self.place
        near, onto = self.sides()
        across = place.y_of(2)
        self.first = [
            self.copies.push(self.part.at[across, k], self.relayed.at[k], onto[k // 2])
            for k in (0, 2, 1, 3)
        ]
        self.first = [self.first[i] for i in (0, 2, 1, 3)]
        self.direct = [
            self.copies.push(
                self.part.at[near[1 - k // 2], k], self.arrived.at[1 - k // 2, k], onto[1 - k // 2]
            )
            for k in range(4)
        ]

    def relay(self, k):
        near, onto = self.sides()
        total = self.part[near[k // 2], k].astype(F32) + self.relayed[k].astype(F32)
        self.stage[k] = total.astype(BF16)
        self.passed[k] = self.copies.push(
            self.stage.at[k], self.arrived.at[k // 2, k], onto[k // 2]
        )

    def plan(self, tasks, after, needs=nothing):
        send = tasks.add(after, self.send, needs)
        self.sums = [
            tasks.add([send], lambda k=k: self.relay(k), lambda k=k: recv([self.first[k]]))
            for k in range(4)
        ]

    def came(self, k):
        return recv([self.direct[k], self.passed[k]])

    def total(self, k):
        total = self.part[self.place.y, k].astype(F32)
        return total + self.arrived[0, k].astype(F32) + self.arrived[1, k].astype(F32)

    def busy(self):
        return sent(self.first + self.direct + list(self.passed.values()))


def lift(left, piece, kind, count):
    total = None
    for i in range(TILES):
        weight = piece[i // 2, i % 2, :, kind].reshape(count, 256)
        one = dot(columns(left, pl.ds(256 * i, 256), 256), weight, ((1,), (1,)))
        total = one if total is None else total + one
    return total


def layer_kernel(*refs):
    (held, grad_held, query_block, key_block, value_block, out_block, attn_gain, mlp_gain, unit_block,
     cos_in, sin_in,
     block_out, grad_out, gains_out, qkv_out, tall_out, out_out, first_out, x_out) = refs[:19]
    spaces = refs[19:61]
    rest = refs[61:]
    (rows, first, second, grads, qkv, probs, mixed, act, back, units, part,
     relayed, summed, arrived, down_relayed, down_summed, down_arrived, middle,
     stage, key_grad, value_grad,
     piece_a, piece_b, piece_c, qkv_w, out_w, gains, gain_row, ends,
     vec, vec_y, vec_x, vec_z, vec_c, half_x, half_z, half_c,
     send_sems, recv_sems, here_sems) = rest[:21] + rest[28:]
    place = Place()
    enter(place)
    copies = Copies(send_sems, recv_sems, here_sems)
    tasks = Tasks(copies)
    width = rows.shape[-1]
    buffers = Buffers(*rest[21:28])

    qkv_block = qkv_w.at[place.x, place.zl, 2 * place.c + place.zh]
    for kind, block in enumerate((query_block, key_block, value_block)):
        qkv_block[kind] = block[...].T
    pieces = (piece_a, piece_b, piece_c)
    forms = [Form(place, ROWS[p], FIRST[p]) for p in range(3)]
    head_form, out_form = Form(place, HD, FIRST[3]), Form(place, HD, FIRST[4])
    pair, single = pl.ds(0, 2), pl.ds(2, 1)
    gather_q = Gather(
        copies, place, head_form, qkv_w.at[:, :, :, pair], qkv_block.at[pair], True
    )
    gather_v = Gather(
        copies, place, head_form, qkv_w.at[:, :, :, single], qkv_block.at[single], True
    )
    gather_o = Gather(copies, place, out_form, out_w, out_block)
    gathers = [
        Gather(copies, place, forms[p], pieces[p], unit_block.at[:, pl.ds(128 * p, ROWS[p])])
        for p in range(3)
    ]
    for gather in (gather_q, gather_v, gather_o, *gathers):
        gather.plan(tasks)

    class Gains:
        pass

    gain = Gains()

    gain_block = vec.at[:, pl.ds(0, 256)]

    def begin_gains():
        vec[0:1, 0:256] = attn_gain[...].astype(F32).reshape(1, 256)
        vec[1:2, 0:256] = mlp_gain[...].astype(F32).reshape(1, 256)
        vec[2:8, 0:256] = jnp.zeros((6, 256), F32)
        target = gains.at[place.x, place.zl]
        gain.local = copies.local(gain_block, target)
        gain.first = [copies.push(gain_block, target, place.at(x=place.x_of(d))) for d in (1, 2, 3)]

    def spread_gains():
        column = gains.at[:, place.zl]
        gain.last = copies.push(column, column, place.at(z=2 * place.zh + 1 - place.zl))

    def have_gains():
        for i in range(TILES):
            gain_row[:, 256 * i : 256 * i + 256] = gains[i // 2, i % 2]

    begun = tasks.add((), begin_gains)
    passed = tasks.add([begun], spread_gains, lambda: here([gain.local]) + recv(gain.first))
    have_gain = tasks.add([passed], have_gains, lambda: recv([gain.last]))

    spread_x = Spread(copies, place, held, rows)
    spread_x.plan(tasks)
    spread_dy = Spread(copies, place, grad_held, grads)
    spread_dy.plan(tasks)

    def norm_first():
        def body(i, carry):
            y, j = lax.div(i, 4), lax.rem(i, 4)
            x = rows[y, j].astype(F32)
            first[y, j] = (x * factor_of(x) * gain_row[0:1, :]).astype(BF16)
            return carry

        lax.fori_loop(0, 16, body, 0)
        gain.x_out = copies.local(rows.at[place.y], x_out)
        gain.first_out = copies.local(first, first_out)

    norm1 = tasks.add([spread_x.have, have_gain], norm_first)

    def project(kind):
        both = lift(first, qkv_w, kind, 4 * HD)
        for h in range(4):
            one = both[:, h * HD : (h + 1) * HD]
            if kind < 2:
                one = turn(one, cos_in[...], sin_in[...])
            qkv[:, h * 3 * HD + kind * HD : h * 3 * HD + kind * HD + HD] = one.astype(BF16)

    projects = [
        tasks.add(
            [norm1, (gather_q, gather_v)[kind // 2].have], lambda kind=kind: project(kind)
        )
        for kind in range(3)
    ]

    def attend(i):
        for h in (2 * i, 2 * i + 1):
            for b in range(4):
                size = 128 * (b + 1)
                now = slice(128 * b, size)
                at = [slice(h * 3 * HD + k * HD, h * 3 * HD + k * HD + HD) for k in range(3)]
                scores = dot(qkv[now, at[0]], qkv[0:size, at[1]], ((1,), (1,)))
                allowed = lax.broadcasted_iota(jnp.int32, (128, size), 0) + 128 * b
                allowed = allowed >= lax.broadcasted_iota(jnp.int32, (128, size), 1)
                scores = jnp.where(allowed, scores * HD**-0.5, -jnp.inf)
                weight = jnp.exp(scores - jnp.max(scores, axis=-1, keepdims=True))
                weight = weight * (1.0 / jnp.sum(weight, axis=-1, keepdims=True))
                weight = weight.astype(BF16)
                start = 64 * b * (b + 1)
                probs[h, :, start : start + size] = weight
                blend = dot(weight, qkv[0:size, at[2]], ((1,), (0,)))
                mixed[now, h * HD : (h + 1) * HD] = blend.astype(BF16)

    attends = [tasks.add(projects, lambda i=i: attend(i)) for i in range(2)]

    def output():
        for i in range(TILES):
            weight = out_w[i // 2, i % 2].reshape(4 * HD, 256)
            total = dot(mixed[...], weight, ((1,), (0,)))
            part[:, :, :, tile_cols(i, 256)] = total.astype(BF16).reshape(4, 4, 32, 256)

    outputs = tasks.add([*attends, gather_o.have], output)
    sum_out = RowSum(copies, place, part, (relayed, summed, arrived))
    sum_out.plan(tasks, [outputs])
    rows_a = Rows(copies, place, second)

    def middle_part(k):
        now = pl.ds(32 * k, 32)
        mid = rows[place.y, k].astype(F32) + sum_out.total(k)
        middle[now, :] = mid
        stage[k] = (mid * factor_of(mid) * gain_row[1:2, :]).astype(BF16)
        rows_a.send(k, stage.at[k])
        second[place.y, k] = stage[k]

    mids = [
        tasks.add(
            [sum_out.sums[k], norm1],
            lambda k=k: middle_part(k),
            lambda k=k: sum_out.came(k) + spread_x.busy(),
        )
        for k in range(4)
    ]
    rows_a.plan(tasks, mids)

    def lift_back(p):
        count = 4 * ROWS[p]
        back[:, 512 * p : 512 * p + count] = lift(grads, pieces[p], 2, count).astype(BF16)

    def open_units(p, kind):
        count = 4 * ROWS[p]
        act[kind, :, 0:count] = lift(second, pieces[p], kind, count).astype(BF16)

    def gating(p):
        for j in range(4 * ROWS[p] // 128):
            cols = slice(128 * j, 128 * j + 128)
            opened, lifted = act[0, :, cols].astype(F32), act[1, :, cols].astype(F32)
            change = back[:, 512 * p + 128 * j : 512 * p + 128 * j + 128].astype(F32)
            sig = 1.0 / (1.0 + jnp.exp(-opened))
            silu = opened * sig
            result = (
                (change * lifted * sig * (1.0 + opened * (1.0 - sig))).astype(BF16),
                (change * silu).astype(BF16),
                (silu * lifted).astype(BF16),
            )
            back[:, 512 * p + 128 * j : 512 * p + 128 * j + 128] = result[2]
            for kind in range(3):
                if kind < 2:
                    act[kind, :, cols] = result[kind]
                turned, at = result[kind].T, 0
                while at < 128:
                    c, row = divmod(128 * j + at, 2 * ROWS[p])
                    size = min(128 - at, 2 * ROWS[p] - row)
                    units[p % 2, c, kind, row : row + size, :] = turned[at : at + size]
                    at += size

    def sum_up(target, p, kinds):
        count = 4 * ROWS[p]

        for i in range(TILES):
            cols = tile_cols(i, 256)
            total = None
            for kind in kinds:
                weight = pieces[p][i // 2, i % 2, :, kind].reshape(count, 256)
                left = act[kind, :, 0:count] if kind < 2 else back[:, 512 * p : 512 * p + count]
                one = dot(left, weight, ((1,), (0,)))
                total = one if total is None else total + one
            if p:
                total += columns(target, cols, 256).astype(F32)
            target[:, :, :, cols] = total.astype(BF16).reshape(4, 4, 32, 256)

    def of_units(count, turned, middle_rows, right):
        def tile(x, target, c):
            cols = tile_cols(x, 512)
            pair = dot(
                turned[c, 0:2, 0 : 2 * count].reshape(4 * count, 512),
                columns(middle_rows, cols, 512),
                ((1,), (0,)),
            ).astype(BF16)
            one = dot(turned[c, 2, 0 : 2 * count], columns(right, cols, 512), ((1,), (0,)))
            one = one.astype(BF16)
            for zl in range(2):
                at = slice(256 * zl, 256 * zl + 256)
                for zh in range(2):
                    block = target.at[x, zl, 2 * c + zh]
                    for kind in range(2):
                        start = (2 * kind + zh) * count
                        block[kind] = pair[start : start + count, at]
                    block[2] = one[zh * count : (zh + 1) * count, at]

        return tile

    def of_pair(x, target, c):
        cols = tile_cols(x, 512)
        both = dot(
            units[1, c, 0:2].reshape(4 * HD, 512), columns(second, cols, 512), ((1,), (0,))
        ).astype(BF16)
        for zl in range(2):
            for zh in range(2):
                for kind in range(2):
                    start = (2 * kind + zh) * HD
                    target[x, zl, 2 * c + zh, kind] = both[
                        start : start + HD, 256 * zl : 256 * zl + 256
                    ]

    def of_values(x, target, c):
        cols = tile_cols(x, 512)
        one = dot(units[1, c, 2], columns(second, cols, 512), ((1,), (0,))).astype(BF16)
        for zl in range(2):
            for zh in range(2):
                target[x, zl, 2 * c + zh, 0] = one[
                    zh * HD : (zh + 1) * HD, 256 * zl : 256 * zl + 256
                ]

    slots = [None, None]

    def put_units(p):
        def put(i, total):
            if slots[i] is not None:
                slots[i].wait()
            start, size = FIRST[p] * i, (FIRST[p], ROWS[p] - FIRST[p])[i]
            ends[i, :, 0:size, :] = total
            slots[i] = copies.local(
                ends.at[i, :, pl.ds(0, size)], tall_out.at[:, pl.ds(128 * p + start, size)]
            )

        return put

    def put_heads(first_kind):
        def put(i, total):
            for kind in range(total.shape[0]):
                cols = slice(FIRST[3] * i, (FIRST[3], HD)[i])
                qkv_out[first_kind + kind, :, cols] = total[kind].T

        return put

    def put_out(i, total):
        out_out[FIRST[4] * i : (FIRST[4], HD)[i], :] = total[0]

    reduces = [
        Reduce(copies, place, form, whole, spaces[7 * i : 7 * i + 7], buffers, put)
        for i, (form, whole, put) in enumerate((
            (forms[0], piece_a, put_units(0)),
            (forms[1], piece_b, put_units(1)),
            (forms[2], piece_c, put_units(2)),
            (head_form, piece_a.at[:, :, :, pair], put_heads(0)),
            (head_form, piece_a.at[:, :, :, single], put_heads(2)),
            (out_form, out_w, put_out),
        ))
    ]
    earlier, filled, all_down = [], [], []
    for p in range(3):
        have = gathers[p].have
        lifted = tasks.add([spread_dy.have, have], lambda p=p: lift_back(p))
        opened = [
            tasks.add([rows_a.have, have] + earlier, lambda p=p, kind=kind: open_units(p, kind))
            for kind in range(2)
        ]
        gated = tasks.add([lifted] + opened + filled[: max(0, p - 1)], lambda p=p: gating(p))
        da2 = tasks.add(
            [gated] + mids,
            lambda p=p: sum_up(part, p, (0, 1)),
            sum_out.busy if p == 0 else nothing,
        )
        downed = tasks.add(
            [gated] + projects + all_down[-1:],
            lambda p=p: sum_up(first, p, (2,)),
            (lambda: here([gain.first_out])) if p == 0 else nothing,
        )
        earlier = [da2]
        all_down.append(downed)
        reduces[p].plan(tasks, of_units(ROWS[p], units.at[p % 2], second, grads), [da2, downed], gathers[p].busy)
        filled = filled + [reduces[p].filled]

    sum_mid = RowSum(copies, place, part, (relayed, summed, arrived))
    sum_mid.plan(tasks, [da2])
    rows_m = Rows(copies, place, rows)
    gain.mlp = jnp.zeros((1, width), F32)

    def mid_back(k):
        now = pl.ds(32 * k, 32)
        result, gain_part = norm_back(sum_mid.total(k), middle[now, :], gain_row[1:2, :])
        gain.mlp += gain_part
        result += grads[place.y, k].astype(F32)
        stage[k] = result.astype(BF16)
        rows_m.send(k, stage.at[k])
        rows[place.y, k] = stage[k]

    dmids = []
    for k in range(4):
        dmids += [tasks.add(
            [sum_mid.sums[k], rows_a.passes[k]] + dmids[:1],
            lambda k=k: mid_back(k),
            lambda k=k: sum_mid.came(k) + sent(rows_a.sent[k]) + (here([gain.x_out]) if k == 0 else []),
        )]
    rows_m.plan(tasks, dmids)
    sum_down = RowSum(copies, place, first, (down_relayed, down_summed, down_arrived))
    sum_down.plan(tasks, all_down)

    out_stage = down_relayed

    def out_part(k):
        now = pl.ds(32 * k, 32)
        out_stage[k] = (middle[now, :] + sum_down.total(k)).astype(BF16)

    def to_quad(source, target, state):
        state.append(copies.local(source.at[place.m], target.at[place.m]))
        for j in (1, 2, 3):
            device, m = place.quad(j)
            state.append(copies.push(source.at[m], target.at[place.m], device))

    out_state, in_state = [], []
    outs = [
        tasks.add([sum_down.sums[k]], lambda k=k: out_part(k), lambda k=k: sum_down.came(k))
        for k in range(4)
    ]
    gone = tasks.add(outs, lambda: to_quad(out_stage, block_out, out_state))
    tasks.add([gone], needs=lambda: here(out_state[:1]) + recv(out_state[1:]))

    def unmix():
        act[0] = sum(
            dot(
                columns(rows, pl.ds(256 * i, 256), 256),
                out_w[i // 2, i % 2].reshape(4 * HD, 256),
                ((1,), (1,)),
            )
            for i in range(TILES)
        ).astype(BF16)

    unmixed = tasks.add([rows_m.have, *earlier], unmix)

    def of_mixed(x, target, c):
        left = mixed[:, pl.ds(pl.multiple_of(2 * c * HD, 128), 2 * HD)].T
        one = dot(left, columns(rows, tile_cols(x, 512), 512), ((1,), (0,))).astype(BF16)
        for zl in range(2):
            for zh in range(2):
                target[x, zl, 2 * c + zh, 0] = one[
                    zh * HD : (zh + 1) * HD, 256 * zl : 256 * zl + 256
                ]

    reduces[5].plan(tasks, of_mixed, [unmixed], gather_o.busy)

    def values_back(i):
        for h in (2 * i, 2 * i + 1):
            at = slice(h * 3 * HD + 2 * HD, h * 3 * HD + 3 * HD)
            value_grad[...] = jnp.zeros(value_grad.shape, F32)
            for b in range(4):
                size = 128 * (b + 1)
                start = 64 * b * (b + 1)
                weight = probs[h, :, start : start + size]
                mix = act[0, 128 * b : size, h * HD : (h + 1) * HD]
                value_grad[0:size, :] += dot(weight, mix, ((0,), (0,)))
            back[:, at] = value_grad[...].astype(BF16)
            start = h % 2 * HD
            units[1, h // 2, 2, start : start + HD, :] = back[:, at].T

    def attend_back(i):
        for h in (2 * i, 2 * i + 1):
            at = [slice(h * 3 * HD + k * HD, h * 3 * HD + k * HD + HD) for k in range(3)]
            key_grad[...] = jnp.zeros(key_grad.shape, F32)
            for b in range(4):
                size = 128 * (b + 1)
                now, so_far = slice(128 * b, size), slice(0, size)
                start = 64 * b * (b + 1)
                weight = probs[h, :, start : start + size]
                mix = act[0, now, h * HD : (h + 1) * HD]
                change = dot(mix, qkv[so_far, at[2]], ((1,), (1,)))
                weight = weight.astype(F32)
                change = weight * (change - jnp.sum(weight * change, axis=-1, keepdims=True))
                change = change.astype(BF16)
                query = dot(change, qkv[so_far, at[1]], ((1,), (0,))) * HD**-0.5
                query = turn_back(query, cos_in[now, :], sin_in[now, :])
                back[now, at[0]] = query.astype(BF16)
                key_grad[so_far, :] += dot(change, qkv[now, at[0]], ((0,), (0,)))
            key = turn_back(key_grad[...] * HD**-0.5, cos_in[...], sin_in[...])
            back[:, at[1]] = key.astype(BF16)
            start = h % 2 * HD
            for kind in range(2):
                units[1, h // 2, kind, start : start + HD, :] = back[:, at[kind]].T

    before = [unmixed, gated] + filled + all_down
    vbacks = [tasks.add(before, lambda i=i: values_back(i)) for i in range(2)]
    abacks = [tasks.add(before, lambda i=i: attend_back(i)) for i in range(2)]

    def first_back():
        for i in range(TILES):
            weight = qkv_w[i // 2, i % 2].reshape(12 * HD, 256)
            total = dot(back[...], weight, ((1,), (0,)))
            grads[:, :, :, tile_cols(i, 256)] = total.astype(BF16).reshape(4, 4, 32, 256)

    da1 = tasks.add([*abacks, *vbacks, *filled, *dmids], first_back, spread_dy.busy)
    sum_first = RowSum(copies, place, grads, (relayed, summed, arrived))
    sum_first.plan(tasks, [da1] + rows_m.passes, sum_mid.busy)

    def reload():
        gain.first_in = copies.local(first_out, second)

    reloaded = tasks.add(filled, reload, rows_a.busy)
    place_free = tasks.add(
        [reloaded, *reduces[0].ended],
        needs=lambda: here([gain.first_in]) + reduces[0].busy(),
    )
    reduces[4].plan(tasks, of_values, [*vbacks, place_free], nothing)
    reduces[3].plan(tasks, of_pair, [*abacks, place_free], nothing)

    gain.attn = jnp.zeros((1, width), F32)

    def in_part(k):
        now = pl.ds(32 * k, 32)
        result, gain_part = norm_back(
            sum_first.total(k), stage[k].astype(F32), gain_row[0:1, :]
        )
        gain.attn += gain_part
        stage[k] = (rows[place.y, k].astype(F32) + result).astype(BF16)

    def load_x():
        gain.x_in = copies.local(x_out, stage)

    def sent_m():
        return sent([copy for pair in rows_m.sent.values() for copy in pair])

    got_x = tasks.add([*dmids, *rows_m.passes], load_x, sent_m)
    have_x = tasks.add([got_x], needs=lambda: here([gain.x_in]))
    ins = [
        tasks.add(
            [sum_first.sums[k], have_x], lambda k=k: in_part(k), lambda k=k: sum_first.came(k)
        )
        for k in range(4)
    ]
    gone = tasks.add(ins, lambda: to_quad(stage, grad_out, in_state))
    tasks.add([gone], needs=lambda: here(in_state[:1]) + recv(in_state[1:]))

    def gain_y():
        vec[0:1, :] = gain.attn
        vec[1:2, :] = gain.mlp
        vec[2:8, :] = jnp.zeros((6, width), F32)
        gain.y = [copies.push(vec, vec_y.at[d - 1], place.at(y=place.y_of(d))) for d in (1, 3, 2)]

    def of_x(x):
        return pl.ds(pl.multiple_of(x * 512, 128), 512)

    def of_z(zl):
        return pl.ds(pl.multiple_of(zl * 256, 128), 256)

    def gain_x():
        half_x[...] = vec[...] + vec_y[0] + vec_y[1] + vec_y[2]
        gain.x = []
        for d in (1, 3, 2):
            x = place.x_of(d)
            gain.x.append(copies.push(half_x.at[:, of_x(x)], vec_x.at[d - 1], place.at(x=x)))

    def gain_z():
        half_z[...] = half_x[:, of_x(place.x)] + vec_x[0] + vec_x[1] + vec_x[2]
        gain.z = []
        for d in (1, 3, 2):
            z, zh, zl = place.z_of(d)
            gain.z.append(copies.push(half_z.at[:, of_z(zl)], vec_z.at[d - 1], place.at(z=z)))

    def gain_c():
        half_c[...] = half_z[:, of_z(place.zl)] + vec_z[0] + vec_z[1] + vec_z[2]
        gain.c = copies.push(half_c, vec_c, place.sibling())

    def gain_end():
        gains_out[...] = half_c[...] + vec_c[...]

    over_y = tasks.add(ins + dmids, gain_y, lambda: sent(gain.first))
    over_x = tasks.add([over_y], gain_x, lambda: recv(gain.y))
    over_z = tasks.add([over_x], gain_z, lambda: recv(gain.x))
    over_c = tasks.add([over_z], gain_c, lambda: recv(gain.z))
    tasks.add([over_c], gain_end, lambda: recv([gain.c]))

    drive(tasks, ORDER)
    for copy in slots:
        copy.wait()
    copies.drain()


def deliver_kernel(rows_in, rows_back, heads, tall, out, *refs):
    count = refs[5].shape[0]
    refs[0][...], refs[1][...], refs[8][...] = rows_in[...], rows_back[...], out[...]
    for kind in range(3):
        refs[2 + kind][...] = heads[kind]
        refs[5 + kind][...] = tall[kind, 0:count, :]


def tables(length):
    half_size = HD // 2
    inverse_freq = np.float32(THETA) ** (-(np.arange(half_size, dtype=np.float32) * 2.0) / HD)
    angles = np.arange(length, dtype=np.float32)[:, None] * inverse_freq.astype(np.float32)[None]
    cos_t, sin_t = np.cos(angles), np.sin(angles)
    return (
        jnp.asarray(np.concatenate([cos_t, cos_t], axis=1), F32),
        jnp.asarray(np.concatenate([-sin_t, sin_t], axis=1), F32),
    )


def local(
    hidden_in,
    cotangent,
    gain_attn,
    w_query,
    w_key,
    w_value,
    w_output,
    gain_mlp,
    w_gate,
    w_up,
    w_down,
):
    held, grad_held = hidden_in[:, 0], cotangent[:, 0]
    width = held.shape[2]
    length = 512
    count = w_gate.shape[1]
    unit_block = jnp.pad(
        jnp.stack([w_gate.T, w_up.T, w_down]), ((0, 0), (0, UNITS - count), (0, 0))
    )
    cos_t, sin_t = tables(length)
    blocks = ((4, 4, 32, width), BF16)
    heads = ((length, 12 * HD), BF16)
    square = ((length, length), BF16)
    own_f32 = ((128, width), F32)
    parts = ((4, 32, width), BF16)
    sums = [parts, parts, ((2, 4, 32, width), BF16)]

    def spaces(kinds, size, first):
        up, low = (kinds, first, 256), (kinds, size - first, 256)
        return [
            ((4, 2, 2, kinds, size, 256), BF16),
            ((2, 2, *up), BF16),
            ((2, 1, 2, *low), BF16),
            ((2, 4, *up), BF16),
            ((2, 2, 2, *low), BF16),
            ((3, *up), BF16),
            ((3, *low), BF16),
        ]

    def whole(kinds, size):
        return ((4, 2, 4, kinds, size, 256), BF16)

    landing = []
    for i, size in enumerate((*ROWS, HD, HD, HD)):
        kinds = (3, 3, 3, 2, 1, 1)[i]
        landing += spaces(kinds, size, FIRST[min(i, 4) if i < 4 else i - 1])
    outs = [
        parts, parts, ((8, 256), F32), ((3, 256, HD), F32), ((3, UNITS, 256), F32),
        ((HD, 256), F32), blocks, parts,
    ]
    up, low = max(FIRST), HD - min(FIRST[0], FIRST[1], FIRST[3])
    buffers = [
        ((2, 2, 2, 3, HD, 256), BF16),
        ((2, 2, 3, up, 256), BF16), ((2, 1, 2, 3, low, 256), BF16),
        ((2, 4, 3, up, 256), BF16), ((2, 2, 2, 3, low, 256), BF16),
        ((3, 3, up, 256), BF16), ((3, 3, low, 256), BF16),
    ]
    scratch = [
        blocks, blocks, blocks, blocks, heads, ((4, 128, 1280), BF16), square,
        ((2, length, length), BF16), heads, ((2, 2, 3, 256, length), BF16), blocks,
        *sums, *sums, own_f32, parts,
        ((length, HD), F32), ((length, HD), F32), *buffers,
        whole(3, ROWS[0]), whole(3, ROWS[1]), whole(3, ROWS[2]), whole(3, HD), whole(1, HD),
        ((4, 2, 8, 256), F32), ((8, width), F32), ((2, 3, max(up, low), 256), F32),
        ((8, width), F32), ((3, 8, width), F32), ((3, 8, 512), F32), ((3, 8, 256), F32),
        ((8, 256), F32), ((8, width), F32), ((8, 512), F32), ((8, 256), F32),
    ]
    block_out, grad_in, gains_out, qkv_g, tall_g, out_g = pl.pallas_call(
        layer_kernel,
        out_shape=[jax.ShapeDtypeStruct(shape, dtype) for shape, dtype in outs + landing],
        in_specs=[ANY] * 2 + [VMEM] * 3 + [ANY] + [VMEM] * 2 + [ANY] + [VMEM] * 2,
        out_specs=[ANY, ANY, VMEM, VMEM, ANY, VMEM, ANY, ANY] + [ANY] * len(landing),
        scratch_shapes=[
            *[pltpu.VMEM(shape, dtype) for shape, dtype in scratch],
            pltpu.SemaphoreType.DMA((COPIES,)),
            pltpu.SemaphoreType.DMA((COPIES,)),
            pltpu.SemaphoreType.DMA((LOCALS,)),
        ],
        compiler_params=pltpu.CompilerParams(
            collective_id=0, has_side_effects=True, vmem_limit_bytes=VMEM_LIMIT
        ),
    )(held, grad_held, w_query, w_key, w_value, w_output[None], gain_attn, gain_mlp, unit_block, cos_t, sin_t)[:6]
    final = [block_out.shape, grad_in.shape] + [qkv_g.shape[1:]] * 3
    final += [(count, tall_g.shape[2])] * 3 + [out_g.shape]
    results = pl.pallas_call(
        deliver_kernel,
        out_shape=[
            jax.ShapeDtypeStruct(shape, BF16 if i < 2 else F32) for i, shape in enumerate(final)
        ],
        in_specs=[VMEM] * 5,
        out_specs=[VMEM] * 9,
    )(block_out, grad_in, qkv_g, tall_g, out_g)
    block_out, grad_in, query_g, key_g, value_g, gate_g, up_g, down_g, out_g = results
    return (
        block_out[:, None],
        grad_in[:, None],
        gains_out[0],
        query_g,
        key_g,
        value_g,
        out_g,
        gains_out[1],
        gate_g.T,
        up_g.T,
        down_g,
    )


def solution(mesh):
    rows = P(None, "fsdp", "tensor", None)
    into, out_of = P("fsdp", "tensor"), P("tensor", "fsdp")
    return jax.shard_map(
        local,
        mesh=mesh,
        in_specs=(
            rows, rows, P("fsdp"), into, into, into, out_of, P("fsdp"), into, into, out_of,
        ),
        out_specs=(
            rows, rows, P("fsdp"), into, into, into, out_of, P("fsdp"), into, into, out_of,
        ),
        check_vma=False,
    )
```

```python
import jax
import jax.numpy as jnp
import numpy as np
from jax import lax
from jax.experimental import pallas as pl
from jax.experimental.pallas import tpu as pltpu
from jax.sharding import PartitionSpec as P


HD = 128
UNITS = 352
ROWS = (128, 128, 96)
FIRST = (64, 64, 48, 64, 64)
EPSILON = 1e-05
THETA = 10000.0
MESH = pl.DeviceIdType.MESH
F32 = jnp.float32
BF16 = jnp.bfloat16
COPIES = 400
LOCALS = 130
TILES = 8
ALL = slice(None)
RECV, SENT, HERE = range(3)
ANY = pl.BlockSpec(memory_space=pl.ANY)
VMEM = pl.BlockSpec(memory_space=pltpu.VMEM)
VMEM_LIMIT = 62 * 2**20

ORDER = (
    57, 59, 58, 9, 60, 0, 67, 18, 68, 54, 69, 1, 61, 71, 70, 10, 13, 64, 19, 22, 63, 4, 3, 65, 2,
    5, 62, 12, 15, 6, 74, 55, 21, 11, 20, 36, 23, 45, 75, 73, 24, 27, 72, 7, 56, 66, 77, 14, 16, 8,
    79, 78, 25, 17, 80, 82, 81, 26, 83, 84, 46, 28, 86, 48, 88, 31, 85, 47, 51, 87, 50, 90, 49, 30,
    92, 29, 52, 76, 91, 37, 89, 32, 33, 96, 34, 94, 53, 95, 40, 93, 35, 98, 39, 42, 38, 156, 41,
    97, 100, 99, 101, 103, 43, 102, 104, 44, 105, 127, 128, 129, 130, 131, 157, 158, 159, 160, 185,
    106, 108, 132, 133, 109, 107, 110, 112, 113, 111, 114, 186, 134, 188, 135, 161, 187, 189, 117,
    115, 136, 137, 118, 116, 138, 162, 139, 190, 140, 141, 142, 143, 192, 164, 193, 119, 191, 163,
    244, 123, 166, 167, 124, 144, 196, 194, 146, 145, 147, 197, 165, 195, 168, 170, 292, 120, 169,
    199, 152, 125, 171, 172, 126, 153, 198, 210, 211, 236, 212, 235, 213, 215, 203, 121, 173, 202,
    200, 175, 237, 214, 122, 217, 245, 174, 216, 219, 176, 234, 201, 220, 246, 218, 221, 238, 239,
    148, 207, 204, 206, 205, 208, 222, 247, 149, 181, 248, 269, 250, 177, 270, 251, 224, 249, 252,
    223, 225, 178, 254, 253, 182, 271, 272, 241, 255, 273, 154, 256, 240, 243, 242, 274, 150, 275,
    277, 155, 278, 226, 276, 279, 183, 184, 293, 257, 259, 295, 297, 258, 230, 227, 260, 231, 294,
    296, 282, 300, 280, 281, 283, 298, 301, 151, 179, 265, 261, 262, 284, 232, 266, 288, 285, 209,
    180, 228, 302, 289, 229, 263, 303, 233, 267, 264, 286, 287, 304, 299, 268, 290, 291,
)


class Place:
    def __init__(self):
        f = lax.axis_index("fsdp")
        t = lax.axis_index("tensor")
        self.x, self.zl = lax.div(f, 2), lax.rem(f, 2)
        self.y, self.m = lax.div(t, 4), lax.rem(t, 4)
        self.zh, self.c = lax.div(self.m, 2), lax.rem(self.m, 2)
        self.z = 2 * self.zh + self.zl

    def at(self, x=None, z=None, y=None, c=None):
        x = self.x if x is None else x
        z = self.z if z is None else z
        y = self.y if y is None else y
        c = self.c if c is None else c
        return (2 * x + lax.rem(z, 2), 4 * y + 2 * lax.div(z, 2) + c)

    def x_of(self, d):
        return lax.rem(self.x + d, 4)

    def y_of(self, d):
        return lax.rem(self.y + d, 4)

    def z_of(self, d):
        z = lax.rem(self.z + d, 4)
        return z, lax.div(z, 2), lax.rem(z, 2)

    def quad(self, j):
        zh = 1 - self.zh if j & 2 else self.zh
        c = 1 - self.c if j & 1 else self.c
        return self.at(z=2 * zh + self.zl, c=c), 2 * zh + c

    def sibling(self):
        return self.at(c=1 - self.c)


class Copies:
    def __init__(self, send, recv, here):
        self.send, self.recv, self.here = send, recv, here
        self.sent, self.waited, self.kept = [], [], 0

    def push(self, src, dst, device):
        k = len(self.sent)
        assert k < COPIES
        copy = pltpu.make_async_remote_copy(
            src_ref=src,
            dst_ref=dst,
            send_sem=self.send.at[k],
            recv_sem=self.recv.at[k],
            device_id=device,
            device_id_type=MESH,
        )
        copy.start()
        self.sent.append(copy)
        return copy

    def local(self, src, dst):
        assert self.kept < LOCALS
        copy = pltpu.make_async_copy(src, dst, self.here.at[self.kept])
        copy.start()
        self.kept += 1
        return copy

    def wait(self, copy, kind):
        if kind == RECV:
            copy.wait_recv()
        elif kind == HERE:
            copy.wait()
        elif not any(copy is other for other in self.waited):
            copy.wait_send()
            self.waited.append(copy)

    def drain(self):
        for copy in self.sent:
            self.wait(copy, SENT)


def recv(copies):
    return [(copy, RECV) for copy in copies]


def sent(copies):
    return [(copy, SENT) for copy in copies]


def here(copies):
    return [(copy, HERE) for copy in copies]


def nothing():
    return ()


class Tasks:
    def __init__(self, copies):
        self.copies, self.all = copies, []

    def add(self, after, run=nothing, needs=nothing):
        self.all.append((list(after), needs, run))
        return len(self.all) - 1


def drive(tasks, order):
    done = set()
    for number in order:
        after, needs, run = tasks.all[number]
        assert done.issuperset(after), number
        for copy, kind in needs():
            tasks.copies.wait(copy, kind)
        run()
        done.add(number)
    assert len(done) == len(tasks.all)


def enter(place):
    barrier = pltpu.get_barrier_semaphore()
    others = [place.at(y=place.y_of(d)) for d in (1, 2, 3)]
    others += [place.at(x=place.x_of(d)) for d in (1, 2, 3)]
    others += [place.at(z=place.z_of(d)[0]) for d in (1, 2, 3)]
    others += [place.quad(1)[0], place.quad(3)[0]]
    for other in others:
        pl.semaphore_signal(barrier, inc=1, device_id=other, device_id_type=MESH)
    pl.semaphore_wait(barrier, len(others))


def dot(left, right, dims):
    return lax.dot_general(left, right, (dims, ((), ())), preferred_element_type=F32)


def turn(rows, cos_t, sin_t):
    return rows * cos_t + pltpu.roll(rows, HD // 2, 1) * sin_t


def turn_back(rows, cos_t, sin_t):
    return rows * cos_t - pltpu.roll(rows, HD // 2, 1) * sin_t


def head_cols(h, part):
    return pl.ds(pl.multiple_of(h * 3 * HD + part * HD, HD), HD)


def tile_cols(i, size):
    return pl.ds(pl.multiple_of(i * size, size), size)


def columns(rows, cols, size):
    return rows[:, :, :, cols].reshape(512, size)


def factor_of(rows):
    return lax.rsqrt(jnp.mean(rows * rows, axis=-1, keepdims=True) + EPSILON)


def norm_back(grad, rows, gain):
    factor = factor_of(rows)
    scaled = grad * gain
    back = factor * scaled - rows * factor**3 * jnp.mean(scaled * rows, axis=-1, keepdims=True)
    return back, jnp.sum(grad * rows * factor, axis=0, keepdims=True)


def fit(ref, shape):
    index = tuple(
        ALL if have == want else pl.ds(0, want) for have, want in zip(ref.shape, shape, strict=True)
    )
    return ref.at[index]


class Form:
    def __init__(self, place, rows, first):
        self.place = place
        self.up, self.low = pl.ds(0, first), pl.ds(first, rows - first)

    def upper(self, ref, x, zl, zh):
        return ref.at[x, zl, 2 * self.place.c + zh, :, self.up]

    def lower(self, ref, x, zl, zh=None):
        block = pl.ds(2 * self.place.c, 2) if zh is None else 2 * self.place.c + zh
        return ref.at[x, zl, block, :, self.low]

    def core(self, ref, x, c):
        return ref.at[x, :, pl.ds(2 * c, 2)]


class Gather:
    def __init__(self, copies, place, form, whole, block, placed=False):
        self.copies, self.place, self.whole, self.block = copies, place, whole, block
        self.form, self.placed = form, placed

    def plan(self, tasks):
        self.passed, self.shared = [], []
        begin = tasks.add((), self.begin)
        spread = tasks.add([begin], self.spread, lambda: here(self.local) + recv(self.first))
        ahead = tasks.add([spread], lambda: self.relay(0), lambda: recv(self.ahead))
        behind = tasks.add([spread], lambda: self.relay(1), lambda: recv(self.behind))
        near = [tasks.add([spread], lambda: self.to_sibling(0))]
        near.append(tasks.add([ahead], lambda: self.to_sibling(3)))
        near.append(tasks.add([behind], lambda: self.to_sibling(1)))
        far = tasks.add(
            [ahead, behind, *near], lambda: self.to_sibling(2), lambda: recv(self.passed)
        )
        self.have = tasks.add([far], needs=lambda: recv(self.shared))

    def busy(self):
        return sent(self.ahead + self.behind + self.passed + self.shared)

    def begin(self):
        place, block, form = self.place, self.block, self.form
        self.local = []
        if not self.placed:
            target = self.whole.at[place.x, place.zl, 2 * place.c + place.zh]
            self.local.append(self.copies.local(block, target))
        upper, lower = block.at[:, form.up], block.at[:, form.low]
        to_upper = form.upper(self.whole, place.x, place.zl, place.zh)
        to_lower = form.lower(self.whole, place.x, place.zl, place.zh)
        self.first = []
        for d in (1, 3, 2):
            self.first.append(self.copies.push(upper, to_upper, place.at(x=place.x_of(d))))
            self.first.append(self.copies.push(lower, to_lower, place.at(z=place.z_of(d)[0])))

    def both(self, upper, lower, to):
        place = self.place
        return [
            self.copies.push(upper, upper, place.at(z=place.z_of(to)[0])),
            self.copies.push(lower, lower, place.at(x=place.x_of(to))),
        ]

    def spread(self):
        place = self.place
        upper = self.form.upper(self.whole, ALL, place.zl, place.zh)
        lower = self.form.lower(self.whole, place.x, ALL)
        self.ahead = self.both(upper, lower, 1)
        self.behind = self.both(upper, lower, 3)

    def relay(self, half):
        side, onto = ((3, 1), (1, 3))[half]
        _, zh, zl = self.place.z_of(side)
        upper = self.form.upper(self.whole, pl.ds(2 * half, 2), zl, zh)
        lower = self.form.lower(self.whole, self.place.x_of(side), pl.ds(half, 1))
        self.passed += self.both(upper, lower, onto)

    def to_sibling(self, d):
        place, form = self.place, self.form
        _, zh, zl = place.z_of(d)
        for part in (
            form.upper(self.whole, ALL, zl, zh),
            form.lower(self.whole, place.x_of(d), ALL),
        ):
            self.shared.append(self.copies.push(part, part, place.sibling()))


class Reduce:
    def __init__(self, copies, place, form, whole, spaces, buffers, put):
        self.copies, self.place, self.whole, self.put = copies, place, whole, put
        self.form, self.buffers = form, buffers
        (self.theirs, up_relayed, low_relayed, up_landed, low_landed, up_last, low_last) = spaces
        self.relayed, self.landed = (up_relayed, low_relayed), (up_landed, low_landed)
        self.last = (up_last, low_last)
        self.swapped, self.relays, self.sent = [], [], []
        self.arrivals, self.done, self.loads = ([], []), ([], []), {}

    def fetched(self, tasks, buffer, after, use, fetch, needs):
        loads = []

        def load():
            loads.extend(self.copies.local(src, dst) for src, dst in fetch())

        first = tasks.add(list(after) + self.buffers.users.get(buffer, []), load, needs)
        last = tasks.add([first], use, lambda: here(loads))
        self.buffers.users[buffer] = [last]
        return last

    def plan(self, tasks, tile, after, needs):
        buffers = self.buffers
        fills = [tasks.add(after, lambda: self.fill(tile, 0), needs)]
        fills.append(tasks.add(fills, lambda: self.fill(tile, 1)))
        self.filled = fills[1]
        adds = []
        for x in range(4):
            slot = fit(buffers.theirs.at[x % 2], self.theirs.shape[1:])
            adds.append(
                self.fetched(
                    tasks,
                    (0, x % 2),
                    [fills[x // 2]],
                    lambda x=x, slot=slot: self.add(x, slot),
                    lambda x=x, slot=slot: [(self.theirs.at[x], slot)],
                    (lambda x=x: recv(self.swapped[x // 2 : x // 2 + 1])) if x % 2 == 0 else nothing,
                )
            )
            if x % 2:
                tasks.all[adds[x] - 1][0].append(adds[x - 1] - 1)
        push = tasks.add(adds, self.push)
        relays = []
        for i in range(2):
            upper = fit(buffers.relayed[0].at[i], self.relayed[0].shape[1:])
            lower = fit(buffers.relayed[1].at[i], self.relayed[1].shape[1:])
            relays.append(
                self.fetched(
                    tasks,
                    (1, i),
                    [push],
                    lambda i=i, upper=upper, lower=lower: self.relay(i, upper, lower),
                    lambda i=i, upper=upper, lower=lower: [
                        (self.relayed[0].at[i], upper),
                        (self.relayed[1].at[i], lower),
                    ],
                    lambda i=i: recv(self.relays[i]),
                )
            )
        self.ended = []
        for i in range(2):
            slot = fit(buffers.landed[i], self.landed[i].shape)
            own = self.fetched(
                tasks,
                (2, i),
                relays,
                lambda i=i, slot=slot: self.own(i, slot),
                lambda i=i, slot=slot: [(self.landed[i], slot)],
                lambda i=i: recv(self.arrivals[i]),
            )
            slot = fit(buffers.last[i], self.last[i].shape)
            self.ended.append(
                self.fetched(
                    tasks,
                    (3, i),
                    [own],
                    lambda i=i, slot=slot: self.end(i, slot),
                    lambda i=i, slot=slot: [(self.last[i], slot)],
                    lambda i=i: recv(self.done[i]),
                )
            )

    def busy(self):
        return sent(self.sent)

    def fill(self, tile, part):
        place = self.place

        for x in (2 * part, 2 * part + 1):
            tile(x, self.whole, 1 - place.c)
            tile(x, self.whole, place.c)
        block = pl.ds(2 * part, 2)
        self.swapped.append(
            self.copies.push(
                self.form.core(self.whole, block, 1 - place.c),
                self.theirs.at[block],
                place.sibling(),
            )
        )
        self.sent.append(self.swapped[-1])

    def add(self, x, load):
        def body(zl, carry):
            to = self.whole.at[x, zl, pl.ds(2 * self.place.c, 2)]
            to[...] = (to[...].astype(F32) + load[zl].astype(F32)).astype(BF16)
            return carry

        lax.fori_loop(0, 2, body, 0)

    def push(self):
        place, whole = self.place, self.whole
        _, zh, zl = place.z_of(2)
        x = place.x_of(2)
        for half, to in ((0, 1), (1, 3)):
            upper = self.form.upper(whole, pl.ds(2 * half, 2), zl, zh)
            lower = self.form.lower(whole, x, pl.ds(half, 1))
            self.relays.append([
                self.copies.push(upper, self.relayed[0].at[half], place.at(z=place.z_of(to)[0])),
                self.copies.push(lower, self.relayed[1].at[half], place.at(x=place.x_of(to))),
            ])
            self.sent += self.relays[-1]
        for half, to in ((0, 1), (1, 3)):
            self.onward(half, 1 - half, to)

    def onward(self, slot, half, to):
        place = self.place
        z, zh, zl = place.z_of(to)
        x = place.x_of(to)
        two, one = pl.ds(2 * half, 2), pl.ds(half, 1)
        pair = (
            self.copies.push(
                self.form.upper(self.whole, two, zl, zh), self.landed[0].at[slot, two], place.at(z=z)
            ),
            self.copies.push(
                self.form.lower(self.whole, x, one), self.landed[1].at[slot, one], place.at(x=x)
            ),
        )
        for i in range(2):
            self.arrivals[i].append(pair[i])
        self.sent += pair

    def relay(self, half, upper, lower):
        to = (1, 3)[half]
        _, zh, zl = self.place.z_of(to)
        for i in range(2):
            at = self.form.upper(self.whole, 2 * half + i, zl, zh)
            at[...] = (at[...].astype(F32) + upper[i].astype(F32)).astype(BF16)
        at = self.form.lower(self.whole, self.place.x_of(to), half)
        at[...] = (at[...].astype(F32) + lower[0].astype(F32)).astype(BF16)
        self.onward(half, half, to)

    def own(self, i, load):
        place, whole = self.place, self.whole
        for k in range((4, 2)[i]):
            at = (
                self.form.upper(whole, k, place.zl, place.zh)
                if i == 0
                else self.form.lower(whole, place.x, k)
            )
            total = at[...].astype(F32) + load[0, k].astype(F32) + load[1, k].astype(F32)
            at[...] = total.astype(BF16)
        for d in (1, 3, 2):
            if i == 0:
                x = place.x_of(d)
                part, device = self.form.upper(whole, x, place.zl, place.zh), place.at(x=x)
            else:
                z, zh, zl = place.z_of(d)
                part, device = self.form.lower(whole, place.x, zl, zh), place.at(z=z)
            self.done[i].append(self.copies.push(part, self.last[i].at[d - 1], device))
        self.sent += self.done[i]

    def end(self, i, load):
        place = self.place
        if i == 0:
            at = self.form.upper(self.whole, place.x, place.zl, place.zh)
        else:
            at = self.form.lower(self.whole, place.x, place.zl, place.zh)
        total = at[...].astype(F32)
        for d in range(3):
            total += load[d].astype(F32)
        self.put(i, total)


class Buffers:
    def __init__(self, theirs, up_relayed, low_relayed, up_landed, low_landed, up_last, low_last):
        self.theirs, self.relayed = theirs, (up_relayed, low_relayed)
        self.landed, self.last = (up_landed, low_landed), (up_last, low_last)
        self.users = {}


def both_ways(copies, place, src, dst):
    return [copies.push(src, dst, place.at(y=place.y_of(d))) for d in (1, 3)]


class Rows:
    def __init__(self, copies, place, whole):
        self.copies, self.place, self.whole = copies, place, whole
        self.sent, self.passed, self.parts = {}, {}, [0, 1, 2, 3]

    def send(self, k, src=None):
        mine = self.whole.at[self.place.y, self.parts[k]]
        self.sent[k] = both_ways(self.copies, self.place, mine if src is None else src, mine)

    def pass_on(self, k):
        side, onto = (3, 1) if k < 2 else (1, 3)
        place = self.place
        block = self.whole.at[place.y_of(side), self.parts[k]]
        self.passed[k] = self.copies.push(block, block, place.at(y=place.y_of(onto)))

    def plan(self, tasks, before):
        self.passes = [
            tasks.add(
                [before[k]],
                lambda k=k: self.pass_on(k),
                lambda k=k: recv([self.sent[k][0 if k < 2 else 1]]),
            )
            for k in range(4)
        ]
        self.have = tasks.add(
            self.passes,
            needs=lambda: recv(
                [self.sent[k][1 if k < 2 else 0] for k in range(4)]
                + [self.passed[k] for k in range(4)]
            ),
        )

    def busy(self):
        return sent([copy for pair in self.sent.values() for copy in pair]) + sent(
            list(self.passed.values())
        )


class Spread(Rows):
    def __init__(self, copies, place, held, whole):
        super().__init__(copies, place, whole)
        self.held = held
        self.parts = [place.m] + [place.quad(j)[1] for j in (1, 2, 3)]

    def quad(self):
        place = self.place
        mine = self.whole.at[place.y, place.m]
        self.own = self.copies.local(self.held.at[place.m], mine)
        self.came = []
        for j in (1, 2, 3):
            device, m = place.quad(j)
            self.came.append(self.copies.push(self.held.at[m], mine, device))

    def plan(self, tasks):
        quad = tasks.add((), self.quad)
        along = [
            tasks.add(
                [quad],
                lambda k=k: self.send(k),
                lambda k=k: recv([self.came[k - 1]]) if k else here([self.own]),
            )
            for k in range(4)
        ]
        super().plan(tasks, along)


class RowSum:
    def __init__(self, copies, place, part, buffers):
        self.copies, self.place, self.part = copies, place, part
        self.relayed, self.stage, self.arrived = buffers
        self.passed = {}

    def sides(self):
        ahead, behind = self.place.y_of(1), self.place.y_of(3)
        return (ahead, behind), (self.place.at(y=ahead), self.place.at(y=behind))

    def send(self):
        place = self.place
        near, onto = self.sides()
        across = place.y_of(2)
        self.first = [
            self.copies.push(self.part.at[across, k], self.relayed.at[k], onto[k // 2])
            for k in (0, 2, 1, 3)
        ]
        self.first = [self.first[i] for i in (0, 2, 1, 3)]
        self.direct = [
            self.copies.push(
                self.part.at[near[1 - k // 2], k], self.arrived.at[1 - k // 2, k], onto[1 - k // 2]
            )
            for k in range(4)
        ]

    def relay(self, k):
        near, onto = self.sides()
        total = self.part[near[k // 2], k].astype(F32) + self.relayed[k].astype(F32)
        self.stage[k] = total.astype(BF16)
        self.passed[k] = self.copies.push(
            self.stage.at[k], self.arrived.at[k // 2, k], onto[k // 2]
        )

    def plan(self, tasks, after, needs=nothing):
        send = tasks.add(after, self.send, needs)
        self.sums = [
            tasks.add([send], lambda k=k: self.relay(k), lambda k=k: recv([self.first[k]]))
            for k in range(4)
        ]

    def came(self, k):
        return recv([self.direct[k], self.passed[k]])

    def total(self, k):
        total = self.part[self.place.y, k].astype(F32)
        return total + self.arrived[0, k].astype(F32) + self.arrived[1, k].astype(F32)

    def busy(self):
        return sent(self.first + self.direct + list(self.passed.values()))


def lift(left, piece, kind, count):
    total = None
    for i in range(TILES):
        weight = piece[i // 2, i % 2, :, kind].reshape(count, 256)
        one = dot(columns(left, pl.ds(256 * i, 256), 256), weight, ((1,), (1,)))
        total = one if total is None else total + one
    return total


def layer_kernel(*refs):
    (held, grad_held, query_block, key_block, value_block, out_block, attn_gain, mlp_gain, unit_block,
     cos_in, sin_in,
     block_out, grad_out, gains_out, qkv_out, tall_out, out_out, first_out, x_out) = refs[:19]
    spaces = refs[19:61]
    rest = refs[61:]
    (rows, first, second, grads, qkv, probs, mixed, act, back, units, part,
     relayed, summed, arrived, down_relayed, down_summed, down_arrived, middle,
     stage, key_grad, value_grad,
     piece_a, piece_b, piece_c, qkv_w, out_w, gains, gain_row, ends,
     vec, vec_y, vec_x, vec_z, vec_c, half_x, half_z, half_c,
     send_sems, recv_sems, here_sems) = rest[:21] + rest[28:]
    place = Place()
    enter(place)
    copies = Copies(send_sems, recv_sems, here_sems)
    tasks = Tasks(copies)
    width = rows.shape[-1]
    buffers = Buffers(*rest[21:28])

    qkv_block = qkv_w.at[place.x, place.zl, 2 * place.c + place.zh]
    for kind, block in enumerate((query_block, key_block, value_block)):
        qkv_block[kind] = block[...].T
    pieces = (piece_a, piece_b, piece_c)
    forms = [Form(place, ROWS[p], FIRST[p]) for p in range(3)]
    head_form, out_form = Form(place, HD, FIRST[3]), Form(place, HD, FIRST[4])
    pair, single = pl.ds(0, 2), pl.ds(2, 1)
    gather_q = Gather(
        copies, place, head_form, qkv_w.at[:, :, :, pair], qkv_block.at[pair], True
    )
    gather_v = Gather(
        copies, place, head_form, qkv_w.at[:, :, :, single], qkv_block.at[single], True
    )
    gather_o = Gather(copies, place, out_form, out_w, out_block)
    gathers = [
        Gather(copies, place, forms[p], pieces[p], unit_block.at[:, pl.ds(128 * p, ROWS[p])])
        for p in range(3)
    ]
    for gather in (gather_q, gather_v, gather_o, *gathers):
        gather.plan(tasks)

    class Gains:
        pass

    gain = Gains()

    gain_block = vec.at[:, pl.ds(0, 256)]

    def begin_gains():
        vec[0:1, 0:256] = attn_gain[...].astype(F32).reshape(1, 256)
        vec[1:2, 0:256] = mlp_gain[...].astype(F32).reshape(1, 256)
        vec[2:8, 0:256] = jnp.zeros((6, 256), F32)
        target = gains.at[place.x, place.zl]
        gain.local = copies.local(gain_block, target)
        gain.first = [copies.push(gain_block, target, place.at(x=place.x_of(d))) for d in (1, 2, 3)]

    def spread_gains():
        column = gains.at[:, place.zl]
        gain.last = copies.push(column, column, place.at(z=2 * place.zh + 1 - place.zl))

    def have_gains():
        for i in range(TILES):
            gain_row[:, 256 * i : 256 * i + 256] = gains[i // 2, i % 2]

    begun = tasks.add((), begin_gains)
    passed = tasks.add([begun], spread_gains, lambda: here([gain.local]) + recv(gain.first))
    have_gain = tasks.add([passed], have_gains, lambda: recv([gain.last]))

    spread_x = Spread(copies, place, held, rows)
    spread_x.plan(tasks)
    spread_dy = Spread(copies, place, grad_held, grads)
    spread_dy.plan(tasks)

    def norm_first():
        def body(i, carry):
            y, j = lax.div(i, 4), lax.rem(i, 4)
            x = rows[y, j].astype(F32)
            first[y, j] = (x * factor_of(x) * gain_row[0:1, :]).astype(BF16)
            return carry

        lax.fori_loop(0, 16, body, 0)
        gain.x_out = copies.local(rows.at[place.y], x_out)
        gain.first_out = copies.local(first, first_out)

    norm1 = tasks.add([spread_x.have, have_gain], norm_first)

    def project(kind):
        both = lift(first, qkv_w, kind, 4 * HD)
        for h in range(4):
            one = both[:, h * HD : (h + 1) * HD]
            if kind < 2:
                one = turn(one, cos_in[...], sin_in[...])
            qkv[:, h * 3 * HD + kind * HD : h * 3 * HD + kind * HD + HD] = one.astype(BF16)

    projects = [
        tasks.add(
            [norm1, (gather_q, gather_v)[kind // 2].have], lambda kind=kind: project(kind)
        )
        for kind in range(3)
    ]

    def attend(i):
        for h in (2 * i, 2 * i + 1):
            for b in range(4):
                size = 128 * (b + 1)
                now = slice(128 * b, size)
                at = [slice(h * 3 * HD + k * HD, h * 3 * HD + k * HD + HD) for k in range(3)]
                scores = dot(qkv[now, at[0]], qkv[0:size, at[1]], ((1,), (1,)))
                allowed = lax.broadcasted_iota(jnp.int32, (128, size), 0) + 128 * b
                allowed = allowed >= lax.broadcasted_iota(jnp.int32, (128, size), 1)
                scores = jnp.where(allowed, scores * HD**-0.5, -jnp.inf)
                weight = jnp.exp(scores - jnp.max(scores, axis=-1, keepdims=True))
                weight = weight * (1.0 / jnp.sum(weight, axis=-1, keepdims=True))
                weight = weight.astype(BF16)
                start = 64 * b * (b + 1)
                probs[h, :, start : start + size] = weight
                blend = dot(weight, qkv[0:size, at[2]], ((1,), (0,)))
                mixed[now, h * HD : (h + 1) * HD] = blend.astype(BF16)

    attends = [tasks.add(projects, lambda i=i: attend(i)) for i in range(2)]

    def output():
        for i in range(TILES):
            weight = out_w[i // 2, i % 2].reshape(4 * HD, 256)
            total = dot(mixed[...], weight, ((1,), (0,)))
            part[:, :, :, tile_cols(i, 256)] = total.astype(BF16).reshape(4, 4, 32, 256)

    outputs = tasks.add([*attends, gather_o.have], output)
    sum_out = RowSum(copies, place, part, (relayed, summed, arrived))
    sum_out.plan(tasks, [outputs])
    rows_a = Rows(copies, place, second)

    def middle_part(k):
        now = pl.ds(32 * k, 32)
        mid = rows[place.y, k].astype(F32) + sum_out.total(k)
        middle[now, :] = mid
        stage[k] = (mid * factor_of(mid) * gain_row[1:2, :]).astype(BF16)
        rows_a.send(k, stage.at[k])
        second[place.y, k] = stage[k]

    mids = [
        tasks.add(
            [sum_out.sums[k], norm1],
            lambda k=k: middle_part(k),
            lambda k=k: sum_out.came(k) + spread_x.busy(),
        )
        for k in range(4)
    ]
    rows_a.plan(tasks, mids)

    def lift_back(p):
        count = 4 * ROWS[p]
        back[:, 512 * p : 512 * p + count] = lift(grads, pieces[p], 2, count).astype(BF16)

    def open_units(p, kind):
        count = 4 * ROWS[p]
        act[kind, :, 0:count] = lift(second, pieces[p], kind, count).astype(BF16)

    def gating(p):
        for j in range(4 * ROWS[p] // 128):
            cols = slice(128 * j, 128 * j + 128)
            opened, lifted = act[0, :, cols].astype(F32), act[1, :, cols].astype(F32)
            change = back[:, 512 * p + 128 * j : 512 * p + 128 * j + 128].astype(F32)
            sig = 1.0 / (1.0 + jnp.exp(-opened))
            silu = opened * sig
            result = (
                (change * lifted * sig * (1.0 + opened * (1.0 - sig))).astype(BF16),
                (change * silu).astype(BF16),
                (silu * lifted).astype(BF16),
            )
            back[:, 512 * p + 128 * j : 512 * p + 128 * j + 128] = result[2]
            for kind in range(3):
                if kind < 2:
                    act[kind, :, cols] = result[kind]
                turned, at = result[kind].T, 0
                while at < 128:
                    c, row = divmod(128 * j + at, 2 * ROWS[p])
                    size = min(128 - at, 2 * ROWS[p] - row)
                    units[p % 2, c, kind, row : row + size, :] = turned[at : at + size]
                    at += size

    def sum_up(target, p, kinds):
        count = 4 * ROWS[p]

        for i in range(TILES):
            cols = tile_cols(i, 256)
            total = None
            for kind in kinds:
                weight = pieces[p][i // 2, i % 2, :, kind].reshape(count, 256)
                left = act[kind, :, 0:count] if kind < 2 else back[:, 512 * p : 512 * p + count]
                one = dot(left, weight, ((1,), (0,)))
                total = one if total is None else total + one
            if p:
                total += columns(target, cols, 256).astype(F32)
            target[:, :, :, cols] = total.astype(BF16).reshape(4, 4, 32, 256)

    def of_units(count, turned, middle_rows, right):
        def tile(x, target, c):
            cols = tile_cols(x, 512)
            pair = dot(
                turned[c, 0:2, 0 : 2 * count].reshape(4 * count, 512),
                columns(middle_rows, cols, 512),
                ((1,), (0,)),
            ).astype(BF16)
            one = dot(turned[c, 2, 0 : 2 * count], columns(right, cols, 512), ((1,), (0,)))
            one = one.astype(BF16)
            for zl in range(2):
                at = slice(256 * zl, 256 * zl + 256)
                for zh in range(2):
                    block = target.at[x, zl, 2 * c + zh]
                    for kind in range(2):
                        start = (2 * kind + zh) * count
                        block[kind] = pair[start : start + count, at]
                    block[2] = one[zh * count : (zh + 1) * count, at]

        return tile

    def of_pair(x, target, c):
        cols = tile_cols(x, 512)
        both = dot(
            units[1, c, 0:2].reshape(4 * HD, 512), columns(second, cols, 512), ((1,), (0,))
        ).astype(BF16)
        for zl in range(2):
            for zh in range(2):
                for kind in range(2):
                    start = (2 * kind + zh) * HD
                    target[x, zl, 2 * c + zh, kind] = both[
                        start : start + HD, 256 * zl : 256 * zl + 256
                    ]

    def of_values(x, target, c):
        cols = tile_cols(x, 512)
        one = dot(units[1, c, 2], columns(second, cols, 512), ((1,), (0,))).astype(BF16)
        for zl in range(2):
            for zh in range(2):
                target[x, zl, 2 * c + zh, 0] = one[
                    zh * HD : (zh + 1) * HD, 256 * zl : 256 * zl + 256
                ]

    slots = [None, None]

    def put_units(p):
        def put(i, total):
            if slots[i] is not None:
                slots[i].wait()
            start, size = FIRST[p] * i, (FIRST[p], ROWS[p] - FIRST[p])[i]
            ends[i, :, 0:size, :] = total
            slots[i] = copies.local(
                ends.at[i, :, pl.ds(0, size)], tall_out.at[:, pl.ds(128 * p + start, size)]
            )

        return put

    def put_heads(first_kind):
        def put(i, total):
            for kind in range(total.shape[0]):
                cols = slice(FIRST[3] * i, (FIRST[3], HD)[i])
                qkv_out[first_kind + kind, :, cols] = total[kind].T

        return put

    def put_out(i, total):
        out_out[FIRST[4] * i : (FIRST[4], HD)[i], :] = total[0]

    reduces = [
        Reduce(copies, place, form, whole, spaces[7 * i : 7 * i + 7], buffers, put)
        for i, (form, whole, put) in enumerate((
            (forms[0], piece_a, put_units(0)),
            (forms[1], piece_b, put_units(1)),
            (forms[2], piece_c, put_units(2)),
            (head_form, piece_a.at[:, :, :, pair], put_heads(0)),
            (head_form, piece_a.at[:, :, :, single], put_heads(2)),
            (out_form, out_w, put_out),
        ))
    ]
    earlier, filled, all_down = [], [], []
    for p in range(3):
        have = gathers[p].have
        lifted = tasks.add([spread_dy.have, have], lambda p=p: lift_back(p))
        opened = [
            tasks.add([rows_a.have, have] + earlier, lambda p=p, kind=kind: open_units(p, kind))
            for kind in range(2)
        ]
        gated = tasks.add([lifted] + opened + filled[: max(0, p - 1)], lambda p=p: gating(p))
        da2 = tasks.add(
            [gated] + mids,
            lambda p=p: sum_up(part, p, (0, 1)),
            sum_out.busy if p == 0 else nothing,
        )
        downed = tasks.add(
            [gated] + projects + all_down[-1:],
            lambda p=p: sum_up(first, p, (2,)),
            (lambda: here([gain.first_out])) if p == 0 else nothing,
        )
        earlier = [da2]
        all_down.append(downed)
        reduces[p].plan(tasks, of_units(ROWS[p], units.at[p % 2], second, grads), [da2, downed], gathers[p].busy)
        filled = filled + [reduces[p].filled]

    sum_mid = RowSum(copies, place, part, (relayed, summed, arrived))
    sum_mid.plan(tasks, [da2])
    rows_m = Rows(copies, place, rows)
    gain.mlp = jnp.zeros((1, width), F32)

    def mid_back(k):
        now = pl.ds(32 * k, 32)
        result, gain_part = norm_back(sum_mid.total(k), middle[now, :], gain_row[1:2, :])
        gain.mlp += gain_part
        result += grads[place.y, k].astype(F32)
        stage[k] = result.astype(BF16)
        rows_m.send(k, stage.at[k])
        rows[place.y, k] = stage[k]

    dmids = []
    for k in range(4):
        dmids += [tasks.add(
            [sum_mid.sums[k], rows_a.passes[k]] + dmids[:1],
            lambda k=k: mid_back(k),
            lambda k=k: sum_mid.came(k) + sent(rows_a.sent[k]) + (here([gain.x_out]) if k == 0 else []),
        )]
    rows_m.plan(tasks, dmids)
    sum_down = RowSum(copies, place, first, (down_relayed, down_summed, down_arrived))
    sum_down.plan(tasks, all_down)

    out_stage = down_relayed

    def out_part(k):
        now = pl.ds(32 * k, 32)
        out_stage[k] = (middle[now, :] + sum_down.total(k)).astype(BF16)

    def to_quad(source, target, state):
        state.append(copies.local(source.at[place.m], target.at[place.m]))
        for j in (1, 2, 3):
            device, m = place.quad(j)
            state.append(copies.push(source.at[m], target.at[place.m], device))

    out_state, in_state = [], []
    outs = [
        tasks.add([sum_down.sums[k]], lambda k=k: out_part(k), lambda k=k: sum_down.came(k))
        for k in range(4)
    ]
    gone = tasks.add(outs, lambda: to_quad(out_stage, block_out, out_state))
    tasks.add([gone], needs=lambda: here(out_state[:1]) + recv(out_state[1:]))

    def unmix():
        act[0] = sum(
            dot(
                columns(rows, pl.ds(256 * i, 256), 256),
                out_w[i // 2, i % 2].reshape(4 * HD, 256),
                ((1,), (1,)),
            )
            for i in range(TILES)
        ).astype(BF16)

    unmixed = tasks.add([rows_m.have, *earlier], unmix)

    def of_mixed(x, target, c):
        left = mixed[:, pl.ds(pl.multiple_of(2 * c * HD, 128), 2 * HD)].T
        one = dot(left, columns(rows, tile_cols(x, 512), 512), ((1,), (0,))).astype(BF16)
        for zl in range(2):
            for zh in range(2):
                target[x, zl, 2 * c + zh, 0] = one[
                    zh * HD : (zh + 1) * HD, 256 * zl : 256 * zl + 256
                ]

    reduces[5].plan(tasks, of_mixed, [unmixed], gather_o.busy)

    def values_back(i):
        for h in (2 * i, 2 * i + 1):
            at = slice(h * 3 * HD + 2 * HD, h * 3 * HD + 3 * HD)
            value_grad[...] = jnp.zeros(value_grad.shape, F32)
            for b in range(4):
                size = 128 * (b + 1)
                start = 64 * b * (b + 1)
                weight = probs[h, :, start : start + size]
                mix = act[0, 128 * b : size, h * HD : (h + 1) * HD]
                value_grad[0:size, :] += dot(weight, mix, ((0,), (0,)))
            back[:, at] = value_grad[...].astype(BF16)
            start = h % 2 * HD
            units[1, h // 2, 2, start : start + HD, :] = back[:, at].T

    def attend_back(i):
        for h in (2 * i, 2 * i + 1):
            at = [slice(h * 3 * HD + k * HD, h * 3 * HD + k * HD + HD) for k in range(3)]
            key_grad[...] = jnp.zeros(key_grad.shape, F32)
            for b in range(4):
                size = 128 * (b + 1)
                now, so_far = slice(128 * b, size), slice(0, size)
                start = 64 * b * (b + 1)
                weight = probs[h, :, start : start + size]
                mix = act[0, now, h * HD : (h + 1) * HD]
                change = dot(mix, qkv[so_far, at[2]], ((1,), (1,)))
                weight = weight.astype(F32)
                change = weight * (change - jnp.sum(weight * change, axis=-1, keepdims=True))
                change = change.astype(BF16)
                query = dot(change, qkv[so_far, at[1]], ((1,), (0,))) * HD**-0.5
                query = turn_back(query, cos_in[now, :], sin_in[now, :])
                back[now, at[0]] = query.astype(BF16)
                key_grad[so_far, :] += dot(change, qkv[now, at[0]], ((0,), (0,)))
            key = turn_back(key_grad[...] * HD**-0.5, cos_in[...], sin_in[...])
            back[:, at[1]] = key.astype(BF16)
            start = h % 2 * HD
            for kind in range(2):
                units[1, h // 2, kind, start : start + HD, :] = back[:, at[kind]].T

    before = [unmixed, gated] + filled + all_down
    vbacks = [tasks.add(before, lambda i=i: values_back(i)) for i in range(2)]
    abacks = [tasks.add(before, lambda i=i: attend_back(i)) for i in range(2)]

    def first_back():
        for i in range(TILES):
            weight = qkv_w[i // 2, i % 2].reshape(12 * HD, 256)
            total = dot(back[...], weight, ((1,), (0,)))
            grads[:, :, :, tile_cols(i, 256)] = total.astype(BF16).reshape(4, 4, 32, 256)

    da1 = tasks.add([*abacks, *vbacks, *filled, *dmids], first_back, spread_dy.busy)
    sum_first = RowSum(copies, place, grads, (relayed, summed, arrived))
    sum_first.plan(tasks, [da1] + rows_m.passes, sum_mid.busy)

    def reload():
        gain.first_in = copies.local(first_out, second)

    reloaded = tasks.add(filled, reload, rows_a.busy)
    place_free = tasks.add(
        [reloaded, *reduces[0].ended],
        needs=lambda: here([gain.first_in]) + reduces[0].busy(),
    )
    reduces[4].plan(tasks, of_values, [*vbacks, place_free], nothing)
    reduces[3].plan(tasks, of_pair, [*abacks, place_free], nothing)

    gain.attn = jnp.zeros((1, width), F32)

    def in_part(k):
        now = pl.ds(32 * k, 32)
        result, gain_part = norm_back(
            sum_first.total(k), stage[k].astype(F32), gain_row[0:1, :]
        )
        gain.attn += gain_part
        stage[k] = (rows[place.y, k].astype(F32) + result).astype(BF16)

    def load_x():
        gain.x_in = copies.local(x_out, stage)

    def sent_m():
        return sent([copy for pair in rows_m.sent.values() for copy in pair])

    got_x = tasks.add([*dmids, *rows_m.passes], load_x, sent_m)
    have_x = tasks.add([got_x], needs=lambda: here([gain.x_in]))
    ins = [
        tasks.add(
            [sum_first.sums[k], have_x], lambda k=k: in_part(k), lambda k=k: sum_first.came(k)
        )
        for k in range(4)
    ]
    gone = tasks.add(ins, lambda: to_quad(stage, grad_out, in_state))
    tasks.add([gone], needs=lambda: here(in_state[:1]) + recv(in_state[1:]))

    def gain_y():
        vec[0:1, :] = gain.attn
        vec[1:2, :] = gain.mlp
        vec[2:8, :] = jnp.zeros((6, width), F32)
        gain.y = [copies.push(vec, vec_y.at[d - 1], place.at(y=place.y_of(d))) for d in (1, 3, 2)]

    def of_x(x):
        return pl.ds(pl.multiple_of(x * 512, 128), 512)

    def of_z(zl):
        return pl.ds(pl.multiple_of(zl * 256, 128), 256)

    def gain_x():
        half_x[...] = vec[...] + vec_y[0] + vec_y[1] + vec_y[2]
        gain.x = []
        for d in (1, 3, 2):
            x = place.x_of(d)
            gain.x.append(copies.push(half_x.at[:, of_x(x)], vec_x.at[d - 1], place.at(x=x)))

    def gain_z():
        half_z[...] = half_x[:, of_x(place.x)] + vec_x[0] + vec_x[1] + vec_x[2]
        gain.z = []
        for d in (1, 3, 2):
            z, zh, zl = place.z_of(d)
            gain.z.append(copies.push(half_z.at[:, of_z(zl)], vec_z.at[d - 1], place.at(z=z)))

    def gain_c():
        half_c[...] = half_z[:, of_z(place.zl)] + vec_z[0] + vec_z[1] + vec_z[2]
        gain.c = copies.push(half_c, vec_c, place.sibling())

    def gain_end():
        gains_out[...] = half_c[...] + vec_c[...]

    over_y = tasks.add(ins + dmids, gain_y, lambda: sent(gain.first))
    over_x = tasks.add([over_y], gain_x, lambda: recv(gain.y))
    over_z = tasks.add([over_x], gain_z, lambda: recv(gain.x))
    over_c = tasks.add([over_z], gain_c, lambda: recv(gain.z))
    tasks.add([over_c], gain_end, lambda: recv([gain.c]))

    drive(tasks, ORDER)
    for copy in slots:
        copy.wait()
    copies.drain()


def deliver_kernel(rows_in, rows_back, heads, tall, out, gains, *refs):
    count = refs[5].shape[0]
    refs[0][...], refs[1][...], refs[8][...] = rows_in[...], rows_back[...], out[...]
    for i in range(2):
        refs[9 + i][...] = gains[i : i + 1, :].reshape(gains.shape[1])
    for kind in range(3):
        refs[2 + kind][...] = heads[kind]
        refs[5 + kind][...] = tall[kind, 0:count, :]


def tables(length):
    half_size = HD // 2
    inverse_freq = np.float32(THETA) ** (-(np.arange(half_size, dtype=np.float32) * 2.0) / HD)
    angles = np.arange(length, dtype=np.float32)[:, None] * inverse_freq.astype(np.float32)[None]
    cos_t, sin_t = np.cos(angles), np.sin(angles)
    return (
        jnp.asarray(np.concatenate([cos_t, cos_t], axis=1), F32),
        jnp.asarray(np.concatenate([-sin_t, sin_t], axis=1), F32),
    )


def local(
    hidden_in,
    cotangent,
    gain_attn,
    w_query,
    w_key,
    w_value,
    w_output,
    gain_mlp,
    w_gate,
    w_up,
    w_down,
):
    held, grad_held = hidden_in[:, 0], cotangent[:, 0]
    width = held.shape[2]
    length = 512
    count = w_gate.shape[1]
    unit_block = jnp.pad(
        jnp.stack([w_gate.T, w_up.T, w_down]), ((0, 0), (0, UNITS - count), (0, 0))
    )
    cos_t, sin_t = tables(length)
    blocks = ((4, 4, 32, width), BF16)
    heads = ((length, 12 * HD), BF16)
    square = ((length, length), BF16)
    own_f32 = ((128, width), F32)
    parts = ((4, 32, width), BF16)
    sums = [parts, parts, ((2, 4, 32, width), BF16)]

    def spaces(kinds, size, first):
        up, low = (kinds, first, 256), (kinds, size - first, 256)
        return [
            ((4, 2, 2, kinds, size, 256), BF16),
            ((2, 2, *up), BF16),
            ((2, 1, 2, *low), BF16),
            ((2, 4, *up), BF16),
            ((2, 2, 2, *low), BF16),
            ((3, *up), BF16),
            ((3, *low), BF16),
        ]

    def whole(kinds, size):
        return ((4, 2, 4, kinds, size, 256), BF16)

    landing = []
    for i, size in enumerate((*ROWS, HD, HD, HD)):
        kinds = (3, 3, 3, 2, 1, 1)[i]
        landing += spaces(kinds, size, FIRST[min(i, 4) if i < 4 else i - 1])
    outs = [
        parts, parts, ((8, 256), F32), ((3, 256, HD), F32), ((3, UNITS, 256), F32),
        ((HD, 256), F32), blocks, parts,
    ]
    up, low = max(FIRST), HD - min(FIRST[0], FIRST[1], FIRST[3])
    buffers = [
        ((2, 2, 2, 3, HD, 256), BF16),
        ((2, 2, 3, up, 256), BF16), ((2, 1, 2, 3, low, 256), BF16),
        ((2, 4, 3, up, 256), BF16), ((2, 2, 2, 3, low, 256), BF16),
        ((3, 3, up, 256), BF16), ((3, 3, low, 256), BF16),
    ]
    scratch = [
        blocks, blocks, blocks, blocks, heads, ((4, 128, 1280), BF16), square,
        ((2, length, length), BF16), heads, ((2, 2, 3, 256, length), BF16), blocks,
        *sums, *sums, own_f32, parts,
        ((length, HD), F32), ((length, HD), F32), *buffers,
        whole(3, ROWS[0]), whole(3, ROWS[1]), whole(3, ROWS[2]), whole(3, HD), whole(1, HD),
        ((4, 2, 8, 256), F32), ((8, width), F32), ((2, 3, max(up, low), 256), F32),
        ((8, width), F32), ((3, 8, width), F32), ((3, 8, 512), F32), ((3, 8, 256), F32),
        ((8, 256), F32), ((8, width), F32), ((8, 512), F32), ((8, 256), F32),
    ]
    block_out, grad_in, gains_out, qkv_g, tall_g, out_g = pl.pallas_call(
        layer_kernel,
        out_shape=[jax.ShapeDtypeStruct(shape, dtype) for shape, dtype in outs + landing],
        in_specs=[ANY] * 2 + [VMEM] * 3 + [ANY] + [VMEM] * 2 + [ANY] + [VMEM] * 2,
        out_specs=[ANY, ANY, VMEM, VMEM, ANY, VMEM, ANY, ANY] + [ANY] * len(landing),
        scratch_shapes=[
            *[pltpu.VMEM(shape, dtype) for shape, dtype in scratch],
            pltpu.SemaphoreType.DMA((COPIES,)),
            pltpu.SemaphoreType.DMA((COPIES,)),
            pltpu.SemaphoreType.DMA((LOCALS,)),
        ],
        compiler_params=pltpu.CompilerParams(
            collective_id=0, has_side_effects=True, vmem_limit_bytes=VMEM_LIMIT
        ),
    )(held, grad_held, w_query, w_key, w_value, w_output[None], gain_attn, gain_mlp, unit_block, cos_t, sin_t)[:6]
    final = [block_out.shape, grad_in.shape] + [qkv_g.shape[1:]] * 3
    final += [(count, tall_g.shape[2])] * 3 + [out_g.shape] + [gains_out.shape[1:]] * 2
    results = pl.pallas_call(
        deliver_kernel,
        out_shape=[
            jax.ShapeDtypeStruct(shape, BF16 if i < 2 else F32) for i, shape in enumerate(final)
        ],
        in_specs=[VMEM] * 6,
        out_specs=[VMEM] * 11,
    )(block_out, grad_in, qkv_g, tall_g, out_g, gains_out)
    block_out, grad_in, query_g, key_g, value_g, gate_g, up_g, down_g, out_g = results[:9]
    attn_g, mlp_g = results[9:]
    return (
        block_out[:, None],
        grad_in[:, None],
        attn_g,
        query_g,
        key_g,
        value_g,
        out_g,
        mlp_g,
        gate_g.T,
        up_g.T,
        down_g,
    )


def solution(mesh):
    rows = P(None, "fsdp", "tensor", None)
    into, out_of = P("fsdp", "tensor"), P("tensor", "fsdp")
    return jax.shard_map(
        local,
        mesh=mesh,
        in_specs=(
            rows, rows, P("fsdp"), into, into, into, out_of, P("fsdp"), into, into, out_of,
        ),
        out_specs=(
            rows, rows, P("fsdp"), into, into, into, out_of, P("fsdp"), into, into, out_of,
        ),
        check_vma=False,
    )
```
